32 devices in a mesh: sy: 4 (over y, x), sx: 2 (over core), grp: 4 (over z).
Axes of the slice: x: 2, y: 2, z: 4, core: 2. Of those that a mesh axis runs over, the one named last changes fastest.
Arguments:
- image: bfloat16 [4, 64, 128, 256], P('grp', None, 'sy', 'sx'), may hold values from -6 to 6
- weight_one: bfloat16 [3, 3, 64, 64], replicated, may hold values from -0.25 to 0.25
- bias_one: float32 [64], replicated, may hold values from -3 to 3
- weight_two: bfloat16 [3, 3, 64, 64], replicated, may hold values from -0.25 to 0.25
- bias_two: float32 [64], replicated, may hold values from -3 to 3
- cotangent: bfloat16 [4, 64, 128, 256], P('grp', None, 'sy', 'sx'), may hold values from -51 to 51
Outputs:
- output: bfloat16 [4, 64, 128, 256], P('grp', None, 'sy', 'sx')
- image_grad: bfloat16 [4, 64, 128, 256], P('grp', None, 'sy', 'sx')
- grad_weight_one: float32 [3, 3, 64, 64], replicated
- grad_bias_one: float32 [64], replicated
- grad_weight_two: float32 [3, 3, 64, 64], replicated
- grad_bias_two: float32 [64], replicated
The draws below stay inside these ranges and needn't reach their ends.
All inputs are finite; a program needn't handle non-finite values.
Results may differ from the reference program's by a relative error of at most 0.0075.
Values may be sent and summed in bfloat16 or wider, within the bound.
No kernel may reach another device: no remote copies, remote signals or barrier semaphores. Data moves between devices by JAX's collectives and lax.ppermute only.
A program may use at most 64 MiB of HBM per device.

```python
import math
import jax
import jax.numpy as jnp
from jax import lax

C = 64
SLIDES = 4
NH = 128
NW = 256


def draw_cotangent(key, part):
    keys = jax.random.split(key, 3)
    shape = (SLIDES, C, NH, NW)
    base = jax.random.truncated_normal(keys[0], -4.0, 4.0, shape, jnp.float32)
    row_scale = jnp.exp(jax.random.uniform(keys[1], (SLIDES, 1, NH, 1), jnp.float32) * (0.5 * math.log(10.0)))
    col_scale = jnp.exp(jax.random.uniform(keys[2], (SLIDES, 1, 1, NW), jnp.float32) * (0.5 * math.log(10.0)))
    rising = 1.0 + 2.0 * jnp.arange(SLIDES, dtype=jnp.float32).reshape(SLIDES, 1, 1, 1) / max(SLIDES - 1, 1)
    return (0.3 * base * row_scale * col_scale * rising).astype(jnp.bfloat16)


def level_of(stream_key, extent, pieces, smallest, high):
    loudness, own = 1.0, jax.random.fold_in(stream_key, 6)
    for dim, parts in pieces:
        heights = jnp.exp(jax.random.uniform(jax.random.fold_in(own, dim), (parts,), jnp.float32, smallest / len(pieces), high / len(pieces)))
        loudness = loudness * jnp.repeat(heights, extent[dim] // parts).reshape([-1 if axis == dim else 1 for axis in range(len(extent))])
    return loudness


def scatter_about(rng, shape, deviation, limit, shards=(), kind=jnp.bfloat16):
    values = deviation * jax.random.normal(rng, shape, jnp.float32)
    if shards:
        values = values * level_of(rng, shape, shards, -0.22, 0.18)
    return jnp.clip(values, -limit, limit).astype(kind)


def setup_inputs(seed: int = 0) -> dict:
    key_of = jax.random.split(jax.random.key(seed), 7)
    image = scatter_about(key_of[0], (SLIDES, C, NH, NW), 1.0, 6.0, ((0, 4), (2, 4), (3, 2)))
    weight_one = scatter_about(key_of[1], (3, 3, C, C), (9 * C) ** -0.5, 0.25)
    bias_one = scatter_about(key_of[2], (C,), 0.5, 3.0, (), jnp.float32)
    weight_two = scatter_about(key_of[3], (3, 3, C, C), (9 * C) ** -0.5, 0.25)
    bias_two = scatter_about(key_of[4], (C,), 0.5, 3.0, (), jnp.float32)
    cotangent = draw_cotangent(jax.random.fold_in(key_of[6], 71), 0)
    return {"image": image, "weight_one": weight_one, "bias_one": bias_one, "weight_two": weight_two, "bias_two": bias_two, "cotangent": cotangent}


def convolve(padded, kernel):
    return lax.conv_general_dilated(padded, kernel, (1, 1), 'VALID', dimension_numbers=('NCHW', 'HWIO', 'NCHW'), preferred_element_type=jnp.float32)

def flipped(kernel):
    return jnp.transpose(kernel[::-1, ::-1], (0, 1, 3, 2))

def pad_edges(field):
    return jnp.pad(field, ((0, 0), (0, 0), (1, 1), (1, 1)))

def kernel_grad(padded, delta):
    rows = delta.shape[2]
    cols = delta.shape[3]
    taps = []
    for row_tap in range(3):
        for col_tap in range(3):
            window = padded[0, :, row_tap:row_tap + rows, col_tap:col_tap + cols].astype(jnp.float32)
            taps.append(jnp.einsum('ihw,ohw->io', window, delta[0].astype(jnp.float32)))
    return jnp.stack(taps).reshape(3, 3, delta.shape[1], delta.shape[1])

def slope(pre):
    gate = jax.nn.sigmoid(pre)
    return gate * (1.0 + pre * (1.0 - gate))

def one_slide(image, cotangent, weight_one, bias_one, weight_two, bias_two):
    image_pad = pad_edges(image[None])
    pre_one = convolve(image_pad, weight_one) + bias_one.reshape(1, -1, 1, 1)
    hidden = (pre_one * jax.nn.sigmoid(pre_one)).astype(jnp.bfloat16)
    hidden_pad = pad_edges(hidden)
    pre_two = convolve(hidden_pad, weight_two) + bias_two.reshape(1, -1, 1, 1)
    output = (pre_two * jax.nn.sigmoid(pre_two)).astype(jnp.bfloat16)
    delta_two = (cotangent[None].astype(jnp.float32) * slope(pre_two)).astype(jnp.bfloat16)
    grad_two = kernel_grad(hidden_pad, delta_two)
    bias_grad_two = lax.optimization_barrier(jnp.sum(delta_two.astype(jnp.float32), axis=(0, 2, 3)))
    hidden_grad = convolve(pad_edges(delta_two), flipped(weight_two))
    delta_one = (hidden_grad * slope(pre_one)).astype(jnp.bfloat16)
    grad_one = kernel_grad(image_pad, delta_one)
    bias_grad_one = lax.optimization_barrier(jnp.sum(delta_one.astype(jnp.float32), axis=(0, 2, 3)))
    image_grad = convolve(pad_edges(delta_one), flipped(weight_one)).astype(jnp.bfloat16)
    return (output[0], image_grad[0], grad_one, bias_grad_one, grad_two, bias_grad_two)

def reference(image, weight_one, bias_one, weight_two, bias_two, cotangent):

    def per_slide(pair):
        return one_slide(pair[0], pair[1], weight_one, bias_one, weight_two, bias_two)
    results = lax.map(per_slide, (image, cotangent))
    factor = (SLIDES * NH * NW) ** (-0.5)
    return (results[0], results[1], lax.optimization_barrier(jnp.sum(results[2], axis=0)) * factor, lax.optimization_barrier(jnp.sum(results[3], axis=0)) * factor, lax.optimization_barrier(jnp.sum(results[4], axis=0)) * factor, lax.optimization_barrier(jnp.sum(results[5], axis=0)) * factor)
```

```python
import functools

import jax
import jax.numpy as jnp
from jax import lax
from jax.experimental import pallas as pl
from jax.experimental.pallas import tpu as pltpu
from jax.sharding import PartitionSpec as P

BF16 = jnp.bfloat16
F32 = jnp.float32
PARAMS = pltpu.CompilerParams(vmem_limit_bytes=56 * 1024 * 1024)
SUMMED = ("sy", "sx", "grp")


def shape_of(shape, dtype):
    return jax.ShapeDtypeStruct(shape, dtype)


def pack_kernel(image_ref, cot_ref, keep_i, keep_c, swap_i, swap_c, direct, cross, image_t, cot_t):
    side = lax.axis_index("sx")
    rows = image_ref.shape[2]
    half = rows // 2
    image_t[...] = jnp.transpose(image_ref[0], (1, 0, 2))
    cot_t[...] = jnp.transpose(cot_ref[0], (1, 0, 2))
    keep_i[...] = image_t[pl.ds(side * (half - 4), half + 4)]
    keep_c[...] = cot_t[pl.ds(side * (half - 2), half + 2)]
    swap_i[...] = image_t[pl.ds((1 - side) * (half - 4), half + 4)]
    swap_c[...] = cot_t[pl.ds((1 - side) * (half - 2), half + 2)]
    direct[0:4] = image_t[pl.ds((1 - side) * (rows - 4), 4)]
    direct[4:6] = cot_t[pl.ds((1 - side) * (rows - 2), 2)]
    cross[0:4] = image_t[pl.ds(side * (rows - 4), 4)]
    cross[4:6] = cot_t[pl.ds(side * (rows - 2), 2)]


def column(row):
    chans = row.shape[1]
    r = lax.broadcasted_iota(jnp.int32, (chans, chans), 0)
    c = lax.broadcasted_iota(jnp.int32, (chans, chans), 1)
    wide = jnp.broadcast_to(row, (chans, chans))
    return jnp.sum(jnp.where(r == c, wide, 0.0), axis=1, keepdims=True)


def weights_kernel(w1, b1, w2, b2, fwd1, fwd2, bwd2, bwd1, bias1, bias2):
    for w, fwd, bwd in ((w1, fwd1, bwd1), (w2, fwd2, bwd2)):
        for a in range(3):
            fwd[a * 64 : a * 64 + 64, :] = jnp.concatenate(
                [jnp.transpose(w[a, b].astype(F32)) for b in range(3)], axis=1
            ).astype(BF16)
            bwd[a * 64 : a * 64 + 64, :] = jnp.concatenate(
                [w[2 - a, 2 - b].astype(F32) for b in range(3)], axis=1
            ).astype(BF16)
    bias1[...] = jnp.broadcast_to(column(b1[...]), bias1.shape)
    bias2[...] = jnp.broadcast_to(column(b2[...]), bias2.shape)


def spread(dst, h, row):
    chans, width = row.shape
    zero = jnp.zeros((chans, 1), row.dtype)
    at = slice(h * width, (h + 1) * width)
    dst[0:chans, at] = jnp.concatenate([zero, row[:, :-1]], axis=1)
    dst[chans : 2 * chans, at] = row
    dst[2 * chans : 3 * chans, at] = jnp.concatenate([row[:, 1:], zero], axis=1)


def sweep(weight_ref, src, count, width, emit):
    weight = weight_ref[...]
    first = second = None
    for h in range(count):
        part = jnp.dot(
            weight, src[0:192, h * width : (h + 1) * width], preferred_element_type=F32
        )
        if h >= 2:
            emit(h - 1, first + part[128:192])
        first = part[64:128] if second is None else second + part[64:128]
        second = part[0:64]


def main_kernel(
    tile_units,
    keep_i,
    keep_c,
    swap_i,
    swap_c,
    direct,
    cross,
    fwd1,
    fwd2,
    bwd2,
    bwd1,
    bias1,
    bias2,
    mine,
    theirs,
    grads,
    image_s,
    cot_s,
    x3,
    h3,
    d3,
    da2,
    da1,
    e3,
    slopes,
):
    side = lax.axis_index("sx")
    place = lax.axis_index("sy")
    places = lax.axis_size("sy")
    half = mine.shape[1]
    width = 2 * mine.shape[3]
    total = places * 2 * half
    start = (2 * place + side) * half
    other = 1 - side
    image_s[side, pl.ds(4 * other, half + 4)] = keep_i[...]
    image_s[other, pl.ds(4 * other, half + 4)] = swap_i[...]
    cot_s[side, pl.ds(2 * other, half + 2)] = keep_c[...]
    cot_s[other, pl.ds(2 * other, half + 2)] = swap_c[...]
    image_s[side, pl.ds((half + 4) * side, 4)] = direct[0:4]
    image_s[other, pl.ds((half + 4) * side, 4)] = cross[0:4]
    cot_s[side, pl.ds((half + 2) * side, 2)] = direct[4:6]
    cot_s[other, pl.ds((half + 2) * side, 2)] = cross[4:6]

    ones = jnp.ones((16, x3.shape[1]), BF16)
    x3[192:208, :] = ones
    h3[192:208, :] = ones[:, : h3.shape[1]]
    blank = jnp.zeros((64, 2 * width), BF16)
    for da in (da2, da1):
        da[0:64, half * width :] = blank
        da[64:128, 0:width] = blank[:, :width]
        da[64:128, (half + 1) * width :] = blank[:, :width]
        da[128:192, 0 : 2 * width] = blank

    def inside(row):
        return jnp.logical_and(start + row >= 0, start + row < total)

    def store_delta(da, j, delta):
        for a in range(3):
            da[a * 64 : a * 64 + 64, (j + a) * width : (j + a + 1) * width] = delta

    def hand_out(slot, j, value):
        left, right = value[:, : width // 2], value[:, width // 2 :]
        own = jnp.where(side == 0, left, right)
        partner = jnp.where(side == 0, right, left)
        mine[slot, j] = own.astype(BF16)
        theirs[slot, j] = partner.astype(BF16)

    for e in range(half + 8):
        spread(x3, e, jnp.concatenate([image_s[0, e], image_s[1, e]], axis=1))

    shift1 = jnp.broadcast_to(bias1[:, 0:1], (64, width))
    shift2 = jnp.broadcast_to(bias2[:, 0:1], (64, width))

    def first(e, acc):
        pre = acc + shift1
        gate = jax.nn.sigmoid(pre)
        hidden = pre * gate
        if e < 4 or e >= half + 4:
            hidden = jnp.where(inside(e - 4), hidden, 0.0)
        spread(h3, e - 1, hidden.astype(BF16))
        if 3 <= e < half + 5:
            slopes[e - 3] = gate * (1.0 + pre * (1.0 - gate))

    sweep(fwd1, x3, half + 8, width, first)

    def second(f, acc):
        g = f - 1
        pre = acc + shift2
        gate = jax.nn.sigmoid(pre)
        cot = jnp.concatenate([cot_s[0, g], cot_s[1, g]], axis=1).astype(F32)
        delta = (cot * (gate * (1.0 + pre * (1.0 - gate)))).astype(BF16)
        spread(d3, g, delta)
        if 2 <= g < half + 2:
            hand_out(0, g - 2, pre * gate)
            store_delta(da2, g - 2, delta)

    sweep(fwd2, h3, half + 6, width, second)

    def third(g, acc):
        k = g - 1
        delta = acc * slopes[k]
        if k == 0 or k == half + 1:
            delta = jnp.where(inside(k - 1), delta, 0.0)
        delta = delta.astype(BF16)
        spread(e3, k, delta)
        if 1 <= k < half + 1:
            store_delta(da1, k - 1, delta)

    sweep(bwd2, d3, half + 4, width, third)

    def fourth(k, acc):
        hand_out(1, k - 1, acc)

    sweep(bwd1, e3, half + 2, width, fourth)

    contract = (((1,), (1,)), ((), ()))
    long = (half + 2) * width
    grad2 = lax.dot_general(
        h3[:, 2 * width : 2 * width + long], da2[...], contract, preferred_element_type=F32
    )
    grad1 = lax.dot_general(
        x3[:, 3 * width : 3 * width + long], da1[...], contract, preferred_element_type=F32
    )
    both = jnp.concatenate([grad2[0:192], grad1[0:192]], axis=1)
    biases = jnp.concatenate([grad2[192:200, 64:128], grad1[192:200, 64:128]], axis=1)
    tiles = [both[8 * (t // 3) : 8 * (t // 3) + 8, 128 * (t % 3) : 128 * (t % 3) + 128] for t in range(72)]
    tiles.append(biases)
    for j in range(grads.shape[0]):
        held = tiles[j * tile_units : (j + 1) * tile_units]
        held = held + [jnp.zeros((8, 128), F32)] * (tile_units - len(held))
        grads[j] = jnp.concatenate(held, axis=1).astype(BF16)


def sum_kernel(factor, parts, out):
    total = parts[0].astype(F32)
    for j in range(1, parts.shape[0]):
        total = total + parts[j].astype(F32)
    scaled = (total * factor).astype(BF16)
    for j in range(out.shape[0]):
        out[j] = scaled


def finish_kernel(tile_units, mine, back, gathered, out, image_grad, gw1, gb1, gw2, gb2):
    side = lax.axis_index("sx")
    half = mine.shape[1]
    here = pl.ds(pl.multiple_of(side * half, half), half)
    there = pl.ds(pl.multiple_of((1 - side) * half, half), half)
    for slot, ref in ((0, out), (1, image_grad)):
        ref[0, :, here, :] = jnp.transpose(mine[slot], (1, 0, 2))
        ref[0, :, there, :] = jnp.transpose(back[slot], (1, 0, 2))

    def tile(t):
        at = (t % tile_units) * 128
        return gathered[t // tile_units][:, at : at + 128].astype(F32)

    for block in range(24):
        line = jnp.concatenate([tile(3 * block + p) for p in range(3)], axis=1)
        b, i = block // 8, (block % 8) * 8
        for a in range(3):
            gw2[a, b, i : i + 8, :] = line[:, a * 64 : a * 64 + 64]
            gw1[a, b, i : i + 8, :] = line[:, 192 + a * 64 : 256 + a * 64]
    biases = tile(72)
    gb2[...] = biases[0:1, 0:64]
    gb1[...] = biases[0:1, 64:128]


def local(image, weight_one, bias_one, weight_two, bias_two, cotangent):
    _, chans, rows, cols = image.shape
    places, sides = lax.axis_size("sy"), lax.axis_size("sx")
    count = places * sides * lax.axis_size("grp")
    half = rows // 2
    width = 2 * cols
    factor = float(rows * cols * count) ** (-0.5)

    keep_i, keep_c, swap_i, swap_c, direct, cross = pl.pallas_call(
        pack_kernel,
        out_shape=[
            shape_of((half + 4, chans, cols), BF16),
            shape_of((half + 2, chans, cols), BF16),
            shape_of((half + 4, chans, cols), BF16),
            shape_of((half + 2, chans, cols), BF16),
            shape_of((6, chans, cols), BF16),
            shape_of((6, chans, cols), BF16),
        ],
        scratch_shapes=[
            pltpu.VMEM((rows, chans, cols), BF16),
            pltpu.VMEM((rows, chans, cols), BF16),
        ],
        compiler_params=PARAMS,
        name="pack",
    )(image, cotangent)
    fwd1, fwd2, bwd2, bwd1, bias1, bias2 = pl.pallas_call(
        weights_kernel,
        out_shape=[shape_of((192, 192), BF16)] * 4 + [shape_of((64, 128), F32)] * 2,
        compiler_params=PARAMS,
        name="weights",
    )(weight_one, bias_one.reshape(1, chans), weight_two, bias_two.reshape(1, chans))

    down = [(2 * s, 2 * s + 2) for s in range(places - 1)]
    up = [(2 * s + 3, 2 * s + 1) for s in range(places - 1)]
    down_cross = [(2 * s + 1, 2 * s + 2) for s in range(places - 1)]
    up_cross = [(2 * s + 2, 2 * s + 1) for s in range(places - 1)]
    direct = lax.ppermute(direct, ("sy", "sx"), down + up)
    cross = lax.ppermute(cross, ("sy", "sx"), down_cross + up_cross)
    swap = [(0, 1), (1, 0)]
    swap_i = lax.ppermute(swap_i, "sx", swap)
    swap_c = lax.ppermute(swap_c, "sx", swap)

    units = -(-73 // count)
    lanes = units * 128
    pieces = shape_of((2, half, chans, cols), BF16)
    mine, theirs, grads = pl.pallas_call(
        functools.partial(main_kernel, units),
        out_shape=[pieces, pieces, shape_of((count, 8, lanes), BF16)],
        scratch_shapes=[
            pltpu.VMEM((2, half + 8, chans, cols), BF16),
            pltpu.VMEM((2, half + 4, chans, cols), BF16),
            pltpu.VMEM((208, (half + 8) * width), BF16),
            pltpu.VMEM((208, (half + 6) * width), BF16),
            pltpu.VMEM((192, (half + 4) * width), BF16),
            pltpu.VMEM((192, (half + 2) * width), BF16),
            pltpu.VMEM((192, (half + 2) * width), BF16),
            pltpu.VMEM((192, (half + 2) * width), BF16),
            pltpu.VMEM((half + 2, chans, width), F32),
        ],
        compiler_params=PARAMS,
        name="blocks",
    )(keep_i, keep_c, swap_i, swap_c, direct, cross, fwd1, fwd2, bwd2, bwd1, bias1, bias2)

    back = lax.ppermute(theirs, "sx", swap)
    parts = lax.all_to_all(grads, SUMMED, 0, 0, tiled=True)
    spread_out = pl.pallas_call(
        functools.partial(sum_kernel, factor),
        out_shape=shape_of((count, 8, lanes), BF16),
        compiler_params=PARAMS,
        name="add",
    )(parts)
    gathered = lax.all_to_all(spread_out, SUMMED, 0, 0, tiled=True)
    weight_shape = shape_of((3, 3, chans, chans), F32)
    out, image_grad, gw1, gb1, gw2, gb2 = pl.pallas_call(
        functools.partial(finish_kernel, units),
        out_shape=[
            shape_of(image.shape, BF16),
            shape_of(image.shape, BF16),
            weight_shape,
            shape_of((1, chans), F32),
            weight_shape,
            shape_of((1, chans), F32),
        ],
        compiler_params=PARAMS,
        name="finish",
    )(mine, back, gathered)
    return out, image_grad, gw1, gb1.reshape(chans), gw2, gb2.reshape(chans)


def solution(mesh):
    return jax.shard_map(
        local,
        mesh=mesh,
        in_specs=(P("grp", None, "sy", "sx"), P(), P(), P(), P(), P("grp", None, "sy", "sx")),
        out_specs=(P("grp", None, "sy", "sx"), P("grp", None, "sy", "sx"), P(), P(), P(), P()),
        check_vma=False,
    )
```

```python
import functools

import jax
import jax.numpy as jnp
from jax import lax
from jax.experimental import pallas as pl
from jax.experimental.pallas import tpu as pltpu
from jax.sharding import PartitionSpec as P

BF16 = jnp.bfloat16
F32 = jnp.float32
PARAMS = pltpu.CompilerParams(vmem_limit_bytes=40 * 1024 * 1024)
CHIPS = ("sy", "grp")
SWAP = [(0, 1), (1, 0)]


def shape_of(shape, dtype):
    return jax.ShapeDtypeStruct(shape, dtype)


def near(*arrays):
    return [pltpu.with_memory_space_constraint(array, pltpu.VMEM) for array in arrays]


def pack_kernel(image_ref, cot_ref, keep_i, keep_c, swap_i, swap_c, direct, cross, image_t, cot_t):
    side = lax.axis_index("sx")
    rows = image_ref.shape[2]
    half = rows // 2
    image_t[...] = jnp.transpose(image_ref[0], (1, 0, 2))
    cot_t[...] = jnp.transpose(cot_ref[0], (1, 0, 2))
    keep_i[...] = image_t[pl.ds(side * (half - 4), half + 4)]
    keep_c[...] = cot_t[pl.ds(side * (half - 2), half + 2)]
    swap_i[...] = image_t[pl.ds((1 - side) * (half - 4), half + 4)]
    swap_c[...] = cot_t[pl.ds((1 - side) * (half - 2), half + 2)]
    direct[0:4] = image_t[pl.ds((1 - side) * (rows - 4), 4)]
    direct[4:6] = cot_t[pl.ds((1 - side) * (rows - 2), 2)]
    cross[0:4] = image_t[pl.ds(side * (rows - 4), 4)]
    cross[4:6] = cot_t[pl.ds(side * (rows - 2), 2)]


def column(row):
    chans = row.shape[1]
    r = lax.broadcasted_iota(jnp.int32, (chans, chans), 0)
    c = lax.broadcasted_iota(jnp.int32, (chans, chans), 1)
    wide = jnp.broadcast_to(row, (chans, chans))
    return jnp.sum(jnp.where(r == c, wide, 0.0), axis=1, keepdims=True)


def weights_kernel(w1, b1, w2, b2, fwd1, fwd2, bwd2, bwd1, bias1, bias2):
    for w, fwd, bwd in ((w1, fwd1, bwd1), (w2, fwd2, bwd2)):
        for a in range(3):
            fwd[a * 64 : a * 64 + 64, :] = jnp.concatenate(
                [jnp.transpose(w[a, b].astype(F32)) for b in range(3)], axis=1
            ).astype(BF16)
            bwd[a * 64 : a * 64 + 64, :] = jnp.concatenate(
                [w[2 - a, 2 - b].astype(F32) for b in range(3)], axis=1
            ).astype(BF16)
    bias1[...] = jnp.broadcast_to(column(b1[...]), bias1.shape)
    bias2[...] = jnp.broadcast_to(column(b2[...]), bias2.shape)


def spread(dst, h, row):
    chans, width = row.shape
    zero = jnp.zeros((chans, 1), row.dtype)
    at = slice(h * width, (h + 1) * width)
    dst[0:chans, at] = jnp.concatenate([zero, row[:, :-1]], axis=1)
    dst[chans : 2 * chans, at] = row
    dst[2 * chans : 3 * chans, at] = jnp.concatenate([row[:, 1:], zero], axis=1)


def sweep(weight_ref, src, count, width, emit):
    weight = weight_ref[...]
    first = second = None
    for h in range(count):
        part = jnp.dot(
            weight, src[0:192, h * width : (h + 1) * width], preferred_element_type=F32
        )
        if h >= 2:
            emit(h - 1, first + part[128:192])
        first = part[64:128] if second is None else second + part[64:128]
        second = part[0:64]


def main_kernel(
    tile_units,
    keep_i,
    keep_c,
    swap_i,
    swap_c,
    direct,
    cross,
    fwd1,
    fwd2,
    bwd2,
    bwd1,
    bias1,
    bias2,
    mine,
    theirs,
    grads_own,
    grads_send,
    image_s,
    cot_s,
    x3,
    h3,
    d3,
    da2,
    da1,
    e3,
    slopes,
):
    side = lax.axis_index("sx")
    place = lax.axis_index("sy")
    places = lax.axis_size("sy")
    half = mine.shape[1]
    width = 2 * mine.shape[3]
    total = places * 2 * half
    start = (2 * place + side) * half
    other = 1 - side
    image_s[side, pl.ds(4 * other, half + 4)] = keep_i[...]
    image_s[other, pl.ds(4 * other, half + 4)] = swap_i[...]
    cot_s[side, pl.ds(2 * other, half + 2)] = keep_c[...]
    cot_s[other, pl.ds(2 * other, half + 2)] = swap_c[...]
    image_s[side, pl.ds((half + 4) * side, 4)] = direct[0:4]
    image_s[other, pl.ds((half + 4) * side, 4)] = cross[0:4]
    cot_s[side, pl.ds((half + 2) * side, 2)] = direct[4:6]
    cot_s[other, pl.ds((half + 2) * side, 2)] = cross[4:6]

    ones = jnp.ones((16, x3.shape[1]), BF16)
    x3[192:208, :] = ones
    h3[192:208, :] = ones[:, : h3.shape[1]]
    blank = jnp.zeros((64, 2 * width), BF16)
    for da in (da2, da1):
        da[0:64, half * width :] = blank
        da[64:128, 0:width] = blank[:, :width]
        da[64:128, (half + 1) * width :] = blank[:, :width]
        da[128:192, 0 : 2 * width] = blank

    def inside(row):
        return jnp.logical_and(start + row >= 0, start + row < total)

    def store_delta(da, j, delta):
        for a in range(3):
            da[a * 64 : a * 64 + 64, (j + a) * width : (j + a + 1) * width] = delta

    def hand_out(slot, j, value):
        left, right = value[:, : width // 2], value[:, width // 2 :]
        own = jnp.where(side == 0, left, right)
        partner = jnp.where(side == 0, right, left)
        mine[slot, j] = own.astype(BF16)
        theirs[slot, j] = partner.astype(BF16)

    for e in range(half + 8):
        spread(x3, e, jnp.concatenate([image_s[0, e], image_s[1, e]], axis=1))

    shift1 = jnp.broadcast_to(bias1[:, 0:1], (64, width))
    shift2 = jnp.broadcast_to(bias2[:, 0:1], (64, width))

    def first(e, acc):
        pre = acc + shift1
        gate = jax.nn.sigmoid(pre)
        hidden = pre * gate
        if e < 4 or e >= half + 4:
            hidden = jnp.where(inside(e - 4), hidden, 0.0)
        spread(h3, e - 1, hidden.astype(BF16))
        if 3 <= e < half + 5:
            slopes[e - 3] = gate * (1.0 + pre * (1.0 - gate))

    sweep(fwd1, x3, half + 8, width, first)

    def second(f, acc):
        g = f - 1
        pre = acc + shift2
        gate = jax.nn.sigmoid(pre)
        cot = jnp.concatenate([cot_s[0, g], cot_s[1, g]], axis=1).astype(F32)
        delta = (cot * (gate * (1.0 + pre * (1.0 - gate)))).astype(BF16)
        spread(d3, g, delta)
        if 2 <= g < half + 2:
            hand_out(0, g - 2, pre * gate)
            store_delta(da2, g - 2, delta)

    sweep(fwd2, h3, half + 6, width, second)

    def third(g, acc):
        k = g - 1
        delta = acc * slopes[k]
        if k == 0 or k == half + 1:
            delta = jnp.where(inside(k - 1), delta, 0.0)
        delta = delta.astype(BF16)
        spread(e3, k, delta)
        if 1 <= k < half + 1:
            store_delta(da1, k - 1, delta)

    sweep(bwd2, d3, half + 4, width, third)

    def fourth(k, acc):
        hand_out(1, k - 1, acc)

    sweep(bwd1, e3, half + 2, width, fourth)

    contract = (((1,), (1,)), ((), ()))
    long = (half + 2) * width
    grad2 = lax.dot_general(
        h3[:, 2 * width : 2 * width + long], da2[...], contract, preferred_element_type=F32
    )
    grad1 = lax.dot_general(
        x3[:, 3 * width : 3 * width + long], da1[...], contract, preferred_element_type=F32
    )
    both = jnp.concatenate([grad2[0:192], grad1[0:192]], axis=1)
    biases = jnp.concatenate([grad2[192:200, 64:128], grad1[192:200, 64:128]], axis=1)
    tiles = [
        both[8 * (t // 3) : 8 * (t // 3) + 8, 128 * (t % 3) : 128 * (t % 3) + 128]
        for t in range(72)
    ]
    empty = jnp.zeros((8, 128), F32)
    low, high = tiles[:36] + [biases], tiles[36:]
    for j in range(grads_own.shape[0]):
        pair = []
        for part in (low, high):
            held = part[j * tile_units : (j + 1) * tile_units]
            pair.append(jnp.concatenate(held + [empty] * (tile_units - len(held)), axis=1))
        grads_own[j] = jnp.where(side == 0, pair[0], pair[1])
        grads_send[j] = jnp.where(side == 0, pair[1], pair[0])


def pair_kernel(own, received, out):
    out[...] = (own[...] + received[...]).astype(BF16)


def sum_kernel(factor, parts, out):
    total = parts[0].astype(F32)
    for j in range(1, parts.shape[0]):
        total = total + parts[j].astype(F32)
    scaled = (total * factor).astype(BF16)
    for j in range(out.shape[0]):
        out[j] = scaled


def outputs_kernel(mine, back, out, image_grad):
    side = lax.axis_index("sx")
    half = mine.shape[1]
    here = pl.ds(pl.multiple_of(side * half, half), half)
    there = pl.ds(pl.multiple_of((1 - side) * half, half), half)
    for slot, ref in ((0, out), (1, image_grad)):
        ref[0, :, here, :] = jnp.transpose(mine[slot], (1, 0, 2))
        ref[0, :, there, :] = jnp.transpose(back[slot], (1, 0, 2))


def grads_kernel(tile_units, gathered, swapped, gw1, gb1, gw2, gb2):
    side = lax.axis_index("sx")

    def tile(part, t):
        at = (t % tile_units) * 128
        here = gathered[t // tile_units][:, at : at + 128].astype(F32)
        there = swapped[t // tile_units][:, at : at + 128].astype(F32)
        return jnp.where(side == part, here, there)

    for block in range(24):
        part, first = block // 12, 3 * (block % 12)
        line = jnp.concatenate([tile(part, first + p) for p in range(3)], axis=1)
        b, i = block // 8, (block % 8) * 8
        for a in range(3):
            gw2[a, b, i : i + 8, :] = line[:, a * 64 : a * 64 + 64]
            gw1[a, b, i : i + 8, :] = line[:, 192 + a * 64 : 256 + a * 64]
    biases = tile(0, 36)
    gb2[...] = biases[0:1, 0:64]
    gb1[...] = biases[0:1, 64:128]


def local(image, weight_one, bias_one, weight_two, bias_two, cotangent):
    _, chans, rows, cols = image.shape
    places, sides = lax.axis_size("sy"), lax.axis_size("sx")
    count = places * sides * lax.axis_size("grp")
    half = rows // 2
    width = 2 * cols
    factor = float(rows * cols * count) ** (-0.5)

    keep_i, keep_c, swap_i, swap_c, direct, cross = pl.pallas_call(
        pack_kernel,
        out_shape=[
            pltpu.VMEM((half + 4, chans, cols), BF16),
            pltpu.VMEM((half + 2, chans, cols), BF16),
            pltpu.VMEM((half + 4, chans, cols), BF16),
            pltpu.VMEM((half + 2, chans, cols), BF16),
            pltpu.VMEM((6, chans, cols), BF16),
            pltpu.VMEM((6, chans, cols), BF16),
        ],
        scratch_shapes=[
            pltpu.VMEM((rows, chans, cols), BF16),
            pltpu.VMEM((rows, chans, cols), BF16),
        ],
        compiler_params=PARAMS,
        name="pack",
    )(image, cotangent)
    fwd1, fwd2, bwd2, bwd1, bias1, bias2 = pl.pallas_call(
        weights_kernel,
        out_shape=[pltpu.VMEM((192, 192), BF16)] * 4 + [pltpu.VMEM((64, 128), F32)] * 2,
        compiler_params=PARAMS,
        name="weights",
    )(weight_one, bias_one.reshape(1, chans), weight_two, bias_two.reshape(1, chans))

    down = [(2 * s, 2 * s + 2) for s in range(places - 1)]
    up = [(2 * s + 3, 2 * s + 1) for s in range(places - 1)]
    down_cross = [(2 * s + 1, 2 * s + 2) for s in range(places - 1)]
    up_cross = [(2 * s + 2, 2 * s + 1) for s in range(places - 1)]
    direct = lax.ppermute(direct, ("sy", "sx"), down + up)
    cross = lax.ppermute(cross, ("sy", "sx"), down_cross + up_cross)
    swap_i = lax.ppermute(swap_i, "sx", SWAP)
    swap_c = lax.ppermute(swap_c, "sx", SWAP)

    chips = count // sides
    units = -(-37 // chips)
    lanes = units * 128
    pieces = pltpu.VMEM((2, half, chans, cols), BF16)
    mine, theirs, grads_own, grads_send = pl.pallas_call(
        functools.partial(main_kernel, units),
        out_shape=[pieces, pieces] + [pltpu.VMEM((chips, 8, lanes), F32)] * 2,
        scratch_shapes=[
            pltpu.VMEM((2, half + 8, chans, cols), BF16),
            pltpu.VMEM((2, half + 4, chans, cols), BF16),
            pltpu.VMEM((208, (half + 8) * width), BF16),
            pltpu.VMEM((208, (half + 6) * width), BF16),
            pltpu.VMEM((192, (half + 4) * width), BF16),
            pltpu.VMEM((192, (half + 2) * width), BF16),
            pltpu.VMEM((192, (half + 2) * width), BF16),
            pltpu.VMEM((192, (half + 2) * width), BF16),
            pltpu.VMEM((half + 2, chans, width), F32),
        ],
        compiler_params=PARAMS,
        name="blocks",
    )(
        *near(keep_i, keep_c, swap_i, swap_c, direct, cross),
        *near(fwd1, fwd2, bwd2, bwd1, bias1, bias2),
    )

    grads_received = lax.ppermute(grads_send, "sx", SWAP)
    back = lax.ppermute(theirs, "sx", SWAP)
    pieces = pltpu.VMEM((chips, 8, lanes), BF16)
    pair = pl.pallas_call(
        pair_kernel, out_shape=pieces, compiler_params=PARAMS, name="pair"
    )(*near(grads_own, grads_received))
    parts = lax.all_to_all(pair, CHIPS, 0, 0, tiled=True)
    out, image_grad = pl.pallas_call(
        outputs_kernel,
        out_shape=[shape_of(image.shape, BF16)] * 2,
        compiler_params=PARAMS,
        name="outputs",
    )(*near(mine, back))
    total = pl.pallas_call(
        functools.partial(sum_kernel, factor),
        out_shape=pieces,
        compiler_params=PARAMS,
        name="add",
    )(*near(parts))
    gathered = lax.all_to_all(total, CHIPS, 0, 0, tiled=True)
    swapped = lax.ppermute(gathered, "sx", SWAP)
    weight_shape = shape_of((3, 3, chans, chans), F32)
    bias_shape = shape_of((1, chans), F32)
    gw1, gb1, gw2, gb2 = pl.pallas_call(
        functools.partial(grads_kernel, units),
        out_shape=[weight_shape, bias_shape, weight_shape, bias_shape],
        compiler_params=PARAMS,
        name="grads",
    )(*near(gathered, swapped))
    return out, image_grad, gw1, gb1.reshape(chans), gw2, gb2.reshape(chans)


def solution(mesh):
    return jax.shard_map(
        local,
        mesh=mesh,
        in_specs=(P("grp", None, "sy", "sx"), P(), P(), P(), P(), P("grp", None, "sy", "sx")),
        out_specs=(P("grp", None, "sy", "sx"), P("grp", None, "sy", "sx"), P(), P(), P(), P()),
        check_vma=False,
    )
```

```python
import functools

import jax
import jax.numpy as jnp
from jax import lax
from jax.experimental import pallas as pl
from jax.experimental.pallas import tpu as pltpu
from jax.sharding import PartitionSpec as P

BF16 = jnp.bfloat16
F32 = jnp.float32
PARAMS = pltpu.CompilerParams(vmem_limit_bytes=40 * 1024 * 1024)
SWAP = [(0, 1), (1, 0)]


def shape_of(shape, dtype):
    return jax.ShapeDtypeStruct(shape, dtype)


def near(*arrays):
    return [pltpu.with_memory_space_constraint(array, pltpu.VMEM) for array in arrays]


def pack_kernel(
    image_ref,
    cot_ref,
    keep_i,
    keep_c,
    swap_i,
    swap_c,
    direct,
    cross,
    image_v,
    cot_v,
    image_t,
    cot_t,
    sems,
):
    side = lax.axis_index("sx")
    rows = image_ref.shape[2]
    half = rows // 2
    jobs = []
    for c in range(image_ref.shape[1] // 16):
        for n, (src, dst, out) in enumerate(((image_ref, image_v, image_t), (cot_ref, cot_v, cot_t))):
            chans = slice(16 * c, 16 * c + 16)
            copy = pltpu.make_async_copy(src.at[0, chans], dst.at[chans], sems.at[2 * c + n])
            copy.start()
            jobs.append((copy, chans, dst, out))
    for copy, chans, dst, out in jobs:
        copy.wait()
        out[:, chans, :] = jnp.transpose(dst[chans], (1, 0, 2))
    keep_i[...] = image_t[pl.ds(side * (half - 4), half + 4)]
    keep_c[...] = cot_t[pl.ds(side * (half - 2), half + 2)]
    swap_i[...] = image_t[pl.ds((1 - side) * (half - 4), half + 4)]
    swap_c[...] = cot_t[pl.ds((1 - side) * (half - 2), half + 2)]
    direct[0:4] = image_t[pl.ds((1 - side) * (rows - 4), 4)]
    direct[4:6] = cot_t[pl.ds((1 - side) * (rows - 2), 2)]
    cross[0:4] = image_t[pl.ds(side * (rows - 4), 4)]
    cross[4:6] = cot_t[pl.ds(side * (rows - 2), 2)]


def column(row):
    chans = row.shape[1]
    r = lax.broadcasted_iota(jnp.int32, (chans, chans), 0)
    c = lax.broadcasted_iota(jnp.int32, (chans, chans), 1)
    wide = jnp.broadcast_to(row, (chans, chans))
    return jnp.sum(jnp.where(r == c, wide, 0.0), axis=1, keepdims=True)


def weights_kernel(w1, b1, w2, b2, fwd1, fwd2, bwd2, bwd1, bias1, bias2):
    for w, fwd, bwd in ((w1, fwd1, bwd1), (w2, fwd2, bwd2)):
        for a in range(3):
            fwd[a * 64 : a * 64 + 64, :] = jnp.concatenate(
                [jnp.transpose(w[a, b].astype(F32)) for b in range(3)], axis=1
            ).astype(BF16)
            bwd[a * 64 : a * 64 + 64, :] = jnp.concatenate(
                [w[2 - a, 2 - b].astype(F32) for b in range(3)], axis=1
            ).astype(BF16)
    bias1[...] = jnp.broadcast_to(column(b1[...]), bias1.shape)
    bias2[...] = jnp.broadcast_to(column(b2[...]), bias2.shape)


def spread(dst, h, row):
    chans, width = row.shape
    zero = jnp.zeros((chans, 1), row.dtype)
    at = slice(h * width, (h + 1) * width)
    dst[0:chans, at] = jnp.concatenate([zero, row[:, :-1]], axis=1)
    dst[chans : 2 * chans, at] = row
    dst[2 * chans : 3 * chans, at] = jnp.concatenate([row[:, 1:], zero], axis=1)


def sweep(weight_ref, src, count, width, emit):
    weight = weight_ref[...]
    first = second = None
    for h in range(count):
        part = jnp.dot(
            weight, src[0:192, h * width : (h + 1) * width], preferred_element_type=F32
        )
        if h >= 2:
            emit(h - 1, first + part[128:192])
        first = part[64:128] if second is None else second + part[64:128]
        second = part[0:64]


def main_kernel(
    tile_units,
    keep_i,
    keep_c,
    swap_i,
    swap_c,
    direct,
    cross,
    fwd1,
    fwd2,
    bwd2,
    bwd1,
    bias1,
    bias2,
    mine,
    theirs,
    grads_own,
    grads_send,
    image_s,
    cot_s,
    x3,
    h3,
    d3,
    da2,
    da1,
    e3,
    slopes,
):
    side = lax.axis_index("sx")
    place = lax.axis_index("sy")
    places = lax.axis_size("sy")
    half = mine.shape[1]
    width = 2 * mine.shape[3]
    total = places * 2 * half
    start = (2 * place + side) * half
    other = 1 - side
    image_s[side, pl.ds(4 * other, half + 4)] = keep_i[...]
    image_s[other, pl.ds(4 * other, half + 4)] = swap_i[...]
    cot_s[side, pl.ds(2 * other, half + 2)] = keep_c[...]
    cot_s[other, pl.ds(2 * other, half + 2)] = swap_c[...]
    image_s[side, pl.ds((half + 4) * side, 4)] = direct[0:4]
    image_s[other, pl.ds((half + 4) * side, 4)] = cross[0:4]
    cot_s[side, pl.ds((half + 2) * side, 2)] = direct[4:6]
    cot_s[other, pl.ds((half + 2) * side, 2)] = cross[4:6]

    ones = jnp.ones((16, x3.shape[1]), BF16)
    x3[192:208, :] = ones
    h3[192:208, :] = ones[:, : h3.shape[1]]
    blank = jnp.zeros((64, 2 * width), BF16)
    for da in (da2, da1):
        da[0:64, half * width :] = blank
        da[64:128, 0:width] = blank[:, :width]
        da[64:128, (half + 1) * width :] = blank[:, :width]
        da[128:192, 0 : 2 * width] = blank

    def inside(row):
        return jnp.logical_and(start + row >= 0, start + row < total)

    def store_delta(da, j, delta):
        for a in range(3):
            da[a * 64 : a * 64 + 64, (j + a) * width : (j + a + 1) * width] = delta

    def hand_out(slot, j, value):
        left, right = value[:, : width // 2], value[:, width // 2 :]
        own = jnp.where(side == 0, left, right)
        partner = jnp.where(side == 0, right, left)
        mine[slot, j] = own.astype(BF16)
        theirs[slot, j] = partner.astype(BF16)

    for e in range(half + 8):
        spread(x3, e, jnp.concatenate([image_s[0, e], image_s[1, e]], axis=1))

    shift1 = jnp.broadcast_to(bias1[:, 0:1], (64, width))
    shift2 = jnp.broadcast_to(bias2[:, 0:1], (64, width))

    def first(e, acc):
        pre = acc + shift1
        gate = jax.nn.sigmoid(pre)
        hidden = pre * gate
        if e < 4 or e >= half + 4:
            hidden = jnp.where(inside(e - 4), hidden, 0.0)
        spread(h3, e - 1, hidden.astype(BF16))
        if 3 <= e < half + 5:
            slopes[e - 3] = gate * (1.0 + pre * (1.0 - gate))

    sweep(fwd1, x3, half + 8, width, first)

    def second(f, acc):
        g = f - 1
        pre = acc + shift2
        gate = jax.nn.sigmoid(pre)
        cot = jnp.concatenate([cot_s[0, g], cot_s[1, g]], axis=1).astype(F32)
        delta = (cot * (gate * (1.0 + pre * (1.0 - gate)))).astype(BF16)
        spread(d3, g, delta)
        if 2 <= g < half + 2:
            hand_out(0, g - 2, pre * gate)
            store_delta(da2, g - 2, delta)

    sweep(fwd2, h3, half + 6, width, second)

    def third(g, acc):
        k = g - 1
        delta = acc * slopes[k]
        if k == 0 or k == half + 1:
            delta = jnp.where(inside(k - 1), delta, 0.0)
        delta = delta.astype(BF16)
        spread(e3, k, delta)
        if 1 <= k < half + 1:
            store_delta(da1, k - 1, delta)

    sweep(bwd2, d3, half + 4, width, third)

    def fourth(k, acc):
        hand_out(1, k - 1, acc)

    sweep(bwd1, e3, half + 2, width, fourth)

    contract = (((1,), (1,)), ((), ()))
    long = (half + 2) * width
    grad2 = lax.dot_general(
        h3[:, 2 * width : 2 * width + long], da2[...], contract, preferred_element_type=F32
    )
    grad1 = lax.dot_general(
        x3[:, 3 * width : 3 * width + long], da1[...], contract, preferred_element_type=F32
    )
    both = jnp.concatenate([grad2[0:192], grad1[0:192]], axis=1)
    biases = jnp.concatenate([grad2[192:200, 64:128], grad1[192:200, 64:128]], axis=1)
    tiles = [
        both[8 * (t // 3) : 8 * (t // 3) + 8, 128 * (t % 3) : 128 * (t % 3) + 128]
        for t in range(72)
    ]
    empty = jnp.zeros((8, 128), F32)
    low, high = tiles[:36] + [biases], tiles[36:]
    for j in range(grads_own.shape[0]):
        pair = []
        for part in (low, high):
            held = part[j * tile_units : (j + 1) * tile_units]
            pair.append(jnp.concatenate(held + [empty] * (tile_units - len(held)), axis=1))
        grads_own[j] = jnp.where(side == 0, pair[0], pair[1])
        grads_send[j] = jnp.where(side == 0, pair[1], pair[0])


def pair_kernel(own, received, out):
    out[...] = (own[...] + received[...]).astype(BF16)


def sum_kernel(factor, parts, out):
    total = parts[0].astype(F32)
    for j in range(1, parts.shape[0]):
        total = total + parts[j].astype(F32)
    scaled = (total * factor).astype(BF16)
    for j in range(out.shape[0]):
        out[j] = scaled


def outputs_kernel(mine, back, out, image_grad):
    side = lax.axis_index("sx")
    half = mine.shape[1]
    here = pl.ds(pl.multiple_of(side * half, half), half)
    there = pl.ds(pl.multiple_of((1 - side) * half, half), half)
    for slot, ref in ((0, out), (1, image_grad)):
        ref[0, :, here, :] = jnp.transpose(mine[slot], (1, 0, 2))
        ref[0, :, there, :] = jnp.transpose(back[slot], (1, 0, 2))


def grads_kernel(tile_units, gathered, swapped, gw1, gb1, gw2, gb2):
    side = lax.axis_index("sx")

    def tile(part, t):
        at = (t % tile_units) * 128
        here = gathered[t // tile_units][:, at : at + 128].astype(F32)
        there = swapped[t // tile_units][:, at : at + 128].astype(F32)
        return jnp.where(side == part, here, there)

    for block in range(24):
        part, first = block // 12, 3 * (block % 12)
        line = jnp.concatenate([tile(part, first + p) for p in range(3)], axis=1)
        b, i = block // 8, (block % 8) * 8
        for a in range(3):
            gw2[a, b, i : i + 8, :] = line[:, a * 64 : a * 64 + 64]
            gw1[a, b, i : i + 8, :] = line[:, 192 + a * 64 : 256 + a * 64]
    biases = tile(0, 36)
    gb2[...] = biases[0:1, 0:64]
    gb1[...] = biases[0:1, 64:128]


def local(image, weight_one, bias_one, weight_two, bias_two, cotangent):
    _, chans, rows, cols = image.shape
    places, sides = lax.axis_size("sy"), lax.axis_size("sx")
    count = places * sides * lax.axis_size("grp")
    half = rows // 2
    width = 2 * cols
    factor = float(rows * cols * count) ** (-0.5)

    keep_i, keep_c, swap_i, swap_c, direct, cross = pl.pallas_call(
        pack_kernel,
        out_shape=[
            pltpu.VMEM((half + 4, chans, cols), BF16),
            pltpu.VMEM((half + 2, chans, cols), BF16),
            pltpu.VMEM((half + 4, chans, cols), BF16),
            pltpu.VMEM((half + 2, chans, cols), BF16),
            pltpu.VMEM((6, chans, cols), BF16),
            pltpu.VMEM((6, chans, cols), BF16),
        ],
        in_specs=[pl.BlockSpec(memory_space=pltpu.HBM)] * 2,
        scratch_shapes=[
            pltpu.VMEM((chans, rows, cols), BF16),
            pltpu.VMEM((chans, rows, cols), BF16),
            pltpu.VMEM((rows, chans, cols), BF16),
            pltpu.VMEM((rows, chans, cols), BF16),
            pltpu.SemaphoreType.DMA((chans // 8,)),
        ],
        compiler_params=PARAMS,
        name="pack",
    )(*[pltpu.with_memory_space_constraint(array, pltpu.HBM) for array in (image, cotangent)])
    fwd1, fwd2, bwd2, bwd1, bias1, bias2 = pl.pallas_call(
        weights_kernel,
        out_shape=[pltpu.VMEM((192, 192), BF16)] * 4 + [pltpu.VMEM((64, 128), F32)] * 2,
        compiler_params=PARAMS,
        name="weights",
    )(weight_one, bias_one.reshape(1, chans), weight_two, bias_two.reshape(1, chans))

    down = [(2 * s, 2 * s + 2) for s in range(places - 1)]
    up = [(2 * s + 3, 2 * s + 1) for s in range(places - 1)]
    down_cross = [(2 * s + 1, 2 * s + 2) for s in range(places - 1)]
    up_cross = [(2 * s + 2, 2 * s + 1) for s in range(places - 1)]
    direct = lax.ppermute(direct, ("sy", "sx"), down + up)
    cross = lax.ppermute(cross, ("sy", "sx"), down_cross + up_cross)
    swap_i = lax.ppermute(swap_i, "sx", SWAP)
    swap_c = lax.ppermute(swap_c, "sx", SWAP)

    planes = count // (places * sides)
    units = -(-37 // places)
    lanes = units * 128
    pieces = pltpu.VMEM((2, half, chans, cols), BF16)
    mine, theirs, grads_own, grads_send = pl.pallas_call(
        functools.partial(main_kernel, units),
        out_shape=[pieces, pieces] + [pltpu.VMEM((places, 8, lanes), F32)] * 2,
        scratch_shapes=[
            pltpu.VMEM((2, half + 8, chans, cols), BF16),
            pltpu.VMEM((2, half + 4, chans, cols), BF16),
            pltpu.VMEM((208, (half + 8) * width), BF16),
            pltpu.VMEM((208, (half + 6) * width), BF16),
            pltpu.VMEM((192, (half + 4) * width), BF16),
            pltpu.VMEM((192, (half + 2) * width), BF16),
            pltpu.VMEM((192, (half + 2) * width), BF16),
            pltpu.VMEM((192, (half + 2) * width), BF16),
            pltpu.VMEM((half + 2, chans, width), F32),
        ],
        compiler_params=PARAMS,
        name="blocks",
    )(
        *near(keep_i, keep_c, swap_i, swap_c, direct, cross),
        *near(fwd1, fwd2, bwd2, bwd1, bias1, bias2),
    )

    grads_received = lax.ppermute(grads_send, "sx", SWAP)
    back = lax.ppermute(theirs, "sx", SWAP)
    pieces = pltpu.VMEM((places, 8, lanes), BF16)
    pair = pl.pallas_call(
        pair_kernel, out_shape=pieces, compiler_params=PARAMS, name="pair"
    )(*near(grads_own, grads_received))
    parts = lax.all_to_all(pair, "sy", 0, 0, tiled=True)
    out, image_grad = pl.pallas_call(
        outputs_kernel,
        out_shape=[shape_of(image.shape, BF16)] * 2,
        compiler_params=PARAMS,
        name="outputs",
    )(*near(mine, back))
    row_total = pl.pallas_call(
        functools.partial(sum_kernel, 1.0),
        out_shape=pltpu.VMEM((planes, 8, lanes), BF16),
        compiler_params=PARAMS,
        name="add_rows",
    )(*near(parts))
    slides = lax.all_to_all(row_total, "grp", 0, 0, tiled=True)
    total = pl.pallas_call(
        functools.partial(sum_kernel, factor),
        out_shape=pieces,
        compiler_params=PARAMS,
        name="add_slides",
    )(*near(slides))
    gathered = lax.all_to_all(total, "sy", 0, 0, tiled=True)
    swapped = lax.ppermute(gathered, "sx", SWAP)
    weight_shape = shape_of((3, 3, chans, chans), F32)
    bias_shape = shape_of((1, chans), F32)
    gw1, gb1, gw2, gb2 = pl.pallas_call(
        functools.partial(grads_kernel, units),
        out_shape=[weight_shape, bias_shape, weight_shape, bias_shape],
        compiler_params=PARAMS,
        name="grads",
    )(*near(gathered, swapped))
    return out, image_grad, gw1, gb1.reshape(chans), gw2, gb2.reshape(chans)


def solution(mesh):
    return jax.shard_map(
        local,
        mesh=mesh,
        in_specs=(P("grp", None, "sy", "sx"), P(), P(), P(), P(), P("grp", None, "sy", "sx")),
        out_specs=(P("grp", None, "sy", "sx"), P("grp", None, "sy", "sx"), P(), P(), P(), P()),
        check_vma=False,
    )
```

```python
import functools

import jax
import jax.numpy as jnp
from jax import lax
from jax.experimental import pallas as pl
from jax.experimental.pallas import tpu as pltpu
from jax.sharding import PartitionSpec as P

BF16 = jnp.bfloat16
F32 = jnp.float32
PARAMS = pltpu.CompilerParams(vmem_limit_bytes=40 * 1024 * 1024)
SWAP = [(0, 1), (1, 0)]


def shape_of(shape, dtype):
    return jax.ShapeDtypeStruct(shape, dtype)


def near(*arrays):
    return [pltpu.with_memory_space_constraint(array, pltpu.VMEM) for array in arrays]


def pack_kernel(
    image_ref,
    cot_ref,
    keep_i,
    keep_c,
    swap_i,
    swap_c,
    direct,
    cross,
    image_v,
    cot_v,
    image_t,
    cot_t,
    sems,
):
    side = lax.axis_index("sx")
    rows = image_ref.shape[2]
    half = rows // 2
    jobs = []
    for c in range(image_ref.shape[1] // 16):
        for n, (src, dst, out) in enumerate(((image_ref, image_v, image_t), (cot_ref, cot_v, cot_t))):
            chans = slice(16 * c, 16 * c + 16)
            copy = pltpu.make_async_copy(src.at[0, chans], dst.at[chans], sems.at[2 * c + n])
            copy.start()
            jobs.append((copy, chans, dst, out))
    for copy, chans, dst, out in jobs:
        copy.wait()
        out[:, chans, :] = jnp.transpose(dst[chans], (1, 0, 2))
    keep_i[...] = image_t[pl.ds(side * (half - 4), half + 4)]
    keep_c[...] = cot_t[pl.ds(side * (half - 2), half + 2)]
    swap_i[...] = image_t[pl.ds((1 - side) * (half - 4), half + 4)]
    swap_c[...] = cot_t[pl.ds((1 - side) * (half - 2), half + 2)]
    direct[0:4] = image_t[pl.ds((1 - side) * (rows - 4), 4)]
    direct[4:6] = cot_t[pl.ds((1 - side) * (rows - 2), 2)]
    cross[0:4] = image_t[pl.ds(side * (rows - 4), 4)]
    cross[4:6] = cot_t[pl.ds(side * (rows - 2), 2)]


def column(row):
    chans = row.shape[1]
    r = lax.broadcasted_iota(jnp.int32, (chans, chans), 0)
    c = lax.broadcasted_iota(jnp.int32, (chans, chans), 1)
    wide = jnp.broadcast_to(row, (chans, chans))
    return jnp.sum(jnp.where(r == c, wide, 0.0), axis=1, keepdims=True)


def weights_kernel(w1, b1, w2, b2, fwd1, fwd2, bwd2, bwd1, bias1, bias2):
    for w, fwd, bwd in ((w1, fwd1, bwd1), (w2, fwd2, bwd2)):
        for a in range(3):
            fwd[a * 64 : a * 64 + 64, :] = jnp.concatenate(
                [jnp.transpose(w[a, b].astype(F32)) for b in range(3)], axis=1
            ).astype(BF16)
            bwd[a * 64 : a * 64 + 64, :] = jnp.concatenate(
                [w[2 - a, 2 - b].astype(F32) for b in range(3)], axis=1
            ).astype(BF16)
    bias1[...] = jnp.broadcast_to(column(b1[...]), bias1.shape)
    bias2[...] = jnp.broadcast_to(column(b2[...]), bias2.shape)


def spread(dst, h, row):
    chans, width = row.shape
    zero = jnp.zeros((chans, 1), row.dtype)
    at = slice(h * width, (h + 1) * width)
    dst[0:chans, at] = jnp.concatenate([zero, row[:, :-1]], axis=1)
    dst[chans : 2 * chans, at] = row
    dst[2 * chans : 3 * chans, at] = jnp.concatenate([row[:, 1:], zero], axis=1)


def sweep(weight_ref, src, count, width, emit):
    weight = weight_ref[...]
    first = second = None
    for h in range(count):
        part = jnp.dot(
            weight, src[0:192, h * width : (h + 1) * width], preferred_element_type=F32
        )
        if h >= 2:
            emit(h - 1, first + part[128:192])
        first = part[64:128] if second is None else second + part[64:128]
        second = part[0:64]


def main_kernel(
    keep_i,
    keep_c,
    swap_i,
    swap_c,
    direct,
    cross,
    fwd1,
    fwd2,
    bwd2,
    bwd1,
    bias1,
    bias2,
    mine,
    theirs,
    grads_own,
    grads_send,
    image_s,
    cot_s,
    x3,
    h3,
    d3,
    da2,
    da1,
    e3,
    slopes,
):
    side = lax.axis_index("sx")
    place = lax.axis_index("sy")
    places = lax.axis_size("sy")
    half = mine.shape[1]
    width = 2 * mine.shape[3]
    total = places * 2 * half
    start = (2 * place + side) * half
    other = 1 - side
    image_s[side, pl.ds(4 * other, half + 4)] = keep_i[...]
    image_s[other, pl.ds(4 * other, half + 4)] = swap_i[...]
    cot_s[side, pl.ds(2 * other, half + 2)] = keep_c[...]
    cot_s[other, pl.ds(2 * other, half + 2)] = swap_c[...]
    image_s[side, pl.ds((half + 4) * side, 4)] = direct[0:4]
    image_s[other, pl.ds((half + 4) * side, 4)] = cross[0:4]
    cot_s[side, pl.ds((half + 2) * side, 2)] = direct[4:6]
    cot_s[other, pl.ds((half + 2) * side, 2)] = cross[4:6]

    ones = jnp.ones((16, x3.shape[1]), BF16)
    x3[192:208, :] = ones
    h3[192:208, :] = ones[:, : h3.shape[1]]
    blank = jnp.zeros((64, 2 * width), BF16)
    for da in (da2, da1):
        da[0:64, half * width :] = blank
        da[64:128, 0:width] = blank[:, :width]
        da[64:128, (half + 1) * width :] = blank[:, :width]
        da[128:192, 0 : 2 * width] = blank

    def inside(row):
        return jnp.logical_and(start + row >= 0, start + row < total)

    def store_delta(da, j, delta):
        for a in range(3):
            da[a * 64 : a * 64 + 64, (j + a) * width : (j + a + 1) * width] = delta

    def hand_out(slot, j, value):
        left, right = value[:, : width // 2], value[:, width // 2 :]
        own = jnp.where(side == 0, left, right)
        partner = jnp.where(side == 0, right, left)
        mine[slot, j] = own.astype(BF16)
        theirs[slot, j] = partner.astype(BF16)

    for e in range(half + 8):
        spread(x3, e, jnp.concatenate([image_s[0, e], image_s[1, e]], axis=1))

    shift1 = jnp.broadcast_to(bias1[:, 0:1], (64, width))
    shift2 = jnp.broadcast_to(bias2[:, 0:1], (64, width))

    def first(e, acc):
        pre = acc + shift1
        gate = jax.nn.sigmoid(pre)
        hidden = pre * gate
        if e < 4 or e >= half + 4:
            hidden = jnp.where(inside(e - 4), hidden, 0.0)
        spread(h3, e - 1, hidden.astype(BF16))
        if 3 <= e < half + 5:
            slopes[e - 3] = gate * (1.0 + pre * (1.0 - gate))

    sweep(fwd1, x3, half + 8, width, first)

    def second(f, acc):
        g = f - 1
        pre = acc + shift2
        gate = jax.nn.sigmoid(pre)
        cot = jnp.concatenate([cot_s[0, g], cot_s[1, g]], axis=1).astype(F32)
        delta = (cot * (gate * (1.0 + pre * (1.0 - gate)))).astype(BF16)
        spread(d3, g, delta)
        if 2 <= g < half + 2:
            hand_out(0, g - 2, pre * gate)
            store_delta(da2, g - 2, delta)

    sweep(fwd2, h3, half + 6, width, second)

    def third(g, acc):
        k = g - 1
        delta = acc * slopes[k]
        if k == 0 or k == half + 1:
            delta = jnp.where(inside(k - 1), delta, 0.0)
        delta = delta.astype(BF16)
        spread(e3, k, delta)
        if 1 <= k < half + 1:
            store_delta(da1, k - 1, delta)

    sweep(bwd2, d3, half + 4, width, third)

    def fourth(k, acc):
        hand_out(1, k - 1, acc)

    sweep(bwd1, e3, half + 2, width, fourth)

    contract = (((1,), (1,)), ((), ()))
    long = (half + 2) * width
    grad2 = lax.dot_general(
        h3[:, 2 * width : 2 * width + long], da2[...], contract, preferred_element_type=F32
    )
    grad1 = lax.dot_general(
        x3[:, 3 * width : 3 * width + long], da1[...], contract, preferred_element_type=F32
    )
    both = jnp.concatenate([grad2[0:192], grad1[0:192]], axis=1)
    biases = jnp.concatenate([grad2[192:200, 64:128], grad1[192:200, 64:128]], axis=1)
    tiles = [
        both[8 * (t // 3) : 8 * (t // 3) + 8, 128 * (t % 3) : 128 * (t % 3) + 128]
        for t in range(72)
    ]
    empty = jnp.zeros((8, 128), F32)
    low, high = tiles[:36] + [biases], tiles[36:]
    for ref, flip in ((grads_own, False), (grads_send, True)):
        for t in range(37):
            here = low[t] if t < len(low) else empty
            there = high[t] if t < len(high) else empty
            first_half = (side == 1) if flip else (side == 0)
            ref[:, 128 * t : 128 * t + 128] = jnp.where(first_half, here, there)


def pair_kernel(own, received, out):
    out[...] = (own[...] + received[...]).astype(BF16)


def add_kernel(factor, held, received, out):
    total = held[...].astype(F32) + received[...].astype(F32)
    out[...] = (total * factor).astype(out.dtype)


def outputs_kernel(mine, back, out, image_grad):
    side = lax.axis_index("sx")
    half = mine.shape[1]
    here = pl.ds(pl.multiple_of(side * half, half), half)
    there = pl.ds(pl.multiple_of((1 - side) * half, half), half)
    for slot, ref in ((0, out), (1, image_grad)):
        ref[0, :, here, :] = jnp.transpose(mine[slot], (1, 0, 2))
        ref[0, :, there, :] = jnp.transpose(back[slot], (1, 0, 2))


def grads_kernel(held, swapped, gw1, gb1, gw2, gb2):
    side = lax.axis_index("sx")

    def tile(part, t):
        at = slice(128 * t, 128 * t + 128)
        return jnp.where(side == part, held[:, at], swapped[:, at])

    for block in range(24):
        part, first = block // 12, 3 * (block % 12)
        line = jnp.concatenate([tile(part, first + p) for p in range(3)], axis=1)
        b, i = block // 8, (block % 8) * 8
        for a in range(3):
            gw2[a, b, i : i + 8, :] = line[:, a * 64 : a * 64 + 64]
            gw1[a, b, i : i + 8, :] = line[:, 192 + a * 64 : 256 + a * 64]
    biases = tile(0, 36)
    gb2[...] = biases[0:1, 0:64]
    gb1[...] = biases[0:1, 64:128]


def exchange_pairs(places, planes):
    def bits(count, stride):
        return [(stride, 1 << k) for k in range(count.bit_length() - 1)]

    rows, slides = bits(places, 0), bits(planes, 1)
    stages = []
    for plan in zip(rows + slides, slides + rows):
        pairs = []
        for s in range(places):
            for x, (axis, bit) in enumerate(plan):
                for g in range(planes):
                    t, h = (s ^ bit, g) if axis == 0 else (s, g ^ bit)
                    pairs.append(((2 * s + x) * planes + g, (2 * t + x) * planes + h))
        stages.append(pairs)
    return stages


def local(image, weight_one, bias_one, weight_two, bias_two, cotangent):
    _, chans, rows, cols = image.shape
    places, sides = lax.axis_size("sy"), lax.axis_size("sx")
    count = places * sides * lax.axis_size("grp")
    half = rows // 2
    width = 2 * cols
    factor = float(rows * cols * count) ** (-0.5)

    keep_i, keep_c, swap_i, swap_c, direct, cross = pl.pallas_call(
        pack_kernel,
        out_shape=[
            pltpu.VMEM((half + 4, chans, cols), BF16),
            pltpu.VMEM((half + 2, chans, cols), BF16),
            pltpu.VMEM((half + 4, chans, cols), BF16),
            pltpu.VMEM((half + 2, chans, cols), BF16),
            pltpu.VMEM((6, chans, cols), BF16),
            pltpu.VMEM((6, chans, cols), BF16),
        ],
        in_specs=[pl.BlockSpec(memory_space=pltpu.HBM)] * 2,
        scratch_shapes=[
            pltpu.VMEM((chans, rows, cols), BF16),
            pltpu.VMEM((chans, rows, cols), BF16),
            pltpu.VMEM((rows, chans, cols), BF16),
            pltpu.VMEM((rows, chans, cols), BF16),
            pltpu.SemaphoreType.DMA((chans // 8,)),
        ],
        compiler_params=PARAMS,
        name="pack",
    )(*[pltpu.with_memory_space_constraint(array, pltpu.HBM) for array in (image, cotangent)])
    fwd1, fwd2, bwd2, bwd1, bias1, bias2 = pl.pallas_call(
        weights_kernel,
        out_shape=[pltpu.VMEM((192, 192), BF16)] * 4 + [pltpu.VMEM((64, 128), F32)] * 2,
        compiler_params=PARAMS,
        name="weights",
    )(weight_one, bias_one.reshape(1, chans), weight_two, bias_two.reshape(1, chans))

    down = [(2 * s, 2 * s + 2) for s in range(places - 1)]
    up = [(2 * s + 3, 2 * s + 1) for s in range(places - 1)]
    down_cross = [(2 * s + 1, 2 * s + 2) for s in range(places - 1)]
    up_cross = [(2 * s + 2, 2 * s + 1) for s in range(places - 1)]
    direct = lax.ppermute(direct, ("sy", "sx"), down + up)
    cross = lax.ppermute(cross, ("sy", "sx"), down_cross + up_cross)
    swap_i = lax.ppermute(swap_i, "sx", SWAP)
    swap_c = lax.ppermute(swap_c, "sx", SWAP)

    pieces = pltpu.VMEM((2, half, chans, cols), BF16)
    mine, theirs, grads_own, grads_send = pl.pallas_call(
        main_kernel,
        out_shape=[pieces, pieces] + [pltpu.VMEM((8, 37 * 128), F32)] * 2,
        scratch_shapes=[
            pltpu.VMEM((2, half + 8, chans, cols), BF16),
            pltpu.VMEM((2, half + 4, chans, cols), BF16),
            pltpu.VMEM((208, (half + 8) * width), BF16),
            pltpu.VMEM((208, (half + 6) * width), BF16),
            pltpu.VMEM((192, (half + 4) * width), BF16),
            pltpu.VMEM((192, (half + 2) * width), BF16),
            pltpu.VMEM((192, (half + 2) * width), BF16),
            pltpu.VMEM((192, (half + 2) * width), BF16),
            pltpu.VMEM((half + 2, chans, width), F32),
        ],
        compiler_params=PARAMS,
        name="blocks",
    )(
        *near(keep_i, keep_c, swap_i, swap_c, direct, cross),
        *near(fwd1, fwd2, bwd2, bwd1, bias1, bias2),
    )

    grads_received = lax.ppermute(grads_send, "sx", SWAP)
    back = lax.ppermute(theirs, "sx", SWAP)
    held = pl.pallas_call(
        pair_kernel,
        out_shape=pltpu.VMEM((8, 37 * 128), BF16),
        compiler_params=PARAMS,
        name="pair",
    )(*near(grads_own, grads_received))
    stages = exchange_pairs(places, lax.axis_size("grp"))
    for n, pairs in enumerate(stages):
        last = n == len(stages) - 1
        received = lax.ppermute(held, ("sy", "sx", "grp"), pairs)
        held = pl.pallas_call(
            functools.partial(add_kernel, factor if last else 1.0),
            out_shape=pltpu.VMEM((8, 37 * 128), F32 if last else BF16),
            compiler_params=PARAMS,
            name="add",
        )(*near(held, received))
    swapped = lax.ppermute(held, "sx", SWAP)
    out, image_grad = pl.pallas_call(
        outputs_kernel,
        out_shape=[shape_of(image.shape, BF16)] * 2,
        compiler_params=PARAMS,
        name="outputs",
    )(*near(mine, back))
    weight_shape = shape_of((3, 3, chans, chans), F32)
    bias_shape = shape_of((1, chans), F32)
    gw1, gb1, gw2, gb2 = pl.pallas_call(
        grads_kernel,
        out_shape=[weight_shape, bias_shape, weight_shape, bias_shape],
        compiler_params=PARAMS,
        name="grads",
    )(*near(held, swapped))
    return out, image_grad, gw1, gb1.reshape(chans), gw2, gb2.reshape(chans)


def solution(mesh):
    return jax.shard_map(
        local,
        mesh=mesh,
        in_specs=(P("grp", None, "sy", "sx"), P(), P(), P(), P(), P("grp", None, "sy", "sx")),
        out_specs=(P("grp", None, "sy", "sx"), P("grp", None, "sy", "sx"), P(), P(), P(), P()),
        check_vma=False,
    )
```

```python
import functools

import jax
import jax.numpy as jnp
from jax import lax
from jax.experimental import pallas as pl
from jax.experimental.pallas import tpu as pltpu
from jax.sharding import PartitionSpec as P

BF16 = jnp.bfloat16
F32 = jnp.float32
PARAMS = pltpu.CompilerParams(vmem_limit_bytes=32 * 1024 * 1024)
SWAP = [(0, 1), (1, 0)]
CONTRACT = (((1,), (1,)), ((), ()))
TILES = 37


def shape_of(shape, dtype):
    return jax.ShapeDtypeStruct(shape, dtype)


def near(*arrays):
    return [pltpu.with_memory_space_constraint(array, pltpu.VMEM) for array in arrays]


def far(*arrays):
    return [pltpu.with_memory_space_constraint(array, pltpu.HBM) for array in arrays]


def turned(side, index, count):
    return index + side * (count - 1 - 2 * index)


def pack_kernel(
    image_ref,
    cot_ref,
    w1,
    b1,
    w2,
    b2,
    image_p,
    cot_p,
    swap,
    edges,
    w1_v,
    b1_v,
    w2_v,
    b2_v,
    image_v,
    cot_v,
    sems,
):
    side = lax.axis_index("sx")
    rows = image_ref.shape[2]
    half = rows // 2
    jobs, small = [], []
    sources = ((image_ref, image_v, image_p), (cot_ref, cot_v, cot_p))
    for c in range(image_ref.shape[1] // 16):
        chans = slice(16 * c, 16 * c + 16)
        for n, (src, dst, out) in enumerate(sources):
            copy = pltpu.make_async_copy(src.at[0, chans], dst.at[chans], sems.at[2 * c + n])
            copy.start()
            jobs.append((copy, chans, dst, out))
    for n, (src, dst) in enumerate(((w1, w1_v), (b1, b1_v), (w2, w2_v), (b2, b2_v))):
        copy = pltpu.make_async_copy(src, dst, sems.at[len(jobs) + n])
        copy.start()
        small.append(copy)
    for copy, chans, dst, out in jobs:
        copy.wait()
        block = jnp.transpose(dst[chans], (1, 0, 2))
        for h in range(rows):
            out[turned(side, h, rows), chans, :] = block[h]
    swap[0 : half + 4] = image_p[half - 4 : rows]
    for k in range(half + 2):
        swap[half + 4 + k] = cot_p[rows - 1 - k]
    for k in range(4):
        edges[k] = image_p[3 - k]
    edges[4:6] = cot_p[0:2]
    for copy in small:
        copy.wait()


def column(row):
    chans = row.shape[1]
    r = lax.broadcasted_iota(jnp.int32, (chans, chans), 0)
    c = lax.broadcasted_iota(jnp.int32, (chans, chans), 1)
    wide = jnp.broadcast_to(row, (chans, chans))
    return jnp.sum(jnp.where(r == c, wide, 0.0), axis=1, keepdims=True)


def weights_kernel(w1, b1, w2, b2, fwd1, fwd2, bwd2, bwd1, bias1, bias2):
    side = lax.axis_index("sx")
    for w, fwd, bwd in ((w1, fwd1, bwd1), (w2, fwd2, bwd2)):
        for a in range(3):
            tap = turned(side, a, 3)
            fwd[a * 64 : a * 64 + 64, :] = jnp.concatenate(
                [jnp.transpose(w[tap, b].astype(F32)) for b in range(3)], axis=1
            ).astype(BF16)
            bwd[a * 64 : a * 64 + 64, :] = jnp.concatenate(
                [w[2 - tap, 2 - b].astype(F32) for b in range(3)], axis=1
            ).astype(BF16)
    bias1[...] = jnp.broadcast_to(column(b1[...]), bias1.shape)
    bias2[...] = jnp.broadcast_to(column(b2[...]), bias2.shape)


def spread(dst, at, row):
    chans, width = row.shape
    zero = jnp.zeros((chans, 1), row.dtype)
    cols = slice(at * width, (at + 1) * width)
    dst[0:chans, cols] = jnp.concatenate([zero, row[:, :-1]], axis=1)
    dst[chans : 2 * chans, cols] = row
    dst[2 * chans : 3 * chans, cols] = jnp.concatenate([row[:, 1:], zero], axis=1)


def sweep(weight_ref, rows, first, emit):
    weight = weight_ref[...]
    upper = lower = None
    for n, (ref, at) in enumerate(rows):
        part = jnp.dot(weight, ref.spread_row(at), preferred_element_type=F32)
        if n >= 2:
            emit(first + n - 1, upper + part[128:192])
        upper = part[64:128] if lower is None else lower + part[64:128]
        lower = part[0:64]


class Rows:
    def __init__(self, ref, width):
        self.ref, self.width = ref, width

    def spread_row(self, at):
        return self.ref[0:192, at * self.width : (at + 1) * self.width]

    def span(self, start, stop):
        return self.ref[:, start * self.width : stop * self.width]


def silu_and_slope(pre):
    gate = jax.nn.sigmoid(pre)
    return pre * gate, gate * (1.0 + pre * (1.0 - gate))


def clear(side, taps, width, start, stop, j0, j1):
    for a in range(3):
        place = pl.ds(pl.multiple_of(64 * turned(side, a, 3), 64), 64)
        for q in range(start, stop):
            if not j0 <= q - a < j1:
                at = q - start
                taps[place, at * width : (at + 1) * width] = jnp.zeros((64, width), BF16)


def store_taps(side, taps, width, start, j, delta):
    for a in range(3):
        place = pl.ds(pl.multiple_of(64 * turned(side, a, 3), 64), 64)
        at = j + a - start
        taps[place, at * width : (at + 1) * width] = delta


def hand_out(side, mine, theirs, at, value):
    width = value.shape[1]
    left, right = value[:, : width // 2], value[:, width // 2 :]
    mine[at] = jnp.where(side == 0, left, right).astype(BF16)
    theirs[at] = jnp.where(side == 0, right, left).astype(BF16)


def inner_kernel(
    image_p,
    cot_p,
    swapped,
    fwd1,
    fwd2,
    bwd2,
    bwd1,
    bias1,
    bias2,
    x3,
    h3,
    d3,
    e3,
    slopes,
    mine,
    theirs,
    grad2,
    grad1,
    image_s,
    cot_s,
    taps2,
    taps1,
):
    side = lax.axis_index("sx")
    half = image_p.shape[0] // 2
    width = 2 * image_p.shape[2]
    last = half + 8
    other = 1 - side
    image_s[side] = image_p[0 : half + 4]
    cot_s[side] = cot_p[0 : half + 2]
    for p in range(half + 4):
        image_s[other, p] = swapped[half + 3 - p]
    cot_s[other] = swapped[half + 4 : 2 * half + 6]
    ones = jnp.ones((16, x3.shape[1]), BF16)
    x3[192:208, :] = ones
    h3[192:208, :] = ones[:, : h3.shape[1]]
    clear(side, taps2, width, 2, half + 2, 2, half)
    clear(side, taps1, width, 3, half + 2, 3, half)
    for p in range(half + 4):
        spread(x3, p, jnp.concatenate([image_s[0, p], image_s[1, p]], axis=1))
    shift1 = jnp.broadcast_to(bias1[:, 0:1], (64, width))
    shift2 = jnp.broadcast_to(bias2[:, 0:1], (64, width))

    def first(e, acc):
        hidden, slope = silu_and_slope(acc + shift1)
        spread(h3, e - 5, hidden.astype(BF16))
        if e < half + 5:
            slopes[e - 5] = slope

    x_rows, h_rows = Rows(x3, width), Rows(h3, width)
    sweep(fwd1, [(x_rows, e - 4) for e in range(4, last)], 4, first)

    def second(e, acc):
        value, slope = silu_and_slope(acc + shift2)
        cot = jnp.concatenate([cot_s[0, e - 4], cot_s[1, e - 4]], axis=1).astype(F32)
        delta = (cot * slope).astype(BF16)
        spread(d3, e - 6, delta)
        if e < half + 4:
            hand_out(side, mine, theirs, e - 6, value)
            store_taps(side, taps2, width, 2, e - 4, delta)

    sweep(fwd2, [(h_rows, e - 5) for e in range(5, last - 1)], 5, second)

    def third(e, acc):
        delta = (acc * slopes[e - 5]).astype(BF16)
        spread(e3, e - 7, delta)
        if e < half + 4:
            store_taps(side, taps1, width, 3, e - 4, delta)

    sweep(bwd2, [(Rows(d3, width), e - 6) for e in range(6, last - 2)], 6, third)

    def fourth(e, acc):
        hand_out(side, mine, theirs, half - 2 + e - 8, acc)

    sweep(bwd1, [(Rows(e3, width), e - 7) for e in range(7, last - 3)], 7, fourth)

    grad2[...] = lax.dot_general(
        h_rows.span(0, half), taps2[...], CONTRACT, preferred_element_type=F32
    )
    grad1[...] = lax.dot_general(
        x_rows.span(2, half + 1), taps1[...], CONTRACT, preferred_element_type=F32
    )


def outer_kernel(
    edges_own,
    edges_other,
    cot_p,
    swapped,
    fwd1,
    fwd2,
    bwd2,
    bwd1,
    bias1,
    bias2,
    x3,
    h3,
    d3,
    e3,
    slopes,
    grad2,
    grad1,
    mine,
    theirs,
    grads_own,
    grads_send,
    image_s,
    cot_s,
    x3_b,
    h3_b,
    d3_b,
    e3_b,
    slopes_b,
    taps2,
    taps1,
):
    side = lax.axis_index("sx")
    place = lax.axis_index("sy")
    half = cot_p.shape[0] // 2
    width = 2 * cot_p.shape[2]
    other = 1 - side
    outside = place == side * (lax.axis_size("sy") - 1)

    def keep(value):
        return jnp.where(outside, 0.0, value.astype(F32)).astype(BF16)

    image_s[side] = keep(edges_own[0:4])
    image_s[other] = keep(edges_other[0:4])
    for half_of, ref in ((side, edges_own), (other, edges_other)):
        cot_s[half_of, 0] = keep(ref[5])
        cot_s[half_of, 1] = keep(ref[4])
    cot_s[side, 2:4] = cot_p[0:2]
    cot_s[other, 2:4] = swapped[half + 4 : half + 6]
    ones = jnp.ones((16, x3_b.shape[1]), BF16)
    x3_b[192:208, :] = ones
    h3_b[192:208, :] = ones
    clear(side, taps2, width, 0, 4, 0, 2)
    clear(side, taps1, width, 0, 5, 0, 3)
    for e in range(4):
        spread(x3_b, e, jnp.concatenate([image_s[0, e], image_s[1, e]], axis=1))
    shift1 = jnp.broadcast_to(bias1[:, 0:1], (64, width))
    shift2 = jnp.broadcast_to(bias2[:, 0:1], (64, width))

    def joined(outer, start, inner, split, first):
        outer, inner = Rows(outer, width), Rows(inner, width)
        return [
            (outer, e - start) if e < split else (inner, e - split)
            for e in range(first, first + 6)
        ]

    def first(e, acc):
        hidden, slope = silu_and_slope(acc + shift1)
        if e < 4:
            hidden = jnp.where(outside, 0.0, hidden)
        spread(h3_b, e - 1, hidden.astype(BF16))
        if e >= 3:
            slopes_b[e - 3] = slope

    sweep(fwd1, joined(x3_b, 0, x3, 4, 0), 0, first)

    def second(e, acc):
        value, slope = silu_and_slope(acc + shift2)
        cot = jnp.concatenate([cot_s[0, e - 2], cot_s[1, e - 2]], axis=1).astype(F32)
        delta = (cot * slope).astype(BF16)
        spread(d3_b, e - 2, delta)
        if e >= 4:
            hand_out(side, mine, theirs, e - 4, value)
            store_taps(side, taps2, width, 0, e - 4, delta)

    sweep(fwd2, joined(h3_b, 1, h3, 5, 1), 1, second)

    def third(e, acc):
        delta = acc * (slopes_b[e - 3] if e < 5 else slopes[e - 5])
        if e < 4:
            delta = jnp.where(outside, 0.0, delta)
        delta = delta.astype(BF16)
        spread(e3_b, e - 3, delta)
        if e >= 4:
            store_taps(side, taps1, width, 0, e - 4, delta)

    sweep(bwd2, joined(d3_b, 2, d3, 6, 2), 2, third)

    def fourth(e, acc):
        hand_out(side, mine, theirs, 2 + e - 4, acc)

    sweep(bwd1, joined(e3_b, 3, e3, 7, 3), 3, fourth)

    def product(left, right):
        return lax.dot_general(left, right, CONTRACT, preferred_element_type=F32)

    total2 = (
        grad2[...]
        + product(Rows(h3_b, width).span(2, 4), taps2[:, : 2 * width])
        + product(Rows(h3, width).span(0, 2), taps2[:, 2 * width :])
    )
    total1 = (
        grad1[...]
        + product(Rows(x3_b, width).span(3, 4), taps1[:, :width])
        + product(Rows(x3, width).span(0, 4), taps1[:, width:])
    )
    both = jnp.concatenate([total2[0:192], total1[0:192]], axis=1)
    biases = jnp.concatenate([total2[192:200, 64:128], total1[192:200, 64:128]], axis=1)
    tiles = [
        both[8 * (t // 3) : 8 * (t // 3) + 8, 128 * (t % 3) : 128 * (t % 3) + 128]
        for t in range(72)
    ]
    empty = jnp.zeros((8, 128), F32)
    low, high = tiles[:36] + [biases], tiles[36:] + [empty]
    for t in range(TILES):
        at = slice(128 * t, 128 * t + 128)
        grads_own[:, at] = jnp.where(side == 0, low[t], high[t])
        grads_send[:, at] = jnp.where(side == 0, high[t], low[t])


def pair_kernel(own, received, out):
    out[...] = (own[...] + received[...]).astype(BF16)


def add_kernel(factor, *refs):
    out = refs[-1]
    terms = [ref[...].astype(F32) for ref in refs[:-1]]
    while len(terms) > 1:
        terms = [sum(terms[n + 1 : n + 2], terms[n]) for n in range(0, len(terms), 2)]
    out[...] = (terms[0] * factor).astype(out.dtype)


def outputs_kernel(mine_a, mine_b, back_a, back_b, out, image_grad, token, natural):
    side = lax.axis_index("sx")
    rows = out.shape[2]
    half = rows // 2
    for slot in range(2):
        near_rows = 2 + 2 * slot
        for j in range(half):
            if j < near_rows:
                own, other = mine_b[2 * slot + j], back_b[2 * slot + j]
            else:
                at = slot * (half - 2) + j - near_rows
                own, other = mine_a[at], back_a[at]
            natural[slot, turned(side, j, rows)] = own
            natural[slot, turned(side, rows - 1 - j, rows)] = other
    for slot, ref in ((0, out), (1, image_grad)):
        ref[0] = jnp.transpose(natural[slot], (1, 0, 2))
    token[...] = jnp.zeros(token.shape, F32)


def grads_kernel(held, swapped, gw1, gb1, gw2, gb2):
    side = lax.axis_index("sx")

    def tile(part, t):
        at = slice(128 * t, 128 * t + 128)
        return jnp.where(side == part, held[:, at], swapped[:, at])

    for block in range(24):
        part, first = block // 12, 3 * (block % 12)
        line = jnp.concatenate([tile(part, first + p) for p in range(3)], axis=1)
        b, i = block // 8, (block % 8) * 8
        for a in range(3):
            gw2[a, b, i : i + 8, :] = line[:, a * 64 : a * 64 + 64]
            gw1[a, b, i : i + 8, :] = line[:, 192 + a * 64 : 256 + a * 64]
    biases = tile(0, 36)
    gb2[...] = biases[0:1, 0:64]
    gb1[...] = biases[0:1, 64:128]


def exchange_stages(places, planes):
    def groups(count, axis):
        bits = [1 << k for k in range(count.bit_length() - 1)]
        pairs = [bits[k : k + 2] for k in range(0, len(bits), 2)]
        return [(axis, [b[0]] + ([b[1], b[0] | b[1]] if len(b) == 2 else [])) for b in pairs]

    rows, slides = groups(places, 0), groups(planes, 1)
    stages = []
    for plan in zip(rows + slides, slides + rows):
        stage = []
        for k in range(3):
            pairs = []
            for s in range(places):
                for x, (axis, masks) in enumerate(plan):
                    for g in range(planes):
                        if k < len(masks):
                            t, h = (s ^ masks[k], g) if axis == 0 else (s, g ^ masks[k])
                            pairs.append(((2 * s + x) * planes + g, (2 * t + x) * planes + h))
            if pairs:
                stage.append(pairs)
        stages.append(stage)
    return stages


def local(image, weight_one, bias_one, weight_two, bias_two, cotangent):
    _, chans, rows, cols = image.shape
    places, planes = lax.axis_size("sy"), lax.axis_size("grp")
    half = rows // 2
    width = 2 * cols
    factor = float(rows * cols * places * planes * lax.axis_size("sx")) ** (-0.5)
    call = functools.partial(pl.pallas_call, compiler_params=PARAMS)

    def rows_of(count):
        return pltpu.VMEM((count, chans, cols), BF16)

    def flat(height, count):
        return pltpu.VMEM((height, count * width), BF16)

    image_p, cot_p, swap, edges, w1, b1, w2, b2 = call(
        pack_kernel,
        out_shape=[
            rows_of(rows),
            rows_of(rows),
            rows_of(2 * half + 6),
            rows_of(6),
            pltpu.VMEM(weight_one.shape, BF16),
            pltpu.VMEM((1, chans), F32),
            pltpu.VMEM(weight_two.shape, BF16),
            pltpu.VMEM((1, chans), F32),
        ],
        in_specs=[pl.BlockSpec(memory_space=pltpu.HBM)] * 6,
        scratch_shapes=[
            pltpu.VMEM((chans, rows, cols), BF16),
            pltpu.VMEM((chans, rows, cols), BF16),
            pltpu.SemaphoreType.DMA((chans // 8 + 4,)),
        ],
        name="pack",
    )(
        *far(image, cotangent, weight_one, bias_one.reshape(1, chans)),
        *far(weight_two, bias_two.reshape(1, chans)),
    )
    swapped = lax.ppermute(swap, "sx", SWAP)
    across = []
    for s in range(places):
        upper, lower = 2 * s + 1, 2 * ((s + 1) % places)
        across += [(upper, lower), (lower, upper)]
    edges_other = lax.ppermute(edges, ("sy", "sx"), across)
    edges_own = lax.ppermute(swapped[half : half + 6], ("sy", "sx"), across)
    weights = call(
        weights_kernel,
        out_shape=[pltpu.VMEM((192, 192), BF16)] * 4 + [pltpu.VMEM((64, 128), F32)] * 2,
        name="weights",
    )(*near(w1, b1, w2, b2))

    x3, h3, d3, e3, slopes, mine_a, theirs_a, grad2, grad1 = call(
        inner_kernel,
        out_shape=[
            flat(208, half + 4),
            flat(208, half + 2),
            flat(192, half),
            flat(192, half - 2),
            pltpu.VMEM((half, chans, width), F32),
            rows_of(2 * half - 6),
            rows_of(2 * half - 6),
            pltpu.VMEM((208, 192), F32),
            pltpu.VMEM((208, 192), F32),
        ],
        scratch_shapes=[
            pltpu.VMEM((2, half + 4, chans, cols), BF16),
            pltpu.VMEM((2, half + 2, chans, cols), BF16),
            flat(192, half),
            flat(192, half - 1),
        ],
        name="inner",
    )(*near(image_p, cot_p, swapped, *weights))
    back_a = lax.ppermute(theirs_a, "sx", SWAP)
    half_grads = pltpu.VMEM((8, TILES * 128), F32)
    mine_b, theirs_b, grads_own, grads_send = call(
        outer_kernel,
        out_shape=[rows_of(6), rows_of(6), half_grads, half_grads],
        scratch_shapes=[
            pltpu.VMEM((2, 4, chans, cols), BF16),
            pltpu.VMEM((2, 4, chans, cols), BF16),
            flat(208, 4),
            flat(208, 4),
            flat(192, 4),
            flat(192, 4),
            pltpu.VMEM((2, chans, width), F32),
            flat(192, 4),
            flat(192, 5),
        ],
        name="outer",
    )(
        *near(edges_own, edges_other, cot_p, swapped, *weights),
        *near(x3, h3, d3, e3, slopes, grad2, grad1),
    )
    grads_received = lax.ppermute(grads_send, "sx", SWAP)
    back_b = lax.ppermute(theirs_b, "sx", SWAP)
    held = call(pair_kernel, out_shape=pltpu.VMEM((8, TILES * 128), BF16), name="pair")(
        *near(grads_own, grads_received)
    )
    out, image_grad, token = call(
        outputs_kernel,
        out_shape=[shape_of(image.shape, BF16)] * 2 + [pltpu.VMEM((8, 128), F32)],
        scratch_shapes=[pltpu.VMEM((2, rows, chans, cols), BF16)],
        name="outputs",
    )(*near(mine_a, mine_b, back_a, back_b))
    stages = exchange_stages(places, planes)
    for n, stage in enumerate(stages):
        final = n == len(stages) - 1
        received = [lax.ppermute(held, ("sy", "sx", "grp"), pairs) for pairs in stage]
        behind = [token] if n == 0 else []
        held = call(
            functools.partial(behind_add if behind else add_kernel, factor if final else 1.0),
            out_shape=pltpu.VMEM((8, TILES * 128), F32 if final else BF16),
            name="add",
        )(*near(*behind, held, *received))
    swapped_sums = lax.ppermute(held, "sx", SWAP)
    weight_shape = shape_of((3, 3, chans, chans), F32)
    bias_shape = shape_of((1, chans), F32)
    gw1, gb1, gw2, gb2 = call(
        grads_kernel,
        out_shape=[weight_shape, bias_shape, weight_shape, bias_shape],
        name="grads",
    )(*near(held, swapped_sums))
    return out, image_grad, gw1, gb1.reshape(chans), gw2, gb2.reshape(chans)


def behind_add(factor, token, *refs):
    add_kernel(factor, *refs)


def solution(mesh):
    return jax.shard_map(
        local,
        mesh=mesh,
        in_specs=(P("grp", None, "sy", "sx"), P(), P(), P(), P(), P("grp", None, "sy", "sx")),
        out_specs=(P("grp", None, "sy", "sx"), P("grp", None, "sy", "sx"), P(), P(), P(), P()),
        check_vma=False,
    )
```

```python
import functools

import jax
import jax.numpy as jnp
from jax import lax
from jax.experimental import pallas as pl
from jax.experimental.pallas import tpu as pltpu
from jax.sharding import PartitionSpec as P

BF16 = jnp.bfloat16
F32 = jnp.float32
PARAMS = pltpu.CompilerParams(vmem_limit_bytes=32 * 1024 * 1024)
SWAP = [(0, 1), (1, 0)]
CONTRACT = (((1,), (1,)), ((), ()))
TILES = 37


def shape_of(shape, dtype):
    return jax.ShapeDtypeStruct(shape, dtype)


def near(*arrays):
    return [pltpu.with_memory_space_constraint(array, pltpu.VMEM) for array in arrays]


def far(*arrays):
    return [pltpu.with_memory_space_constraint(array, pltpu.HBM) for array in arrays]


def lasting(micros):
    return pl.CostEstimate(flops=int(micros * 1.1e9), transcendentals=0, bytes_accessed=0)


def turned(side, index, count):
    return index + side * (count - 1 - 2 * index)


def pack_kernel(
    image_ref,
    cot_ref,
    w1,
    b1,
    w2,
    b2,
    image_p,
    cot_p,
    swap,
    edges,
    w1_v,
    b1_v,
    w2_v,
    b2_v,
    image_v,
    cot_v,
    sems,
):
    side = lax.axis_index("sx")
    rows = image_ref.shape[2]
    half = rows // 2
    jobs, small = [], []
    sources = ((image_ref, image_v, image_p), (cot_ref, cot_v, cot_p))
    for c in range(image_ref.shape[1] // 16):
        chans = slice(16 * c, 16 * c + 16)
        for n, (src, dst, out) in enumerate(sources):
            copy = pltpu.make_async_copy(src.at[0, chans], dst.at[chans], sems.at[2 * c + n])
            copy.start()
            jobs.append((copy, chans, dst, out))
    for n, (src, dst) in enumerate(((w1, w1_v), (b1, b1_v), (w2, w2_v), (b2, b2_v))):
        copy = pltpu.make_async_copy(src, dst, sems.at[len(jobs) + n])
        copy.start()
        small.append(copy)
    for copy, chans, dst, out in jobs:
        copy.wait()
        block = jnp.transpose(dst[chans], (1, 0, 2))
        for h in range(rows):
            out[turned(side, h, rows), chans, :] = block[h]
    swap[0 : half + 4] = image_p[half - 4 : rows]
    for k in range(half + 2):
        swap[half + 4 + k] = cot_p[rows - 1 - k]
    for k in range(4):
        edges[k] = image_p[3 - k]
    edges[4:6] = cot_p[0:2]
    for copy in small:
        copy.wait()


def column(row):
    chans = row.shape[1]
    r = lax.broadcasted_iota(jnp.int32, (chans, chans), 0)
    c = lax.broadcasted_iota(jnp.int32, (chans, chans), 1)
    wide = jnp.broadcast_to(row, (chans, chans))
    return jnp.sum(jnp.where(r == c, wide, 0.0), axis=1, keepdims=True)


def weights_kernel(w1, b1, w2, b2, fwd1, fwd2, bwd2, bwd1, bias1, bias2):
    side = lax.axis_index("sx")
    for w, fwd, bwd in ((w1, fwd1, bwd1), (w2, fwd2, bwd2)):
        for a in range(3):
            tap = turned(side, a, 3)
            fwd[a * 64 : a * 64 + 64, :] = jnp.concatenate(
                [jnp.transpose(w[tap, b].astype(F32)) for b in range(3)], axis=1
            ).astype(BF16)
            bwd[a * 64 : a * 64 + 64, :] = jnp.concatenate(
                [w[2 - tap, 2 - b].astype(F32) for b in range(3)], axis=1
            ).astype(BF16)
    bias1[...] = jnp.broadcast_to(column(b1[...]), bias1.shape)
    bias2[...] = jnp.broadcast_to(column(b2[...]), bias2.shape)


def spread(dst, at, row):
    chans, width = row.shape
    zero = jnp.zeros((chans, 1), row.dtype)
    cols = slice(at * width, (at + 1) * width)
    dst[0:chans, cols] = jnp.concatenate([zero, row[:, :-1]], axis=1)
    dst[chans : 2 * chans, cols] = row
    dst[2 * chans : 3 * chans, cols] = jnp.concatenate([row[:, 1:], zero], axis=1)


def sweep(weight_ref, rows, first, emit):
    weight = weight_ref[...]
    upper = lower = None
    for n, (ref, at) in enumerate(rows):
        part = jnp.dot(weight, ref.spread_row(at), preferred_element_type=F32)
        if n >= 2:
            emit(first + n - 1, upper + part[128:192])
        upper = part[64:128] if lower is None else lower + part[64:128]
        lower = part[0:64]


class Rows:
    def __init__(self, ref, width):
        self.ref, self.width = ref, width

    def spread_row(self, at):
        return self.ref[0:192, at * self.width : (at + 1) * self.width]

    def span(self, start, stop):
        return self.ref[:, start * self.width : stop * self.width]


def silu_and_slope(pre):
    gate = jax.nn.sigmoid(pre)
    return pre * gate, gate * (1.0 + pre * (1.0 - gate))


def clear(side, taps, width, start, stop, j0, j1):
    for a in range(3):
        place = pl.ds(pl.multiple_of(64 * turned(side, a, 3), 64), 64)
        for q in range(start, stop):
            if not j0 <= q - a < j1:
                at = q - start
                taps[place, at * width : (at + 1) * width] = jnp.zeros((64, width), BF16)


def store_taps(side, taps, width, start, j, delta):
    for a in range(3):
        place = pl.ds(pl.multiple_of(64 * turned(side, a, 3), 64), 64)
        at = j + a - start
        taps[place, at * width : (at + 1) * width] = delta


def hand_out(side, mine, theirs, at, value):
    width = value.shape[1]
    left, right = value[:, : width // 2], value[:, width // 2 :]
    mine[at] = jnp.where(side == 0, left, right).astype(BF16)
    theirs[at] = jnp.where(side == 0, right, left).astype(BF16)


def inner_kernel(
    image_p,
    cot_p,
    swapped,
    fwd1,
    fwd2,
    bwd2,
    bwd1,
    bias1,
    bias2,
    x3,
    h3,
    d3,
    e3,
    slopes,
    mine,
    theirs,
    grad2,
    grad1,
    image_s,
    cot_s,
    taps2,
    taps1,
):
    side = lax.axis_index("sx")
    half = image_p.shape[0] // 2
    width = 2 * image_p.shape[2]
    last = half + 8
    other = 1 - side
    image_s[side] = image_p[0 : half + 4]
    cot_s[side] = cot_p[0 : half + 2]
    for p in range(half + 4):
        image_s[other, p] = swapped[half + 3 - p]
    cot_s[other] = swapped[half + 4 : 2 * half + 6]
    ones = jnp.ones((16, x3.shape[1]), BF16)
    x3[192:208, :] = ones
    h3[192:208, :] = ones[:, : h3.shape[1]]
    clear(side, taps2, width, 2, half + 2, 2, half)
    clear(side, taps1, width, 3, half + 2, 3, half)
    for p in range(half + 4):
        spread(x3, p, jnp.concatenate([image_s[0, p], image_s[1, p]], axis=1))
    shift1 = jnp.broadcast_to(bias1[:, 0:1], (64, width))
    shift2 = jnp.broadcast_to(bias2[:, 0:1], (64, width))

    def first(e, acc):
        hidden, slope = silu_and_slope(acc + shift1)
        spread(h3, e - 5, hidden.astype(BF16))
        if e < half + 5:
            slopes[e - 5] = slope

    x_rows, h_rows = Rows(x3, width), Rows(h3, width)
    sweep(fwd1, [(x_rows, e - 4) for e in range(4, last)], 4, first)

    def second(e, acc):
        value, slope = silu_and_slope(acc + shift2)
        cot = jnp.concatenate([cot_s[0, e - 4], cot_s[1, e - 4]], axis=1).astype(F32)
        delta = (cot * slope).astype(BF16)
        spread(d3, e - 6, delta)
        if e < half + 4:
            hand_out(side, mine, theirs, e - 6, value)
            store_taps(side, taps2, width, 2, e - 4, delta)

    sweep(fwd2, [(h_rows, e - 5) for e in range(5, last - 1)], 5, second)

    def third(e, acc):
        delta = (acc * slopes[e - 5]).astype(BF16)
        spread(e3, e - 7, delta)
        if e < half + 4:
            store_taps(side, taps1, width, 3, e - 4, delta)

    sweep(bwd2, [(Rows(d3, width), e - 6) for e in range(6, last - 2)], 6, third)

    def fourth(e, acc):
        hand_out(side, mine, theirs, half - 2 + e - 8, acc)

    sweep(bwd1, [(Rows(e3, width), e - 7) for e in range(7, last - 3)], 7, fourth)

    grad2[...] = lax.dot_general(
        h_rows.span(0, half), taps2[...], CONTRACT, preferred_element_type=F32
    )
    grad1[...] = lax.dot_general(
        x_rows.span(2, half + 1), taps1[...], CONTRACT, preferred_element_type=F32
    )


def outer_kernel(
    edges_own,
    edges_other,
    cot_p,
    swapped,
    fwd1,
    fwd2,
    bwd2,
    bwd1,
    bias1,
    bias2,
    x3,
    h3,
    d3,
    e3,
    slopes,
    grad2,
    grad1,
    mine,
    theirs,
    grads_own,
    grads_send,
    image_s,
    cot_s,
    x3_b,
    h3_b,
    d3_b,
    e3_b,
    slopes_b,
    taps2,
    taps1,
):
    side = lax.axis_index("sx")
    place = lax.axis_index("sy")
    half = cot_p.shape[0] // 2
    width = 2 * cot_p.shape[2]
    other = 1 - side
    outside = place == side * (lax.axis_size("sy") - 1)

    def keep(value):
        return jnp.where(outside, 0.0, value.astype(F32)).astype(BF16)

    image_s[side] = keep(edges_own[0:4])
    image_s[other] = keep(edges_other[0:4])
    for half_of, ref in ((side, edges_own), (other, edges_other)):
        cot_s[half_of, 0] = keep(ref[5])
        cot_s[half_of, 1] = keep(ref[4])
    cot_s[side, 2:4] = cot_p[0:2]
    cot_s[other, 2:4] = swapped[half + 4 : half + 6]
    ones = jnp.ones((16, x3_b.shape[1]), BF16)
    x3_b[192:208, :] = ones
    h3_b[192:208, :] = ones
    clear(side, taps2, width, 0, 4, 0, 2)
    clear(side, taps1, width, 0, 5, 0, 3)
    for e in range(4):
        spread(x3_b, e, jnp.concatenate([image_s[0, e], image_s[1, e]], axis=1))
    shift1 = jnp.broadcast_to(bias1[:, 0:1], (64, width))
    shift2 = jnp.broadcast_to(bias2[:, 0:1], (64, width))

    def joined(outer, start, inner, split, first):
        outer, inner = Rows(outer, width), Rows(inner, width)
        return [
            (outer, e - start) if e < split else (inner, e - split)
            for e in range(first, first + 6)
        ]

    def first(e, acc):
        hidden, slope = silu_and_slope(acc + shift1)
        if e < 4:
            hidden = jnp.where(outside, 0.0, hidden)
        spread(h3_b, e - 1, hidden.astype(BF16))
        if e >= 3:
            slopes_b[e - 3] = slope

    sweep(fwd1, joined(x3_b, 0, x3, 4, 0), 0, first)

    def second(e, acc):
        value, slope = silu_and_slope(acc + shift2)
        cot = jnp.concatenate([cot_s[0, e - 2], cot_s[1, e - 2]], axis=1).astype(F32)
        delta = (cot * slope).astype(BF16)
        spread(d3_b, e - 2, delta)
        if e >= 4:
            hand_out(side, mine, theirs, e - 4, value)
            store_taps(side, taps2, width, 0, e - 4, delta)

    sweep(fwd2, joined(h3_b, 1, h3, 5, 1), 1, second)

    def third(e, acc):
        delta = acc * (slopes_b[e - 3] if e < 5 else slopes[e - 5])
        if e < 4:
            delta = jnp.where(outside, 0.0, delta)
        delta = delta.astype(BF16)
        spread(e3_b, e - 3, delta)
        if e >= 4:
            store_taps(side, taps1, width, 0, e - 4, delta)

    sweep(bwd2, joined(d3_b, 2, d3, 6, 2), 2, third)

    def fourth(e, acc):
        hand_out(side, mine, theirs, 2 + e - 4, acc)

    sweep(bwd1, joined(e3_b, 3, e3, 7, 3), 3, fourth)

    def product(left, right):
        return lax.dot_general(left, right, CONTRACT, preferred_element_type=F32)

    total2 = (
        grad2[...]
        + product(Rows(h3_b, width).span(2, 4), taps2[:, : 2 * width])
        + product(Rows(h3, width).span(0, 2), taps2[:, 2 * width :])
    )
    total1 = (
        grad1[...]
        + product(Rows(x3_b, width).span(3, 4), taps1[:, :width])
        + product(Rows(x3, width).span(0, 4), taps1[:, width:])
    )
    both = jnp.concatenate([total2[0:192], total1[0:192]], axis=1)
    biases = jnp.concatenate([total2[192:200, 64:128], total1[192:200, 64:128]], axis=1)
    tiles = [
        both[8 * (t // 3) : 8 * (t // 3) + 8, 128 * (t % 3) : 128 * (t % 3) + 128]
        for t in range(72)
    ]
    empty = jnp.zeros((8, 128), F32)
    low, high = tiles[:36] + [biases], tiles[36:] + [empty]
    for t in range(TILES):
        at = slice(128 * t, 128 * t + 128)
        grads_own[:, at] = jnp.where(side == 0, low[t], high[t])
        grads_send[:, at] = jnp.where(side == 0, high[t], low[t])


def pair_kernel(own, received, out):
    out[...] = (own[...] + received[...]).astype(BF16)


def add_kernel(factor, *refs):
    out = refs[-1]
    terms = [ref[...].astype(F32) for ref in refs[:-1]]
    while len(terms) > 1:
        terms = [sum(terms[n + 1 : n + 2], terms[n]) for n in range(0, len(terms), 2)]
    out[...] = (terms[0] * factor).astype(out.dtype)


def outputs_kernel(mine_a, mine_b, back_a, back_b, out, image_grad, token, natural):
    side = lax.axis_index("sx")
    rows = out.shape[2]
    half = rows // 2
    for slot in range(2):
        near_rows = 2 + 2 * slot
        for j in range(half):
            if j < near_rows:
                own, other = mine_b[2 * slot + j], back_b[2 * slot + j]
            else:
                at = slot * (half - 2) + j - near_rows
                own, other = mine_a[at], back_a[at]
            natural[slot, turned(side, j, rows)] = own
            natural[slot, turned(side, rows - 1 - j, rows)] = other
    for slot, ref in ((0, out), (1, image_grad)):
        ref[0] = jnp.transpose(natural[slot], (1, 0, 2))
    token[...] = jnp.zeros(token.shape, F32)


def grads_kernel(held, swapped, gw1, gb1, gw2, gb2):
    side = lax.axis_index("sx")

    def tile(part, t):
        at = slice(128 * t, 128 * t + 128)
        return jnp.where(side == part, held[:, at], swapped[:, at])

    for block in range(24):
        part, first = block // 12, 3 * (block % 12)
        line = jnp.concatenate([tile(part, first + p) for p in range(3)], axis=1)
        b, i = block // 8, (block % 8) * 8
        for a in range(3):
            gw2[a, b, i : i + 8, :] = line[:, a * 64 : a * 64 + 64]
            gw1[a, b, i : i + 8, :] = line[:, 192 + a * 64 : 256 + a * 64]
    biases = tile(0, 36)
    gb2[...] = biases[0:1, 0:64]
    gb1[...] = biases[0:1, 64:128]


def exchange_stages(places, planes):
    def groups(count, axis):
        bits = [1 << k for k in range(count.bit_length() - 1)]
        pairs = [bits[k : k + 2] for k in range(0, len(bits), 2)]
        return [(axis, [b[0]] + ([b[1], b[0] | b[1]] if len(b) == 2 else [])) for b in pairs]

    rows, slides = groups(places, 0), groups(planes, 1)
    stages = []
    for plan in zip(rows + slides, slides + rows):
        stage = []
        for k in range(3):
            pairs = []
            for s in range(places):
                for x, (axis, masks) in enumerate(plan):
                    for g in range(planes):
                        if k < len(masks):
                            t, h = (s ^ masks[k], g) if axis == 0 else (s, g ^ masks[k])
                            pairs.append(((2 * s + x) * planes + g, (2 * t + x) * planes + h))
            if pairs:
                stage.append(pairs)
        stages.append(stage)
    return stages


def local(image, weight_one, bias_one, weight_two, bias_two, cotangent):
    _, chans, rows, cols = image.shape
    places, planes = lax.axis_size("sy"), lax.axis_size("grp")
    half = rows // 2
    width = 2 * cols
    factor = float(rows * cols * places * planes * lax.axis_size("sx")) ** (-0.5)
    call = functools.partial(pl.pallas_call, compiler_params=PARAMS)

    def rows_of(count):
        return pltpu.VMEM((count, chans, cols), BF16)

    def flat(height, count):
        return pltpu.VMEM((height, count * width), BF16)

    image_p, cot_p, swap, edges, w1, b1, w2, b2 = call(
        pack_kernel,
        out_shape=[
            rows_of(rows),
            rows_of(rows),
            rows_of(2 * half + 6),
            rows_of(6),
            pltpu.VMEM(weight_one.shape, BF16),
            pltpu.VMEM((1, chans), F32),
            pltpu.VMEM(weight_two.shape, BF16),
            pltpu.VMEM((1, chans), F32),
        ],
        in_specs=[pl.BlockSpec(memory_space=pltpu.HBM)] * 6,
        scratch_shapes=[
            pltpu.VMEM((chans, rows, cols), BF16),
            pltpu.VMEM((chans, rows, cols), BF16),
            pltpu.SemaphoreType.DMA((chans // 8 + 4,)),
        ],
        name="pack",
    )(
        *far(image, cotangent, weight_one, bias_one.reshape(1, chans)),
        *far(weight_two, bias_two.reshape(1, chans)),
    )
    swapped = lax.ppermute(swap, "sx", SWAP)
    across = []
    for s in range(places):
        upper, lower = 2 * s + 1, 2 * ((s + 1) % places)
        across += [(upper, lower), (lower, upper)]
    edges_other = lax.ppermute(edges, ("sy", "sx"), across)
    edges_own = lax.ppermute(swapped[half : half + 6], ("sy", "sx"), across)
    weights = call(
        weights_kernel,
        out_shape=[pltpu.VMEM((192, 192), BF16)] * 4 + [pltpu.VMEM((64, 128), F32)] * 2,
        cost_estimate=lasting(0.3),
        name="weights",
    )(*near(w1, b1, w2, b2))

    x3, h3, d3, e3, slopes, mine_a, theirs_a, grad2, grad1 = call(
        inner_kernel,
        out_shape=[
            flat(208, half + 4),
            flat(208, half + 2),
            flat(192, half),
            flat(192, half - 2),
            pltpu.VMEM((half, chans, width), F32),
            rows_of(2 * half - 6),
            rows_of(2 * half - 6),
            pltpu.VMEM((208, 192), F32),
            pltpu.VMEM((208, 192), F32),
        ],
        scratch_shapes=[
            pltpu.VMEM((2, half + 4, chans, cols), BF16),
            pltpu.VMEM((2, half + 2, chans, cols), BF16),
            flat(192, half),
            flat(192, half - 1),
        ],
        cost_estimate=lasting(4.0),
        name="inner",
    )(*near(image_p, cot_p, swapped, *weights))
    back_a = lax.ppermute(theirs_a, "sx", SWAP)
    half_grads = pltpu.VMEM((8, TILES * 128), F32)
    mine_b, theirs_b, grads_own, grads_send = call(
        outer_kernel,
        out_shape=[rows_of(6), rows_of(6), half_grads, half_grads],
        scratch_shapes=[
            pltpu.VMEM((2, 4, chans, cols), BF16),
            pltpu.VMEM((2, 4, chans, cols), BF16),
            flat(208, 4),
            flat(208, 4),
            flat(192, 4),
            flat(192, 4),
            pltpu.VMEM((2, chans, width), F32),
            flat(192, 4),
            flat(192, 5),
        ],
        cost_estimate=lasting(2.0),
        name="outer",
    )(
        *near(edges_own, edges_other, cot_p, swapped, *weights),
        *near(x3, h3, d3, e3, slopes, grad2, grad1),
    )
    grads_received = lax.ppermute(grads_send, "sx", SWAP)
    back_b = lax.ppermute(theirs_b, "sx", SWAP)
    held = call(pair_kernel, out_shape=pltpu.VMEM((8, TILES * 128), BF16), name="pair")(
        *near(grads_own, grads_received)
    )
    out, image_grad, token = call(
        outputs_kernel,
        out_shape=[shape_of(image.shape, BF16)] * 2 + [pltpu.VMEM((8, 128), F32)],
        scratch_shapes=[pltpu.VMEM((2, rows, chans, cols), BF16)],
        cost_estimate=lasting(1.3),
        name="outputs",
    )(*near(mine_a, mine_b, back_a, back_b))
    stages = exchange_stages(places, planes)
    for n, stage in enumerate(stages):
        final = n == len(stages) - 1
        received = [lax.ppermute(held, ("sy", "sx", "grp"), pairs) for pairs in stage]
        behind = [token] if n == 0 else []
        held = call(
            functools.partial(behind_add if behind else add_kernel, factor if final else 1.0),
            out_shape=pltpu.VMEM((8, TILES * 128), F32 if final else BF16),
            name="add",
        )(*near(*behind, held, *received))
    swapped_sums = lax.ppermute(held, "sx", SWAP)
    weight_shape = shape_of((3, 3, chans, chans), F32)
    bias_shape = shape_of((1, chans), F32)
    gw1, gb1, gw2, gb2 = call(
        grads_kernel,
        out_shape=[weight_shape, bias_shape, weight_shape, bias_shape],
        name="grads",
    )(*near(held, swapped_sums))
    return out, image_grad, gw1, gb1.reshape(chans), gw2, gb2.reshape(chans)


def behind_add(factor, token, *refs):
    add_kernel(factor, *refs)


def solution(mesh):
    return jax.shard_map(
        local,
        mesh=mesh,
        in_specs=(P("grp", None, "sy", "sx"), P(), P(), P(), P(), P("grp", None, "sy", "sx")),
        out_specs=(P("grp", None, "sy", "sx"), P("grp", None, "sy", "sx"), P(), P(), P(), P()),
        check_vma=False,
    )
```

```python
import functools

import jax
import jax.numpy as jnp
from jax import lax
from jax.experimental import pallas as pl
from jax.experimental.pallas import tpu as pltpu
from jax.sharding import PartitionSpec as P

BF16 = jnp.bfloat16
F32 = jnp.float32
PARAMS = pltpu.CompilerParams(vmem_limit_bytes=32 * 1024 * 1024)
SWAP = [(0, 1), (1, 0)]
CONTRACT = (((1,), (1,)), ((), ()))
TILES = 37


def shape_of(shape, dtype):
    return jax.ShapeDtypeStruct(shape, dtype)


def near(*arrays):
    return [pltpu.with_memory_space_constraint(array, pltpu.VMEM) for array in arrays]


def far(*arrays):
    return [pltpu.with_memory_space_constraint(array, pltpu.HBM) for array in arrays]


def lasting(micros):
    return pl.CostEstimate(flops=int(micros * 1.1e9), transcendentals=0, bytes_accessed=0)


def turned(side, index, count):
    return index + side * (count - 1 - 2 * index)


def pack_kernel(
    image_ref,
    cot_ref,
    w1,
    b1,
    w2,
    b2,
    image_p,
    cot_p,
    swap,
    edges,
    w1_v,
    b1_v,
    w2_v,
    b2_v,
    image_v,
    cot_v,
    sems,
):
    side = lax.axis_index("sx")
    rows = image_ref.shape[2]
    half = rows // 2
    jobs, small = [], []
    sources = ((image_ref, image_v, image_p), (cot_ref, cot_v, cot_p))
    for c in range(image_ref.shape[1] // 16):
        chans = slice(16 * c, 16 * c + 16)
        for n, (src, dst, out) in enumerate(sources):
            copy = pltpu.make_async_copy(src.at[0, chans], dst.at[chans], sems.at[2 * c + n])
            copy.start()
            jobs.append((copy, chans, dst, out))
    for n, (src, dst) in enumerate(((w1, w1_v), (b1, b1_v), (w2, w2_v), (b2, b2_v))):
        copy = pltpu.make_async_copy(src, dst, sems.at[len(jobs) + n])
        copy.start()
        small.append(copy)
    for copy, chans, dst, out in jobs:
        copy.wait()
        block = jnp.transpose(dst[chans], (1, 0, 2))
        for h in range(rows):
            out[turned(side, h, rows), chans, :] = block[h]
    swap[0 : half + 4] = image_p[half - 4 : rows]
    for k in range(half + 2):
        swap[half + 4 + k] = cot_p[rows - 1 - k]
    for k in range(4):
        edges[k] = image_p[3 - k]
    edges[4:6] = cot_p[0:2]
    for copy in small:
        copy.wait()


def column(row):
    chans = row.shape[1]
    r = lax.broadcasted_iota(jnp.int32, (chans, chans), 0)
    c = lax.broadcasted_iota(jnp.int32, (chans, chans), 1)
    wide = jnp.broadcast_to(row, (chans, chans))
    return jnp.sum(jnp.where(r == c, wide, 0.0), axis=1, keepdims=True)


def weights_kernel(w1, b1, w2, b2, fwd1, fwd2, bwd2, bwd1, bias1, bias2):
    side = lax.axis_index("sx")
    for w, fwd, bwd in ((w1, fwd1, bwd1), (w2, fwd2, bwd2)):
        for a in range(3):
            tap = turned(side, a, 3)
            fwd[a * 64 : a * 64 + 64, :] = jnp.concatenate(
                [jnp.transpose(w[tap, b].astype(F32)) for b in range(3)], axis=1
            ).astype(BF16)
            bwd[a * 64 : a * 64 + 64, :] = jnp.concatenate(
                [w[2 - tap, 2 - b].astype(F32) for b in range(3)], axis=1
            ).astype(BF16)
    bias1[...] = jnp.broadcast_to(column(b1[...]), bias1.shape)
    bias2[...] = jnp.broadcast_to(column(b2[...]), bias2.shape)


def spread(dst, at, row):
    chans, width = row.shape
    zero = jnp.zeros((chans, 1), row.dtype)
    cols = slice(at * width, (at + 1) * width)
    dst[0:chans, cols] = jnp.concatenate([zero, row[:, :-1]], axis=1)
    dst[chans : 2 * chans, cols] = row
    dst[2 * chans : 3 * chans, cols] = jnp.concatenate([row[:, 1:], zero], axis=1)


def sweep(weight_ref, rows, first, emit):
    weight = weight_ref[...]
    upper = lower = None
    for n, (ref, at) in enumerate(rows):
        part = jnp.dot(weight, ref.spread_row(at), preferred_element_type=F32)
        if n >= 2:
            emit(first + n - 1, upper + part[128:192])
        upper = part[64:128] if lower is None else lower + part[64:128]
        lower = part[0:64]


class Rows:
    def __init__(self, ref, width):
        self.ref, self.width = ref, width

    def spread_row(self, at):
        return self.ref[0:192, at * self.width : (at + 1) * self.width]

    def span(self, start, stop):
        return self.ref[:, start * self.width : stop * self.width]


def joined(width, outer, start, inner, split, first, count):
    outer, inner = Rows(outer, width), Rows(inner, width)
    return [
        (outer, e - start) if e < split else (inner, e - split)
        for e in range(first, first + count)
    ]


def silu_and_slope(pre):
    gate = jax.nn.sigmoid(pre)
    return pre * gate, gate * (1.0 + pre * (1.0 - gate))


def clear(side, taps, width, start, stop, j0, j1):
    for a in range(3):
        place = pl.ds(pl.multiple_of(64 * turned(side, a, 3), 64), 64)
        for q in range(start, stop):
            if not j0 <= q - a < j1:
                at = q - start
                taps[place, at * width : (at + 1) * width] = jnp.zeros((64, width), BF16)


def store_taps(side, taps, width, start, j, delta):
    for a in range(3):
        place = pl.ds(pl.multiple_of(64 * turned(side, a, 3), 64), 64)
        at = j + a - start
        taps[place, at * width : (at + 1) * width] = delta


def hand_out(side, mine, theirs, at, value):
    width = value.shape[1]
    left, right = value[:, : width // 2], value[:, width // 2 :]
    mine[at] = jnp.where(side == 0, left, right).astype(BF16)
    theirs[at] = jnp.where(side == 0, right, left).astype(BF16)


def inner_kernel(
    image_p,
    cot_p,
    swapped,
    fwd1,
    fwd2,
    bwd2,
    bias1,
    bias2,
    x3,
    h3,
    d3,
    e3,
    slopes,
    mine,
    theirs,
    grad2,
    grad1,
    image_s,
    cot_s,
    taps2,
    taps1,
):
    side = lax.axis_index("sx")
    half = image_p.shape[0] // 2
    width = 2 * image_p.shape[2]
    last = half + 8
    other = 1 - side
    image_s[side] = image_p[0 : half + 4]
    cot_s[side] = cot_p[0 : half + 2]
    for p in range(half + 4):
        image_s[other, p] = swapped[half + 3 - p]
    cot_s[other] = swapped[half + 4 : 2 * half + 6]
    ones = jnp.ones((16, x3.shape[1]), BF16)
    x3[192:208, :] = ones
    h3[192:208, :] = ones[:, : h3.shape[1]]
    clear(side, taps2, width, 2, half + 2, 2, half)
    clear(side, taps1, width, 3, half + 2, 3, half)
    for p in range(half + 4):
        spread(x3, p, jnp.concatenate([image_s[0, p], image_s[1, p]], axis=1))
    shift1 = jnp.broadcast_to(bias1[:, 0:1], (64, width))
    shift2 = jnp.broadcast_to(bias2[:, 0:1], (64, width))

    def first(e, acc):
        hidden, slope = silu_and_slope(acc + shift1)
        spread(h3, e - 5, hidden.astype(BF16))
        if e < half + 5:
            slopes[e - 5] = slope

    x_rows, h_rows = Rows(x3, width), Rows(h3, width)
    sweep(fwd1, [(x_rows, e - 4) for e in range(4, last)], 4, first)

    def second(e, acc):
        value, slope = silu_and_slope(acc + shift2)
        cot = jnp.concatenate([cot_s[0, e - 4], cot_s[1, e - 4]], axis=1).astype(F32)
        delta = (cot * slope).astype(BF16)
        spread(d3, e - 6, delta)
        if e < half + 4:
            hand_out(side, mine, theirs, e - 6, value)
            store_taps(side, taps2, width, 2, e - 4, delta)

    sweep(fwd2, [(h_rows, e - 5) for e in range(5, last - 1)], 5, second)

    def third(e, acc):
        delta = (acc * slopes[e - 5]).astype(BF16)
        spread(e3, e - 7, delta)
        if e < half + 4:
            store_taps(side, taps1, width, 3, e - 4, delta)

    sweep(bwd2, [(Rows(d3, width), e - 6) for e in range(6, last - 2)], 6, third)

    grad2[...] = lax.dot_general(
        h_rows.span(0, half), taps2[...], CONTRACT, preferred_element_type=F32
    )
    grad1[...] = lax.dot_general(
        x_rows.span(2, half + 1), taps1[...], CONTRACT, preferred_element_type=F32
    )


def outer_kernel(
    edges,
    cot_p,
    swapped,
    fwd1,
    fwd2,
    bwd2,
    bias1,
    bias2,
    x3,
    h3,
    d3,
    slopes,
    grad2,
    grad1,
    e3_b,
    mine,
    theirs,
    grads_own,
    grads_send,
    image_s,
    cot_s,
    x3_b,
    h3_b,
    d3_b,
    slopes_b,
    taps2,
    taps1,
):
    side = lax.axis_index("sx")
    place = lax.axis_index("sy")
    half = cot_p.shape[0] // 2
    width = 2 * cot_p.shape[2]
    other = 1 - side
    outside = place == side * (lax.axis_size("sy") - 1)

    for half_of, at in ((other, 0), (side, 6)):
        image_s[half_of] = edges[at : at + 4]
        cot_s[half_of, 0] = edges[at + 5]
        cot_s[half_of, 1] = edges[at + 4]
    cot_s[side, 2:4] = cot_p[0:2]
    cot_s[other, 2:4] = swapped[half + 4 : half + 6]
    ones = jnp.ones((16, x3_b.shape[1]), BF16)
    x3_b[192:208, :] = ones
    h3_b[192:208, :] = ones
    clear(side, taps2, width, 0, 4, 0, 2)
    clear(side, taps1, width, 0, 5, 0, 3)
    for e in range(4):
        spread(x3_b, e, jnp.concatenate([image_s[0, e], image_s[1, e]], axis=1))
    shift1 = jnp.broadcast_to(bias1[:, 0:1], (64, width))
    shift2 = jnp.broadcast_to(bias2[:, 0:1], (64, width))

    def first(e, acc):
        hidden, slope = silu_and_slope(acc + shift1)
        if e < 4:
            hidden = jnp.where(outside, 0.0, hidden)
        spread(h3_b, e - 1, hidden.astype(BF16))
        if e >= 3:
            slopes_b[e - 3] = slope

    sweep(fwd1, joined(width, x3_b, 0, x3, 4, 0, 6), 0, first)

    def second(e, acc):
        value, slope = silu_and_slope(acc + shift2)
        cot = jnp.concatenate([cot_s[0, e - 2], cot_s[1, e - 2]], axis=1).astype(F32)
        delta = (cot * slope).astype(BF16)
        spread(d3_b, e - 2, delta)
        if e >= 4:
            hand_out(side, mine, theirs, e - 4, value)
            store_taps(side, taps2, width, 0, e - 4, delta)

    sweep(fwd2, joined(width, h3_b, 1, h3, 5, 1, 6), 1, second)

    def third(e, acc):
        delta = acc * (slopes_b[e - 3] if e < 5 else slopes[e - 5])
        if e < 4:
            delta = jnp.where(outside, 0.0, delta)
        delta = delta.astype(BF16)
        spread(e3_b, e - 3, delta)
        if e >= 4:
            store_taps(side, taps1, width, 0, e - 4, delta)

    sweep(bwd2, joined(width, d3_b, 2, d3, 6, 2, 6), 2, third)

    def product(left, right):
        return lax.dot_general(left, right, CONTRACT, preferred_element_type=F32)

    total2 = (
        grad2[...]
        + product(Rows(h3_b, width).span(2, 4), taps2[:, : 2 * width])
        + product(Rows(h3, width).span(0, 2), taps2[:, 2 * width :])
    )
    total1 = (
        grad1[...]
        + product(Rows(x3_b, width).span(3, 4), taps1[:, :width])
        + product(Rows(x3, width).span(0, 4), taps1[:, width:])
    )
    both = jnp.concatenate([total2[0:192], total1[0:192]], axis=1)
    biases = jnp.concatenate([total2[192:200, 64:128], total1[192:200, 64:128]], axis=1)
    tiles = [
        both[8 * (t // 3) : 8 * (t // 3) + 8, 128 * (t % 3) : 128 * (t % 3) + 128]
        for t in range(72)
    ]
    empty = jnp.zeros((8, 128), F32)
    low, high = tiles[:36] + [biases], tiles[36:] + [empty]
    for t in range(TILES):
        at = slice(128 * t, 128 * t + 128)
        grads_own[:, at] = jnp.where(side == 0, low[t], high[t])
        grads_send[:, at] = jnp.where(side == 0, high[t], low[t])


def pair_kernel(own, received, out):
    out[...] = (own[...] + received[...]).astype(BF16)


def add_kernel(factor, *refs):
    out = refs[-1]
    terms = [ref[...].astype(F32) for ref in refs[:-1]]
    while len(terms) > 1:
        terms = [sum(terms[n + 1 : n + 2], terms[n]) for n in range(0, len(terms), 2)]
    out[...] = (terms[0] * factor).astype(out.dtype)


def passing_add(add, passed, *refs):
    add(*refs[:-1])


def behind_add(add, done, *refs):
    add(*refs)


def input_kernel(held, e3_b, e3, bwd1, mine_a, mine_b, theirs_a, theirs_b, mine, theirs):
    side = lax.axis_index("sx")
    half = mine.shape[0] // 2
    width = 2 * mine.shape[2]
    for whole, inner, outer in ((mine, mine_a, mine_b), (theirs, theirs_a, theirs_b)):
        whole[0:2] = outer[...]
        whole[2:half] = inner[...]

    def emit(e, acc):
        hand_out(side, mine, theirs, half + e - 4, acc)

    sweep(bwd1, joined(width, e3_b, 3, e3, 7, 3, half + 2), 3, emit)


def outputs_kernel(mine, back, out, image_grad, token, natural):
    side = lax.axis_index("sx")
    rows = out.shape[2]
    half = rows // 2
    for slot in range(2):
        for j in range(half):
            natural[slot, turned(side, j, rows)] = mine[slot * half + j]
            natural[slot, turned(side, rows - 1 - j, rows)] = back[slot * half + j]
    for slot, ref in ((0, out), (1, image_grad)):
        ref[0] = jnp.transpose(natural[slot], (1, 0, 2))
    token[...] = jnp.zeros(token.shape, F32)


def border_kernel(edges, swapped, out):
    half = swapped.shape[0] // 2 - 3
    out[0:6] = edges[...]
    out[6:12] = swapped[half : half + 6]


def grads_kernel(held, swapped, gw1, gb1, gw2, gb2):
    side = lax.axis_index("sx")

    def tile(part, t):
        at = slice(128 * t, 128 * t + 128)
        return jnp.where(side == part, held[:, at], swapped[:, at])

    for block in range(24):
        part, first = block // 12, 3 * (block % 12)
        line = jnp.concatenate([tile(part, first + p) for p in range(3)], axis=1)
        b, i = block // 8, (block % 8) * 8
        for a in range(3):
            gw2[a, b, i : i + 8, :] = line[:, a * 64 : a * 64 + 64]
            gw1[a, b, i : i + 8, :] = line[:, 192 + a * 64 : 256 + a * 64]
    biases = tile(0, 36)
    gb2[...] = biases[0:1, 0:64]
    gb1[...] = biases[0:1, 64:128]


def exchange_stages(places, planes):
    def groups(count, axis):
        bits = [1 << k for k in range(count.bit_length() - 1)]
        pairs = [bits[k : k + 2] for k in range(0, len(bits), 2)]
        return [(axis, [b[0]] + ([b[1], b[0] | b[1]] if len(b) == 2 else [])) for b in pairs]

    rows, slides = groups(places, 0), groups(planes, 1)
    stages = []
    for plan in zip(rows + slides, slides + rows):
        stage = []
        for k in range(3):
            pairs = []
            for s in range(places):
                for x, (axis, masks) in enumerate(plan):
                    for g in range(planes):
                        if k < len(masks):
                            t, h = (s ^ masks[k], g) if axis == 0 else (s, g ^ masks[k])
                            pairs.append(((2 * s + x) * planes + g, (2 * t + x) * planes + h))
            if pairs:
                stage.append(pairs)
        stages.append(stage)
    return stages


def local(image, weight_one, bias_one, weight_two, bias_two, cotangent):
    _, chans, rows, cols = image.shape
    places, planes = lax.axis_size("sy"), lax.axis_size("grp")
    half = rows // 2
    width = 2 * cols
    factor = float(rows * cols * places * planes * lax.axis_size("sx")) ** (-0.5)
    call = functools.partial(pl.pallas_call, compiler_params=PARAMS)

    def rows_of(count):
        return pltpu.VMEM((count, chans, cols), BF16)

    def flat(height, count):
        return pltpu.VMEM((height, count * width), BF16)

    image_p, cot_p, swap, edges, w1, b1, w2, b2 = call(
        pack_kernel,
        out_shape=[
            rows_of(rows),
            rows_of(rows),
            rows_of(2 * half + 6),
            rows_of(6),
            pltpu.VMEM(weight_one.shape, BF16),
            pltpu.VMEM((1, chans), F32),
            pltpu.VMEM(weight_two.shape, BF16),
            pltpu.VMEM((1, chans), F32),
        ],
        in_specs=[pl.BlockSpec(memory_space=pltpu.HBM)] * 6,
        scratch_shapes=[
            pltpu.VMEM((chans, rows, cols), BF16),
            pltpu.VMEM((chans, rows, cols), BF16),
            pltpu.SemaphoreType.DMA((chans // 8 + 4,)),
        ],
        name="pack",
    )(
        *far(image, cotangent, weight_one, bias_one.reshape(1, chans)),
        *far(weight_two, bias_two.reshape(1, chans)),
    )
    swapped = lax.ppermute(swap, "sx", SWAP)
    across = []
    for s in range(places - 1):
        across += [(2 * s + 1, 2 * s + 2), (2 * s + 2, 2 * s + 1)]
    border = call(border_kernel, out_shape=rows_of(12), name="border")(*near(edges, swapped))
    edges = lax.ppermute(border, ("sy", "sx"), across)
    fwd1, fwd2, bwd2, bwd1, bias1, bias2 = call(
        weights_kernel,
        out_shape=[pltpu.VMEM((192, 192), BF16)] * 4 + [pltpu.VMEM((64, 128), F32)] * 2,
        cost_estimate=lasting(0.3),
        name="weights",
    )(*near(w1, b1, w2, b2))

    x3, h3, d3, e3, slopes, mine_a, theirs_a, grad2, grad1 = call(
        inner_kernel,
        out_shape=[
            flat(208, half + 4),
            flat(208, half + 2),
            flat(192, half),
            flat(192, half - 2),
            pltpu.VMEM((half, chans, width), F32),
            rows_of(half - 2),
            rows_of(half - 2),
            pltpu.VMEM((208, 192), F32),
            pltpu.VMEM((208, 192), F32),
        ],
        scratch_shapes=[
            pltpu.VMEM((2, half + 4, chans, cols), BF16),
            pltpu.VMEM((2, half + 2, chans, cols), BF16),
            flat(192, half),
            flat(192, half - 1),
        ],
        cost_estimate=lasting(4.0),
        name="inner",
    )(*near(image_p, cot_p, swapped, fwd1, fwd2, bwd2, bias1, bias2))
    half_grads = pltpu.VMEM((8, TILES * 128), F32)
    e3_b, mine_b, theirs_b, grads_own, grads_send = call(
        outer_kernel,
        out_shape=[flat(192, 4), rows_of(2), rows_of(2), half_grads, half_grads],
        scratch_shapes=[
            pltpu.VMEM((2, 4, chans, cols), BF16),
            pltpu.VMEM((2, 4, chans, cols), BF16),
            flat(208, 4),
            flat(208, 4),
            flat(192, 4),
            pltpu.VMEM((2, chans, width), F32),
            flat(192, 4),
            flat(192, 5),
        ],
        cost_estimate=lasting(2.0),
        name="outer",
    )(
        *near(edges, cot_p, swapped, fwd1, fwd2, bwd2, bias1, bias2),
        *near(x3, h3, d3, slopes, grad2, grad1),
    )
    grads_received = lax.ppermute(grads_send, "sx", SWAP)
    held = call(pair_kernel, out_shape=pltpu.VMEM((8, TILES * 128), BF16), name="pair")(
        *near(grads_own, grads_received)
    )
    stages = exchange_stages(places, planes)
    for n, stage in enumerate(stages):
        final = n == len(stages) - 1
        received = [lax.ppermute(held, ("sy", "sx", "grp"), pairs) for pairs in stage]
        sums = pltpu.VMEM((8, TILES * 128), F32 if final else BF16)
        add = functools.partial(add_kernel, factor if final else 1.0)
        if n == 0:
            mine, theirs = call(
                input_kernel,
                out_shape=[rows_of(rows), rows_of(rows)],
                cost_estimate=lasting(1.0),
                name="input",
            )(*near(held, e3_b, e3, bwd1, mine_a, mine_b, theirs_a, theirs_b))
            held, theirs = call(
                functools.partial(passing_add, add),
                out_shape=[sums, rows_of(rows)],
                input_output_aliases={0: 1},
                name="add",
            )(*near(theirs, held, *received))
            back = lax.ppermute(theirs, "sx", SWAP)
            out, image_grad, done = call(
                outputs_kernel,
                out_shape=[shape_of(image.shape, BF16)] * 2 + [pltpu.VMEM((8, 128), F32)],
                scratch_shapes=[pltpu.VMEM((2, rows, chans, cols), BF16)],
                cost_estimate=lasting(1.3),
                name="outputs",
            )(*near(mine, back))
        elif n == 1:
            held = call(functools.partial(behind_add, add), out_shape=sums, name="add")(
                *near(done, held, *received)
            )
        else:
            held = call(add, out_shape=sums, name="add")(*near(held, *received))
    swapped_sums = lax.ppermute(held, "sx", SWAP)
    weight_shape = shape_of((3, 3, chans, chans), F32)
    bias_shape = shape_of((1, chans), F32)
    gw1, gb1, gw2, gb2 = call(
        grads_kernel,
        out_shape=[weight_shape, bias_shape, weight_shape, bias_shape],
        name="grads",
    )(*near(held, swapped_sums))
    return out, image_grad, gw1, gb1.reshape(chans), gw2, gb2.reshape(chans)


def solution(mesh):
    return jax.shard_map(
        local,
        mesh=mesh,
        in_specs=(P("grp", None, "sy", "sx"), P(), P(), P(), P(), P("grp", None, "sy", "sx")),
        out_specs=(P("grp", None, "sy", "sx"), P("grp", None, "sy", "sx"), P(), P(), P(), P()),
        check_vma=False,
    )
```

```python
import functools

import jax
import jax.numpy as jnp
from jax import lax
from jax.experimental import pallas as pl
from jax.experimental.pallas import tpu as pltpu
from jax.sharding import PartitionSpec as P

BF16 = jnp.bfloat16
F32 = jnp.float32
PARAMS = pltpu.CompilerParams(vmem_limit_bytes=32 * 1024 * 1024)
SWAP = [(0, 1), (1, 0)]
CONTRACT = (((1,), (1,)), ((), ()))
CHUNK = 10 * 128


def shape_of(shape, dtype):
    return jax.ShapeDtypeStruct(shape, dtype)


def near(*arrays):
    return [pltpu.with_memory_space_constraint(array, pltpu.VMEM) for array in arrays]


def far(*arrays):
    return [pltpu.with_memory_space_constraint(array, pltpu.HBM) for array in arrays]


def lasting(micros):
    return pl.CostEstimate(flops=int(micros * 1.1e9), transcendentals=0, bytes_accessed=0)


def turned(side, index, count):
    return index + side * (count - 1 - 2 * index)


def pack_kernel(
    image_ref,
    cot_ref,
    w1,
    b1,
    w2,
    b2,
    image_p,
    cot_p,
    swap,
    edges,
    w1_v,
    b1_v,
    w2_v,
    b2_v,
    image_v,
    cot_v,
    sems,
):
    side = lax.axis_index("sx")
    rows = image_ref.shape[2]
    half = rows // 2
    jobs, small = [], []
    sources = ((image_ref, image_v, image_p), (cot_ref, cot_v, cot_p))
    for c in range(image_ref.shape[1] // 16):
        chans = slice(16 * c, 16 * c + 16)
        for n, (src, dst, out) in enumerate(sources):
            copy = pltpu.make_async_copy(src.at[0, chans], dst.at[chans], sems.at[2 * c + n])
            copy.start()
            jobs.append((copy, chans, dst, out))
    for n, (src, dst) in enumerate(((w1, w1_v), (b1, b1_v), (w2, w2_v), (b2, b2_v))):
        copy = pltpu.make_async_copy(src, dst, sems.at[len(jobs) + n])
        copy.start()
        small.append(copy)
    for copy, chans, dst, out in jobs:
        copy.wait()
        block = jnp.transpose(dst[chans], (1, 0, 2))
        for h in range(rows):
            out[turned(side, h, rows), chans, :] = block[h]
    swap[0 : half + 4] = image_p[half - 4 : rows]
    for k in range(half + 2):
        swap[half + 4 + k] = cot_p[rows - 1 - k]
    for k in range(4):
        edges[k] = image_p[3 - k]
    edges[4:6] = cot_p[0:2]
    for copy in small:
        copy.wait()


def column(row):
    chans = row.shape[1]
    r = lax.broadcasted_iota(jnp.int32, (chans, chans), 0)
    c = lax.broadcasted_iota(jnp.int32, (chans, chans), 1)
    wide = jnp.broadcast_to(row, (chans, chans))
    return jnp.sum(jnp.where(r == c, wide, 0.0), axis=1, keepdims=True)


def weights_kernel(w1, b1, w2, b2, fwd1, fwd2, bwd2, bwd1, bias1, bias2):
    side = lax.axis_index("sx")
    for w, fwd, bwd in ((w1, fwd1, bwd1), (w2, fwd2, bwd2)):
        for a in range(3):
            tap = turned(side, a, 3)
            fwd[a * 64 : a * 64 + 64, :] = jnp.concatenate(
                [jnp.transpose(w[tap, b].astype(F32)) for b in range(3)], axis=1
            ).astype(BF16)
            bwd[a * 64 : a * 64 + 64, :] = jnp.concatenate(
                [w[2 - tap, 2 - b].astype(F32) for b in range(3)], axis=1
            ).astype(BF16)
    bias1[...] = jnp.broadcast_to(column(b1[...]), bias1.shape)
    bias2[...] = jnp.broadcast_to(column(b2[...]), bias2.shape)


def spread(dst, at, row):
    chans, width = row.shape
    zero = jnp.zeros((chans, 1), row.dtype)
    cols = slice(at * width, (at + 1) * width)
    dst[0:chans, cols] = jnp.concatenate([zero, row[:, :-1]], axis=1)
    dst[chans : 2 * chans, cols] = row
    dst[2 * chans : 3 * chans, cols] = jnp.concatenate([row[:, 1:], zero], axis=1)


def sweep(weight_ref, rows, first, emit):
    weight = weight_ref[...]
    upper = lower = None
    for n, (ref, at) in enumerate(rows):
        part = jnp.dot(weight, ref.spread_row(at), preferred_element_type=F32)
        if n >= 2:
            emit(first + n - 1, upper + part[128:192])
        upper = part[64:128] if lower is None else lower + part[64:128]
        lower = part[0:64]


class Rows:
    def __init__(self, ref, width):
        self.ref, self.width = ref, width

    def spread_row(self, at):
        return self.ref[0:192, at * self.width : (at + 1) * self.width]

    def span(self, start, stop):
        return self.ref[:, start * self.width : stop * self.width]


def joined(width, outer, start, inner, split, first, count):
    outer, inner = Rows(outer, width), Rows(inner, width)
    return [
        (outer, e - start) if e < split else (inner, e - split)
        for e in range(first, first + count)
    ]


def silu_and_slope(pre):
    gate = jax.nn.sigmoid(pre)
    return pre * gate, gate * (1.0 + pre * (1.0 - gate))


def clear(side, taps, width, start, stop, j0, j1):
    for a in range(3):
        place = pl.ds(pl.multiple_of(64 * turned(side, a, 3), 64), 64)
        for q in range(start, stop):
            if not j0 <= q - a < j1:
                at = q - start
                taps[place, at * width : (at + 1) * width] = jnp.zeros((64, width), BF16)


def store_taps(side, taps, width, start, j, delta):
    for a in range(3):
        place = pl.ds(pl.multiple_of(64 * turned(side, a, 3), 64), 64)
        at = j + a - start
        taps[place, at * width : (at + 1) * width] = delta


def hand_out(side, mine, theirs, at, value):
    width = value.shape[1]
    left, right = value[:, : width // 2], value[:, width // 2 :]
    mine[at] = jnp.where(side == 0, left, right).astype(BF16)
    theirs[at] = jnp.where(side == 0, right, left).astype(BF16)


def inner_kernel(
    image_p,
    cot_p,
    swapped,
    fwd1,
    fwd2,
    bwd2,
    bias1,
    bias2,
    x3,
    h3,
    d3,
    e3,
    slopes,
    mine,
    theirs,
    grad2,
    grad1,
    image_s,
    cot_s,
    taps2,
    taps1,
):
    side = lax.axis_index("sx")
    half = image_p.shape[0] // 2
    width = 2 * image_p.shape[2]
    last = half + 8
    other = 1 - side
    image_s[side] = image_p[0 : half + 4]
    cot_s[side] = cot_p[0 : half + 2]
    for p in range(half + 4):
        image_s[other, p] = swapped[half + 3 - p]
    cot_s[other] = swapped[half + 4 : 2 * half + 6]
    ones = jnp.ones((16, x3.shape[1]), BF16)
    x3[192:208, :] = ones
    h3[192:208, :] = ones[:, : h3.shape[1]]
    clear(side, taps2, width, 2, half + 2, 2, half)
    clear(side, taps1, width, 3, half + 2, 3, half)
    for p in range(half + 4):
        spread(x3, p, jnp.concatenate([image_s[0, p], image_s[1, p]], axis=1))
    shift1 = jnp.broadcast_to(bias1[:, 0:1], (64, width))
    shift2 = jnp.broadcast_to(bias2[:, 0:1], (64, width))

    def first(e, acc):
        hidden, slope = silu_and_slope(acc + shift1)
        spread(h3, e - 5, hidden.astype(BF16))
        if e < half + 5:
            slopes[e - 5] = slope

    x_rows, h_rows = Rows(x3, width), Rows(h3, width)
    sweep(fwd1, [(x_rows, e - 4) for e in range(4, last)], 4, first)

    def second(e, acc):
        value, slope = silu_and_slope(acc + shift2)
        cot = jnp.concatenate([cot_s[0, e - 4], cot_s[1, e - 4]], axis=1).astype(F32)
        delta = (cot * slope).astype(BF16)
        spread(d3, e - 6, delta)
        if e < half + 4:
            hand_out(side, mine, theirs, e - 6, value)
            store_taps(side, taps2, width, 2, e - 4, delta)

    sweep(fwd2, [(h_rows, e - 5) for e in range(5, last - 1)], 5, second)

    def third(e, acc):
        delta = (acc * slopes[e - 5]).astype(BF16)
        spread(e3, e - 7, delta)
        if e < half + 4:
            store_taps(side, taps1, width, 3, e - 4, delta)

    sweep(bwd2, [(Rows(d3, width), e - 6) for e in range(6, last - 2)], 6, third)

    grad2[...] = lax.dot_general(
        h_rows.span(0, half), taps2[...], CONTRACT, preferred_element_type=F32
    )
    grad1[...] = lax.dot_general(
        x_rows.span(2, half + 1), taps1[...], CONTRACT, preferred_element_type=F32
    )


def outer_kernel(
    edges_own,
    edges_other,
    cot_p,
    swapped,
    fwd1,
    fwd2,
    bwd2,
    bias1,
    bias2,
    x3,
    h3,
    d3,
    slopes,
    grad2,
    grad1,
    e3_b,
    mine,
    theirs,
    grads_own,
    grads_send,
    image_s,
    cot_s,
    x3_b,
    h3_b,
    d3_b,
    slopes_b,
    taps2,
    taps1,
):
    side = lax.axis_index("sx")
    place = lax.axis_index("sy")
    half = cot_p.shape[0] // 2
    width = 2 * cot_p.shape[2]
    other = 1 - side
    outside = place == side * (lax.axis_size("sy") - 1)

    for half_of, edges in ((side, edges_own), (other, edges_other)):
        image_s[half_of] = edges[0:4]
        cot_s[half_of, 0] = edges[5]
        cot_s[half_of, 1] = edges[4]
    cot_s[side, 2:4] = cot_p[0:2]
    cot_s[other, 2:4] = swapped[half + 4 : half + 6]
    ones = jnp.ones((16, x3_b.shape[1]), BF16)
    x3_b[192:208, :] = ones
    h3_b[192:208, :] = ones
    clear(side, taps2, width, 0, 4, 0, 2)
    clear(side, taps1, width, 0, 5, 0, 3)
    for e in range(4):
        spread(x3_b, e, jnp.concatenate([image_s[0, e], image_s[1, e]], axis=1))
    shift1 = jnp.broadcast_to(bias1[:, 0:1], (64, width))
    shift2 = jnp.broadcast_to(bias2[:, 0:1], (64, width))

    def first(e, acc):
        hidden, slope = silu_and_slope(acc + shift1)
        if e < 4:
            hidden = jnp.where(outside, 0.0, hidden)
        spread(h3_b, e - 1, hidden.astype(BF16))
        if e >= 3:
            slopes_b[e - 3] = slope

    sweep(fwd1, joined(width, x3_b, 0, x3, 4, 0, 6), 0, first)

    def second(e, acc):
        value, slope = silu_and_slope(acc + shift2)
        cot = jnp.concatenate([cot_s[0, e - 2], cot_s[1, e - 2]], axis=1).astype(F32)
        delta = (cot * slope).astype(BF16)
        spread(d3_b, e - 2, delta)
        if e >= 4:
            hand_out(side, mine, theirs, e - 4, value)
            store_taps(side, taps2, width, 0, e - 4, delta)

    sweep(fwd2, joined(width, h3_b, 1, h3, 5, 1, 6), 1, second)

    def third(e, acc):
        delta = acc * (slopes_b[e - 3] if e < 5 else slopes[e - 5])
        if e < 4:
            delta = jnp.where(outside, 0.0, delta)
        delta = delta.astype(BF16)
        spread(e3_b, e - 3, delta)
        if e >= 4:
            store_taps(side, taps1, width, 0, e - 4, delta)

    sweep(bwd2, joined(width, d3_b, 2, d3, 6, 2, 6), 2, third)

    def product(left, right):
        return lax.dot_general(left, right, CONTRACT, preferred_element_type=F32)

    total2 = (
        grad2[...]
        + product(Rows(h3_b, width).span(2, 4), taps2[:, : 2 * width])
        + product(Rows(h3, width).span(0, 2), taps2[:, 2 * width :])
    )
    total1 = (
        grad1[...]
        + product(Rows(x3_b, width).span(3, 4), taps1[:, :width])
        + product(Rows(x3, width).span(0, 4), taps1[:, width:])
    )
    both = jnp.concatenate([total2[0:192], total1[0:192]], axis=1)
    biases = jnp.concatenate([total2[192:200, 64:128], total1[192:200, 64:128]], axis=1)
    tiles = [
        both[8 * (t // 3) : 8 * (t // 3) + 8, 128 * (t % 3) : 128 * (t % 3) + 128]
        for t in range(72)
    ]
    empty = jnp.zeros((8, 128), F32)
    for c in range(4):
        low = tiles[9 * c : 9 * c + 9] + [biases if c == 0 else empty]
        high = tiles[36 + 9 * c : 45 + 9 * c] + [empty]
        for t in range(10):
            at = slice(128 * t, 128 * t + 128)
            grads_own[c, :, at] = jnp.where(side == 0, low[t], high[t])
            grads_send[c, :, at] = jnp.where(side == 0, high[t], low[t])


def member():
    side = lax.axis_index("sx")
    return jnp.where(side == 0, lax.axis_index("sy") % 4, lax.axis_index("grp") % 4)


def pair_kernel(own, received, kept, *sent):
    me = member()
    kept[...] = own[me] + received[me]
    for k, out in enumerate(sent):
        at = me ^ (k + 1)
        out[...] = (own[at] + received[at]).astype(BF16)


def collect_kernel(held, *refs):
    me = member()
    out = refs[-1]
    out[me] = held[...]
    for k, ref in enumerate(refs[:-1]):
        out[me ^ (k + 1)] = ref[...]


def add_kernel(factor, *refs):
    out = refs[-1]
    terms = [ref[...].astype(F32) for ref in refs[:-1]]
    while len(terms) > 1:
        terms = [sum(terms[n + 1 : n + 2], terms[n]) for n in range(0, len(terms), 2)]
    out[...] = (terms[0] * factor).astype(out.dtype)


def passing_add(add, passed, *refs):
    add(*refs[:-1])


def behind_add(add, done, *refs):
    add(*refs)


def input_kernel(held, e3_b, e3, bwd1, mine_a, mine_b, theirs_a, theirs_b, mine, theirs):
    side = lax.axis_index("sx")
    half = mine.shape[0] // 2
    width = 2 * mine.shape[2]
    for whole, inner, outer in ((mine, mine_a, mine_b), (theirs, theirs_a, theirs_b)):
        whole[0:2] = outer[...]
        whole[2:half] = inner[...]

    def emit(e, acc):
        hand_out(side, mine, theirs, half + e - 4, acc)

    sweep(bwd1, joined(width, e3_b, 3, e3, 7, 3, half + 2), 3, emit)


def outputs_kernel(mine, back, out, image_grad, token, natural):
    side = lax.axis_index("sx")
    rows = out.shape[2]
    half = rows // 2
    for slot in range(2):
        for j in range(half):
            natural[slot, turned(side, j, rows)] = mine[slot * half + j]
            natural[slot, turned(side, rows - 1 - j, rows)] = back[slot * half + j]
    for slot, ref in ((0, out), (1, image_grad)):
        ref[0] = jnp.transpose(natural[slot], (1, 0, 2))
    token[...] = jnp.zeros(token.shape, F32)


def place_half(values, part, gw1, gw2, buffer, sems):
    copies = []
    for k in range(12):
        at = 384 * (k % 3)
        line = values[k // 3][:, at : at + 384].astype(F32)
        for a in range(3):
            buffer[0, a, 8 * k : 8 * k + 8] = line[:, 192 + 64 * a : 256 + 64 * a]
            buffer[1, a, 8 * k : 8 * k + 8] = line[:, 64 * a : 64 * a + 64]
        if k % 4 == 3:
            m = k // 4
            block = 3 * part + m
            b, i = block // 2, pl.multiple_of(32 * (block % 2), 32)
            for layer, gw in enumerate((gw1, gw2)):
                for a in range(3):
                    copy = pltpu.make_async_copy(
                        buffer.at[layer, a, 32 * m : 32 * m + 32],
                        gw.at[a, b, pl.ds(i, 32)],
                        sems.at[len(copies)],
                    )
                    copy.start()
                    copies.append(copy)
    for copy in copies:
        copy.wait()


def own_grads_kernel(held, gw1, gw2, buffer, sems):
    place_half(held, lax.axis_index("sx"), gw1, gw2, buffer, sems)


def other_grads_kernel(held, swapped, gw1_in, gw2_in, gw1, gw2, gb1, gb2, buffer, sems):
    side = lax.axis_index("sx")
    biases = [ref[0][:, CHUNK - 128 :].astype(F32)[0:1] for ref in (held, swapped)]
    line = jnp.where(side == 0, biases[0], biases[1])
    gb2[...] = line[:, 0:64]
    gb1[...] = line[:, 64:128]
    place_half(swapped, 1 - side, gw1, gw2, buffer, sems)


def exchange_stages(places, planes):
    def groups(count, axis):
        bits = [1 << k for k in range(count.bit_length() - 1)]
        pairs = [bits[k : k + 2] for k in range(0, len(bits), 2)]
        return [(axis, [b[0]] + ([b[1], b[0] | b[1]] if len(b) == 2 else [])) for b in pairs]

    rows, slides = groups(places, 0), groups(planes, 1)
    stages = []
    for plan in zip(rows + slides, slides + rows):
        stage = []
        for k in range(3):
            pairs = []
            for s in range(places):
                for x, (axis, masks) in enumerate(plan):
                    for g in range(planes):
                        if k < len(masks):
                            t, h = (s ^ masks[k], g) if axis == 0 else (s, g ^ masks[k])
                            pairs.append(((2 * s + x) * planes + g, (2 * t + x) * planes + h))
            if pairs:
                stage.append(pairs)
        stages.append(stage)
    return stages


def local(image, weight_one, bias_one, weight_two, bias_two, cotangent):
    _, chans, rows, cols = image.shape
    places, planes = lax.axis_size("sy"), lax.axis_size("grp")
    half = rows // 2
    width = 2 * cols
    factor = float(rows * cols * places * planes * lax.axis_size("sx")) ** (-0.5)
    call = functools.partial(pl.pallas_call, compiler_params=PARAMS)

    def rows_of(count):
        return pltpu.VMEM((count, chans, cols), BF16)

    def flat(height, count):
        return pltpu.VMEM((height, count * width), BF16)

    image_p, cot_p, swap, edges, w1, b1, w2, b2 = call(
        pack_kernel,
        out_shape=[
            rows_of(rows),
            rows_of(rows),
            rows_of(2 * half + 6),
            rows_of(6),
            pltpu.VMEM(weight_one.shape, BF16),
            pltpu.VMEM((1, chans), F32),
            pltpu.VMEM(weight_two.shape, BF16),
            pltpu.VMEM((1, chans), F32),
        ],
        in_specs=[pl.BlockSpec(memory_space=pltpu.HBM)] * 6,
        scratch_shapes=[
            pltpu.VMEM((chans, rows, cols), BF16),
            pltpu.VMEM((chans, rows, cols), BF16),
            pltpu.SemaphoreType.DMA((chans // 8 + 4,)),
        ],
        name="pack",
    )(
        *far(image, cotangent, weight_one, bias_one.reshape(1, chans)),
        *far(weight_two, bias_two.reshape(1, chans)),
    )
    swapped = lax.ppermute(swap, "sx", SWAP)
    across = []
    for s in range(places - 1):
        across += [(2 * s + 1, 2 * s + 2), (2 * s + 2, 2 * s + 1)]
    edges_other = lax.ppermute(edges, ("sy", "sx"), across)
    edges_own = lax.ppermute(swapped[half : half + 6], ("sy", "sx"), across)
    fwd1, fwd2, bwd2, bwd1, bias1, bias2 = call(
        weights_kernel,
        out_shape=[pltpu.VMEM((192, 192), BF16)] * 4 + [pltpu.VMEM((64, 128), F32)] * 2,
        cost_estimate=lasting(0.3),
        name="weights",
    )(*near(w1, b1, w2, b2))

    x3, h3, d3, e3, slopes, mine_a, theirs_a, grad2, grad1 = call(
        inner_kernel,
        out_shape=[
            flat(208, half + 4),
            flat(208, half + 2),
            flat(192, half),
            flat(192, half - 2),
            pltpu.VMEM((half, chans, width), F32),
            rows_of(half - 2),
            rows_of(half - 2),
            pltpu.VMEM((208, 192), F32),
            pltpu.VMEM((208, 192), F32),
        ],
        scratch_shapes=[
            pltpu.VMEM((2, half + 4, chans, cols), BF16),
            pltpu.VMEM((2, half + 2, chans, cols), BF16),
            flat(192, half),
            flat(192, half - 1),
        ],
        cost_estimate=lasting(4.0),
        name="inner",
    )(*near(image_p, cot_p, swapped, fwd1, fwd2, bwd2, bias1, bias2))
    half_grads = pltpu.VMEM((4, 8, CHUNK), F32)
    e3_b, mine_b, theirs_b, grads_own, grads_send = call(
        outer_kernel,
        out_shape=[flat(192, 4), rows_of(2), rows_of(2), half_grads, half_grads],
        scratch_shapes=[
            pltpu.VMEM((2, 4, chans, cols), BF16),
            pltpu.VMEM((2, 4, chans, cols), BF16),
            flat(208, 4),
            flat(208, 4),
            flat(192, 4),
            pltpu.VMEM((2, chans, width), F32),
            flat(192, 4),
            flat(192, 5),
        ],
        cost_estimate=lasting(2.0),
        name="outer",
    )(
        *near(edges_own, edges_other, cot_p, swapped, fwd1, fwd2, bwd2, bias1, bias2),
        *near(x3, h3, d3, slopes, grad2, grad1),
    )
    grads_received = lax.ppermute(grads_send, "sx", SWAP)
    stages = exchange_stages(places, planes)
    chunk = pltpu.VMEM((8, CHUNK), BF16)

    def trade(stage, values):
        return [
            lax.ppermute(value, ("sy", "sx", "grp"), pairs) for value, pairs in zip(values, stage)
        ]

    kept, *sent = call(
        pair_kernel, out_shape=[pltpu.VMEM((8, CHUNK), F32)] + [chunk] * 3, name="pair"
    )(*near(grads_own, grads_received))
    received = trade(stages[0], sent)
    mine, theirs = call(
        input_kernel,
        out_shape=[rows_of(rows), rows_of(rows)],
        cost_estimate=lasting(1.0),
        name="input",
    )(*near(kept, e3_b, e3, bwd1, mine_a, mine_b, theirs_a, theirs_b))
    held, theirs = call(
        functools.partial(passing_add, functools.partial(add_kernel, 1.0)),
        out_shape=[chunk, rows_of(rows)],
        input_output_aliases={0: 1},
        name="add",
    )(*near(theirs, kept, *received))
    back = lax.ppermute(theirs, "sx", SWAP)
    out, image_grad, done = call(
        outputs_kernel,
        out_shape=[shape_of(image.shape, BF16)] * 2 + [pltpu.VMEM((8, 128), F32)],
        scratch_shapes=[pltpu.VMEM((2, rows, chans, cols), BF16)],
        cost_estimate=lasting(1.3),
        name="outputs",
    )(*near(mine, back))
    for n, stage in enumerate(stages[1:], 2):
        received = trade(stage, [held] * len(stage))
        add = functools.partial(add_kernel, factor if n == len(stages) else 1.0)
        if n == 2:
            held = call(functools.partial(behind_add, add), out_shape=chunk, name="add")(
                *near(done, held, *received)
            )
        else:
            held = call(add, out_shape=chunk, name="add")(*near(held, *received))
    held = call(collect_kernel, out_shape=pltpu.VMEM((4, 8, CHUNK), BF16), name="collect")(
        *near(held, *trade(stages[0], [held] * 3))
    )
    swapped_sums = lax.ppermute(held, "sx", SWAP)
    weight_shape = shape_of((3, 3, chans, chans), F32)
    bias_shape = shape_of((1, chans), F32)
    hbm, vmem = pl.BlockSpec(memory_space=pltpu.HBM), pl.BlockSpec(memory_space=pltpu.VMEM)
    scratch = [pltpu.VMEM((2, 3, 96, chans), F32), pltpu.SemaphoreType.DMA((18,))]
    gw1, gw2 = call(
        own_grads_kernel,
        out_shape=[weight_shape] * 2,
        out_specs=[hbm] * 2,
        scratch_shapes=scratch,
        cost_estimate=lasting(0.6),
        name="own_grads",
    )(*near(held))
    gw1, gw2, gb1, gb2 = call(
        other_grads_kernel,
        out_shape=[weight_shape, weight_shape, bias_shape, bias_shape],
        in_specs=[vmem, vmem, hbm, hbm],
        out_specs=[hbm, hbm, vmem, vmem],
        input_output_aliases={2: 0, 3: 1},
        scratch_shapes=scratch,
        name="other_grads",
    )(*near(held, swapped_sums), *far(gw1, gw2))
    return out, image_grad, gw1, gb1.reshape(chans), gw2, gb2.reshape(chans)


def solution(mesh):
    return jax.shard_map(
        local,
        mesh=mesh,
        in_specs=(P("grp", None, "sy", "sx"), P(), P(), P(), P(), P("grp", None, "sy", "sx")),
        out_specs=(P("grp", None, "sy", "sx"), P("grp", None, "sy", "sx"), P(), P(), P(), P()),
        check_vma=False,
    )
```

```python
import functools

import jax
import jax.numpy as jnp
from jax import lax
from jax.experimental import pallas as pl
from jax.experimental.pallas import tpu as pltpu
from jax.sharding import PartitionSpec as P

BF16 = jnp.bfloat16
F32 = jnp.float32
PARAMS = pltpu.CompilerParams(vmem_limit_bytes=32 * 1024 * 1024)
SWAP = [(0, 1), (1, 0)]
CONTRACT = (((1,), (1,)), ((), ()))
TILES = 37


def shape_of(shape, dtype):
    return jax.ShapeDtypeStruct(shape, dtype)


def near(*arrays):
    return [pltpu.with_memory_space_constraint(array, pltpu.VMEM) for array in arrays]


def far(*arrays):
    return [pltpu.with_memory_space_constraint(array, pltpu.HBM) for array in arrays]


def lasting(micros):
    return pl.CostEstimate(flops=int(micros * 1.1e9), transcendentals=0, bytes_accessed=0)


def turned(side, index, count):
    return index + side * (count - 1 - 2 * index)


def pack_kernel(
    image_ref,
    cot_ref,
    w1,
    b1,
    w2,
    b2,
    image_p,
    cot_p,
    swap,
    edges,
    w1_v,
    b1_v,
    w2_v,
    b2_v,
    image_v,
    cot_v,
    sems,
):
    side = lax.axis_index("sx")
    rows = image_ref.shape[2]
    half = rows // 2
    jobs, small = [], []
    sources = ((image_ref, image_v, image_p), (cot_ref, cot_v, cot_p))
    for c in range(image_ref.shape[1] // 16):
        chans = slice(16 * c, 16 * c + 16)
        for n, (src, dst, out) in enumerate(sources):
            copy = pltpu.make_async_copy(src.at[0, chans], dst.at[chans], sems.at[2 * c + n])
            copy.start()
            jobs.append((copy, chans, dst, out))
    for n, (src, dst) in enumerate(((w1, w1_v), (b1, b1_v), (w2, w2_v), (b2, b2_v))):
        copy = pltpu.make_async_copy(src, dst, sems.at[len(jobs) + n])
        copy.start()
        small.append(copy)
    for copy, chans, dst, out in jobs:
        copy.wait()
        block = jnp.transpose(dst[chans], (1, 0, 2))
        for h in range(rows):
            out[turned(side, h, rows), chans, :] = block[h]
    swap[0 : half + 4] = image_p[half - 4 : rows]
    for k in range(half + 2):
        swap[half + 4 + k] = cot_p[rows - 1 - k]
    for k in range(4):
        edges[k] = image_p[3 - k]
    edges[4:6] = cot_p[0:2]
    for copy in small:
        copy.wait()


def column(row):
    chans = row.shape[1]
    r = lax.broadcasted_iota(jnp.int32, (chans, chans), 0)
    c = lax.broadcasted_iota(jnp.int32, (chans, chans), 1)
    wide = jnp.broadcast_to(row, (chans, chans))
    return jnp.sum(jnp.where(r == c, wide, 0.0), axis=1, keepdims=True)


def weights_kernel(w1, b1, w2, b2, fwd1, fwd2, bwd2, bwd1, bias1, bias2):
    side = lax.axis_index("sx")
    for w, fwd, bwd in ((w1, fwd1, bwd1), (w2, fwd2, bwd2)):
        for a in range(3):
            tap = turned(side, a, 3)
            fwd[a * 64 : a * 64 + 64, :] = jnp.concatenate(
                [jnp.transpose(w[tap, b].astype(F32)) for b in range(3)], axis=1
            ).astype(BF16)
            bwd[a * 64 : a * 64 + 64, :] = jnp.concatenate(
                [w[2 - tap, 2 - b].astype(F32) for b in range(3)], axis=1
            ).astype(BF16)
    bias1[...] = jnp.broadcast_to(column(b1[...]), bias1.shape)
    bias2[...] = jnp.broadcast_to(column(b2[...]), bias2.shape)


def spread(dst, at, row):
    chans, width = row.shape
    zero = jnp.zeros((chans, 1), row.dtype)
    cols = slice(at * width, (at + 1) * width)
    dst[0:chans, cols] = jnp.concatenate([zero, row[:, :-1]], axis=1)
    dst[chans : 2 * chans, cols] = row
    dst[2 * chans : 3 * chans, cols] = jnp.concatenate([row[:, 1:], zero], axis=1)


def sweep(weight_ref, rows, first, emit):
    weight = weight_ref[...]
    upper = lower = None
    for n, (ref, at) in enumerate(rows):
        part = jnp.dot(weight, ref.spread_row(at), preferred_element_type=F32)
        if n >= 2:
            emit(first + n - 1, upper + part[128:192])
        upper = part[64:128] if lower is None else lower + part[64:128]
        lower = part[0:64]


class Rows:
    def __init__(self, ref, width):
        self.ref, self.width = ref, width

    def spread_row(self, at):
        return self.ref[0:192, at * self.width : (at + 1) * self.width]

    def span(self, start, stop):
        return self.ref[:, start * self.width : stop * self.width]


def joined(width, outer, start, inner, split, first, count):
    outer, inner = Rows(outer, width), Rows(inner, width)
    return [
        (outer, e - start) if e < split else (inner, e - split)
        for e in range(first, first + count)
    ]


def silu_and_slope(pre):
    gate = 0.5 + 0.5 * jnp.tanh(0.5 * pre)
    value = pre * gate
    return value, gate + value * (1.0 - gate)


def clear(side, taps, width, start, stop, j0, j1):
    for a in range(3):
        place = pl.ds(pl.multiple_of(64 * turned(side, a, 3), 64), 64)
        for q in range(start, stop):
            if not j0 <= q - a < j1:
                at = q - start
                taps[place, at * width : (at + 1) * width] = jnp.zeros((64, width), BF16)


def store_taps(side, taps, width, start, j, delta):
    for a in range(3):
        place = pl.ds(pl.multiple_of(64 * turned(side, a, 3), 64), 64)
        at = j + a - start
        taps[place, at * width : (at + 1) * width] = delta


def hand_out(side, mine, theirs, at, value):
    width = value.shape[1]
    left, right = value[:, : width // 2], value[:, width // 2 :]
    mine[at] = jnp.where(side == 0, left, right).astype(BF16)
    theirs[at] = jnp.where(side == 0, right, left).astype(BF16)


def inner_kernel(
    image_p,
    cot_p,
    swapped,
    fwd1,
    fwd2,
    bwd2,
    bias1,
    bias2,
    x3,
    h3,
    d3,
    e3,
    slopes,
    mine,
    theirs,
    grad2,
    grad1,
    image_s,
    cot_s,
    taps2,
    taps1,
):
    side = lax.axis_index("sx")
    half = image_p.shape[0] // 2
    width = 2 * image_p.shape[2]
    last = half + 8
    other = 1 - side
    image_s[side] = image_p[0 : half + 4]
    cot_s[side] = cot_p[0 : half + 2]
    for p in range(half + 4):
        image_s[other, p] = swapped[half + 3 - p]
    cot_s[other] = swapped[half + 4 : 2 * half + 6]
    ones = jnp.ones((16, x3.shape[1]), BF16)
    x3[192:208, :] = ones
    h3[192:208, :] = ones[:, : h3.shape[1]]
    clear(side, taps2, width, 2, half + 2, 2, half)
    clear(side, taps1, width, 3, half + 2, 3, half)
    for p in range(half + 4):
        spread(x3, p, jnp.concatenate([image_s[0, p], image_s[1, p]], axis=1))
    shift1 = jnp.broadcast_to(bias1[:, 0:1], (64, width))
    shift2 = jnp.broadcast_to(bias2[:, 0:1], (64, width))

    def first(e, acc):
        hidden, slope = silu_and_slope(acc + shift1)
        spread(h3, e - 5, hidden.astype(BF16))
        if e < half + 5:
            slopes[e - 5] = slope

    x_rows, h_rows = Rows(x3, width), Rows(h3, width)
    sweep(fwd1, [(x_rows, e - 4) for e in range(4, last)], 4, first)

    def second(e, acc):
        value, slope = silu_and_slope(acc + shift2)
        cot = jnp.concatenate([cot_s[0, e - 4], cot_s[1, e - 4]], axis=1).astype(F32)
        delta = (cot * slope).astype(BF16)
        spread(d3, e - 6, delta)
        if e < half + 4:
            hand_out(side, mine, theirs, e - 6, value)
            store_taps(side, taps2, width, 2, e - 4, delta)

    sweep(fwd2, [(h_rows, e - 5) for e in range(5, last - 1)], 5, second)

    def third(e, acc):
        delta = (acc * slopes[e - 5]).astype(BF16)
        spread(e3, e - 7, delta)
        if e < half + 4:
            store_taps(side, taps1, width, 3, e - 4, delta)

    sweep(bwd2, [(Rows(d3, width), e - 6) for e in range(6, last - 2)], 6, third)

    grad2[...] = lax.dot_general(
        h_rows.span(0, half), taps2[...], CONTRACT, preferred_element_type=F32
    )
    grad1[...] = lax.dot_general(
        x_rows.span(2, half + 1), taps1[...], CONTRACT, preferred_element_type=F32
    )


def outer_kernel(
    edges_own,
    edges_other,
    cot_p,
    swapped,
    fwd1,
    fwd2,
    bwd2,
    bias1,
    bias2,
    x3,
    h3,
    d3,
    slopes,
    grad2,
    grad1,
    e3_b,
    mine,
    theirs,
    grads_own,
    grads_send,
    image_s,
    cot_s,
    x3_b,
    h3_b,
    d3_b,
    slopes_b,
    taps2,
    taps1,
):
    side = lax.axis_index("sx")
    place = lax.axis_index("sy")
    half = cot_p.shape[0] // 2
    width = 2 * cot_p.shape[2]
    other = 1 - side
    outside = place == side * (lax.axis_size("sy") - 1)


    def keep(value):
        return jnp.where(outside, 0.0, value.astype(F32)).astype(BF16)

    for half_of, edges in ((side, edges_own), (other, edges_other)):
        image_s[half_of] = keep(edges[0:4])
        cot_s[half_of, 0] = keep(edges[5])
        cot_s[half_of, 1] = keep(edges[4])
    cot_s[side, 2:4] = cot_p[0:2]
    cot_s[other, 2:4] = swapped[half + 4 : half + 6]
    ones = jnp.ones((16, x3_b.shape[1]), BF16)
    x3_b[192:208, :] = ones
    h3_b[192:208, :] = ones
    clear(side, taps2, width, 0, 4, 0, 2)
    clear(side, taps1, width, 0, 5, 0, 3)
    for e in range(4):
        spread(x3_b, e, jnp.concatenate([image_s[0, e], image_s[1, e]], axis=1))
    shift1 = jnp.broadcast_to(bias1[:, 0:1], (64, width))
    shift2 = jnp.broadcast_to(bias2[:, 0:1], (64, width))

    def first(e, acc):
        hidden, slope = silu_and_slope(acc + shift1)
        if e < 4:
            hidden = jnp.where(outside, 0.0, hidden)
        spread(h3_b, e - 1, hidden.astype(BF16))
        if e >= 3:
            slopes_b[e - 3] = slope

    sweep(fwd1, joined(width, x3_b, 0, x3, 4, 0, 6), 0, first)

    def second(e, acc):
        value, slope = silu_and_slope(acc + shift2)
        cot = jnp.concatenate([cot_s[0, e - 2], cot_s[1, e - 2]], axis=1).astype(F32)
        delta = (cot * slope).astype(BF16)
        spread(d3_b, e - 2, delta)
        if e >= 4:
            hand_out(side, mine, theirs, e - 4, value)
            store_taps(side, taps2, width, 0, e - 4, delta)

    sweep(fwd2, joined(width, h3_b, 1, h3, 5, 1, 6), 1, second)

    def third(e, acc):
        delta = acc * (slopes_b[e - 3] if e < 5 else slopes[e - 5])
        if e < 4:
            delta = jnp.where(outside, 0.0, delta)
        delta = delta.astype(BF16)
        spread(e3_b, e - 3, delta)
        if e >= 4:
            store_taps(side, taps1, width, 0, e - 4, delta)

    sweep(bwd2, joined(width, d3_b, 2, d3, 6, 2, 6), 2, third)

    def product(left, right):
        return lax.dot_general(left, right, CONTRACT, preferred_element_type=F32)

    total2 = (
        grad2[...]
        + product(Rows(h3_b, width).span(2, 4), taps2[:, : 2 * width])
        + product(Rows(h3, width).span(0, 2), taps2[:, 2 * width :])
    )
    total1 = (
        grad1[...]
        + product(Rows(x3_b, width).span(3, 4), taps1[:, :width])
        + product(Rows(x3, width).span(0, 4), taps1[:, width:])
    )
    both = jnp.concatenate([total2[0:192], total1[0:192]], axis=1)
    biases = jnp.concatenate([total2[192:200, 64:128], total1[192:200, 64:128]], axis=1)
    tiles = [
        both[8 * (t // 3) : 8 * (t // 3) + 8, 128 * (t % 3) : 128 * (t % 3) + 128]
        for t in range(72)
    ]
    empty = jnp.zeros((8, 128), F32)
    low, high = tiles[:36] + [biases], tiles[36:] + [empty]
    for t in range(TILES):
        at = slice(128 * t, 128 * t + 128)
        grads_own[:, at] = jnp.where(side == 0, low[t], high[t])
        grads_send[:, at] = jnp.where(side == 0, high[t], low[t])


def pair_kernel(own, received, out):
    out[...] = (own[...] + received[...]).astype(BF16)


def add_kernel(factor, *refs):
    out = refs[-1]
    terms = [ref[...].astype(F32) for ref in refs[:-1]]
    while len(terms) > 1:
        terms = [sum(terms[n + 1 : n + 2], terms[n]) for n in range(0, len(terms), 2)]
    out[...] = (terms[0] * factor).astype(out.dtype)


def passing_add(add, passed, *refs):
    add(*refs[:-1])


def behind_add(add, done, *refs):
    add(*refs)


def input_kernel(held, e3_b, e3, bwd1, mine_a, mine_b, theirs_a, theirs_b, mine, theirs):
    side = lax.axis_index("sx")
    half = mine.shape[0] // 2
    width = 2 * mine.shape[2]
    for whole, inner, outer in ((mine, mine_a, mine_b), (theirs, theirs_a, theirs_b)):
        whole[0:2] = outer[...]
        whole[2:half] = inner[...]

    def emit(e, acc):
        hand_out(side, mine, theirs, half + e - 4, acc)

    sweep(bwd1, joined(width, e3_b, 3, e3, 7, 3, half + 2), 3, emit)


def outputs_kernel(mine, back, out, image_grad, token, natural):
    side = lax.axis_index("sx")
    rows = out.shape[2]
    half = rows // 2
    for slot in range(2):
        for j in range(half):
            natural[slot, turned(side, j, rows)] = mine[slot * half + j]
            natural[slot, turned(side, rows - 1 - j, rows)] = back[slot * half + j]
    for slot, ref in ((0, out), (1, image_grad)):
        ref[0] = jnp.transpose(natural[slot], (1, 0, 2))
    token[...] = jnp.zeros(token.shape, F32)


def grads_kernel(held, swapped, gw1, gb1, gw2, gb2):
    side = lax.axis_index("sx")

    def tile(part, t):
        at = slice(128 * t, 128 * t + 128)
        return jnp.where(side == part, held[:, at], swapped[:, at])

    for block in range(24):
        part, first = block // 12, 3 * (block % 12)
        line = jnp.concatenate([tile(part, first + p) for p in range(3)], axis=1)
        b, i = block // 8, (block % 8) * 8
        for a in range(3):
            gw2[a, b, i : i + 8, :] = line[:, a * 64 : a * 64 + 64]
            gw1[a, b, i : i + 8, :] = line[:, 192 + a * 64 : 256 + a * 64]
    biases = tile(0, 36)
    gb2[...] = biases[0:1, 0:64]
    gb1[...] = biases[0:1, 64:128]


def exchange_stages(places, planes):
    def groups(count, axis):
        bits = [1 << k for k in range(count.bit_length() - 1)]
        pairs = [bits[k : k + 2] for k in range(0, len(bits), 2)]
        return [(axis, [b[0]] + ([b[1], b[0] | b[1]] if len(b) == 2 else [])) for b in pairs]

    rows, slides = groups(places, 0), groups(planes, 1)
    stages = []
    for plan in zip(rows + slides, slides + rows):
        stage = []
        for k in range(3):
            pairs = []
            for s in range(places):
                for x, (axis, masks) in enumerate(plan):
                    for g in range(planes):
                        if k < len(masks):
                            t, h = (s ^ masks[k], g) if axis == 0 else (s, g ^ masks[k])
                            pairs.append(((2 * s + x) * planes + g, (2 * t + x) * planes + h))
            if pairs:
                stage.append(pairs)
        stages.append(stage)
    return stages


def local(image, weight_one, bias_one, weight_two, bias_two, cotangent):
    _, chans, rows, cols = image.shape
    places, planes = lax.axis_size("sy"), lax.axis_size("grp")
    half = rows // 2
    width = 2 * cols
    factor = float(rows * cols * places * planes * lax.axis_size("sx")) ** (-0.5)
    call = functools.partial(pl.pallas_call, compiler_params=PARAMS)

    def rows_of(count):
        return pltpu.VMEM((count, chans, cols), BF16)

    def flat(height, count):
        return pltpu.VMEM((height, count * width), BF16)

    image_p, cot_p, swap, edges, w1, b1, w2, b2 = call(
        pack_kernel,
        out_shape=[
            rows_of(rows),
            rows_of(rows),
            rows_of(2 * half + 6),
            rows_of(6),
            pltpu.VMEM(weight_one.shape, BF16),
            pltpu.VMEM((1, chans), F32),
            pltpu.VMEM(weight_two.shape, BF16),
            pltpu.VMEM((1, chans), F32),
        ],
        in_specs=[pl.BlockSpec(memory_space=pltpu.HBM)] * 6,
        scratch_shapes=[
            pltpu.VMEM((chans, rows, cols), BF16),
            pltpu.VMEM((chans, rows, cols), BF16),
            pltpu.SemaphoreType.DMA((chans // 8 + 4,)),
        ],
        name="pack",
    )(
        *far(image, cotangent, weight_one, bias_one.reshape(1, chans)),
        *far(weight_two, bias_two.reshape(1, chans)),
    )
    swapped = lax.ppermute(swap, "sx", SWAP)
    across = []
    for s in range(places):
        upper, lower = 2 * s + 1, 2 * ((s + 1) % places)
        across += [(upper, lower), (lower, upper)]
    edges_other = lax.ppermute(edges, ("sy", "sx"), across)
    edges_own = lax.ppermute(swapped[half : half + 6], ("sy", "sx"), across)
    fwd1, fwd2, bwd2, bwd1, bias1, bias2 = call(
        weights_kernel,
        out_shape=[pltpu.VMEM((192, 192), BF16)] * 4 + [pltpu.VMEM((64, 128), F32)] * 2,
        cost_estimate=lasting(0.3),
        name="weights",
    )(*near(w1, b1, w2, b2))

    x3, h3, d3, e3, slopes, mine_a, theirs_a, grad2, grad1 = call(
        inner_kernel,
        out_shape=[
            flat(208, half + 4),
            flat(208, half + 2),
            flat(192, half),
            flat(192, half - 2),
            pltpu.VMEM((half, chans, width), F32),
            rows_of(half - 2),
            rows_of(half - 2),
            pltpu.VMEM((208, 192), F32),
            pltpu.VMEM((208, 192), F32),
        ],
        scratch_shapes=[
            pltpu.VMEM((2, half + 4, chans, cols), BF16),
            pltpu.VMEM((2, half + 2, chans, cols), BF16),
            flat(192, half),
            flat(192, half - 1),
        ],
        cost_estimate=lasting(4.0),
        name="inner",
    )(*near(image_p, cot_p, swapped, fwd1, fwd2, bwd2, bias1, bias2))
    half_grads = pltpu.VMEM((8, TILES * 128), F32)
    e3_b, mine_b, theirs_b, grads_own, grads_send = call(
        outer_kernel,
        out_shape=[flat(192, 4), rows_of(2), rows_of(2), half_grads, half_grads],
        scratch_shapes=[
            pltpu.VMEM((2, 4, chans, cols), BF16),
            pltpu.VMEM((2, 4, chans, cols), BF16),
            flat(208, 4),
            flat(208, 4),
            flat(192, 4),
            pltpu.VMEM((2, chans, width), F32),
            flat(192, 4),
            flat(192, 5),
        ],
        cost_estimate=lasting(2.0),
        name="outer",
    )(
        *near(edges_own, edges_other, cot_p, swapped, fwd1, fwd2, bwd2, bias1, bias2),
        *near(x3, h3, d3, slopes, grad2, grad1),
    )
    grads_received = lax.ppermute(grads_send, "sx", SWAP)
    held = call(pair_kernel, out_shape=pltpu.VMEM((8, TILES * 128), BF16), name="pair")(
        *near(grads_own, grads_received)
    )
    stages = exchange_stages(places, planes)
    for n, stage in enumerate(stages):
        final = n == len(stages) - 1
        received = [lax.ppermute(held, ("sy", "sx", "grp"), pairs) for pairs in stage]
        sums = pltpu.VMEM((8, TILES * 128), F32 if final else BF16)
        add = functools.partial(add_kernel, factor if final else 1.0)
        if n == 0:
            mine, theirs = call(
                input_kernel,
                out_shape=[rows_of(rows), rows_of(rows)],
                cost_estimate=lasting(1.0),
                name="input",
            )(*near(held, e3_b, e3, bwd1, mine_a, mine_b, theirs_a, theirs_b))
            held, theirs = call(
                functools.partial(passing_add, add),
                out_shape=[sums, rows_of(rows)],
                input_output_aliases={0: 1},
                name="add",
            )(*near(theirs, held, *received))
            back = lax.ppermute(theirs, "sx", SWAP)
            out, image_grad, done = call(
                outputs_kernel,
                out_shape=[shape_of(image.shape, BF16)] * 2 + [pltpu.VMEM((8, 128), F32)],
                scratch_shapes=[pltpu.VMEM((2, rows, chans, cols), BF16)],
                cost_estimate=lasting(1.3),
                name="outputs",
            )(*near(mine, back))
        elif n == 1:
            held = call(functools.partial(behind_add, add), out_shape=sums, name="add")(
                *near(done, held, *received)
            )
        else:
            held = call(add, out_shape=sums, name="add")(*near(held, *received))
    swapped_sums = lax.ppermute(held, "sx", SWAP)
    weight_shape = shape_of((3, 3, chans, chans), F32)
    bias_shape = shape_of((1, chans), F32)
    gw1, gb1, gw2, gb2 = call(
        grads_kernel,
        out_shape=[weight_shape, bias_shape, weight_shape, bias_shape],
        name="grads",
    )(*near(held, swapped_sums))
    return out, image_grad, gw1, gb1.reshape(chans), gw2, gb2.reshape(chans)


def solution(mesh):
    return jax.shard_map(
        local,
        mesh=mesh,
        in_specs=(P("grp", None, "sy", "sx"), P(), P(), P(), P(), P("grp", None, "sy", "sx")),
        out_specs=(P("grp", None, "sy", "sx"), P("grp", None, "sy", "sx"), P(), P(), P(), P()),
        check_vma=False,
    )
```

```python
import functools

import jax
import jax.numpy as jnp
from jax import lax
from jax.experimental import pallas as pl
from jax.experimental.pallas import tpu as pltpu
from jax.sharding import PartitionSpec as P

BF16 = jnp.bfloat16
F32 = jnp.float32
PARAMS = pltpu.CompilerParams(vmem_limit_bytes=32 * 1024 * 1024)
SWAP = [(0, 1), (1, 0)]
CONTRACT = (((1,), (1,)), ((), ()))
TILES = 73


def shape_of(shape, dtype):
    return jax.ShapeDtypeStruct(shape, dtype)


def near(*arrays):
    return [pltpu.with_memory_space_constraint(array, pltpu.VMEM) for array in arrays]


def far(*arrays):
    return [pltpu.with_memory_space_constraint(array, pltpu.HBM) for array in arrays]


def lasting(micros):
    return pl.CostEstimate(flops=int(micros * 1.1e9), transcendentals=0, bytes_accessed=0)


def turned(side, index, count):
    return index + side * (count - 1 - 2 * index)


def pack_kernel(
    image_ref,
    cot_ref,
    w1,
    b1,
    w2,
    b2,
    image_p,
    cot_p,
    swap,
    edges,
    far_edges,
    w1_v,
    b1_v,
    w2_v,
    b2_v,
    image_v,
    cot_v,
    sems,
):
    side = lax.axis_index("sx")
    rows = image_ref.shape[2]
    half = rows // 2
    jobs, small = [], []
    sources = ((image_ref, image_v, image_p), (cot_ref, cot_v, cot_p))
    for c in range(image_ref.shape[1] // 16):
        chans = slice(16 * c, 16 * c + 16)
        for n, (src, dst, out) in enumerate(sources):
            copy = pltpu.make_async_copy(src.at[0, chans], dst.at[chans], sems.at[2 * c + n])
            copy.start()
            jobs.append((copy, chans, dst, out))
    for n, (src, dst) in enumerate(((w1, w1_v), (b1, b1_v), (w2, w2_v), (b2, b2_v))):
        copy = pltpu.make_async_copy(src, dst, sems.at[len(jobs) + n])
        copy.start()
        small.append(copy)
    for copy, chans, dst, out in jobs:
        copy.wait()
        block = jnp.transpose(dst[chans], (1, 0, 2))
        for h in range(rows):
            out[turned(side, h, rows), chans, :] = block[h]
    swap[0 : half + 4] = image_p[half - 4 : rows]
    for k in range(half + 2):
        swap[half + 4 + k] = cot_p[rows - 1 - k]
    for k in range(4):
        edges[k] = image_p[3 - k]
    edges[4:6] = cot_p[0:2]
    far_edges[0:4] = image_p[rows - 4 : rows]
    far_edges[4] = cot_p[rows - 1]
    far_edges[5] = cot_p[rows - 2]
    for copy in small:
        copy.wait()


def column(row):
    chans = row.shape[1]
    r = lax.broadcasted_iota(jnp.int32, (chans, chans), 0)
    c = lax.broadcasted_iota(jnp.int32, (chans, chans), 1)
    wide = jnp.broadcast_to(row, (chans, chans))
    return jnp.sum(jnp.where(r == c, wide, 0.0), axis=1, keepdims=True)


def weights_kernel(w1, b1, w2, b2, fwd1, fwd2, bwd2, bwd1, bias1, bias2):
    side = lax.axis_index("sx")
    for w, fwd, bwd in ((w1, fwd1, bwd1), (w2, fwd2, bwd2)):
        for a in range(3):
            tap = turned(side, a, 3)
            fwd[a * 64 : a * 64 + 64, :] = jnp.concatenate(
                [jnp.transpose(w[tap, b].astype(F32)) for b in range(3)], axis=1
            ).astype(BF16)
            bwd[a * 64 : a * 64 + 64, :] = jnp.concatenate(
                [w[2 - tap, 2 - b].astype(F32) for b in range(3)], axis=1
            ).astype(BF16)
    bias1[...] = jnp.broadcast_to(column(b1[...]), bias1.shape)
    bias2[...] = jnp.broadcast_to(column(b2[...]), bias2.shape)


def spread(dst, at, row):
    chans, width = row.shape
    zero = jnp.zeros((chans, 1), row.dtype)
    cols = slice(at * width, (at + 1) * width)
    dst[0:chans, cols] = jnp.concatenate([zero, row[:, :-1]], axis=1)
    dst[chans : 2 * chans, cols] = row
    dst[2 * chans : 3 * chans, cols] = jnp.concatenate([row[:, 1:], zero], axis=1)


def sweep(weight_ref, rows, first, emit):
    weight = weight_ref[...]
    upper = lower = None
    for n, (ref, at) in enumerate(rows):
        part = jnp.dot(weight, ref.spread_row(at), preferred_element_type=F32)
        if n >= 2:
            emit(first + n - 1, upper + part[128:192])
        upper = part[64:128] if lower is None else lower + part[64:128]
        lower = part[0:64]


class Rows:
    def __init__(self, ref, width):
        self.ref, self.width = ref, width

    def spread_row(self, at):
        return self.ref[0:192, at * self.width : (at + 1) * self.width]

    def span(self, start, stop):
        return self.ref[:, start * self.width : stop * self.width]


def joined(width, outer, start, inner, split, first, count):
    outer, inner = Rows(outer, width), Rows(inner, width)
    return [
        (outer, e - start) if e < split else (inner, e - split)
        for e in range(first, first + count)
    ]


def silu_and_slope(pre):
    gate = 0.5 + 0.5 * jnp.tanh(0.5 * pre)
    value = pre * gate
    return value, gate + value * (1.0 - gate)


def clear(side, taps, width, start, stop, j0, j1):
    for a in range(3):
        place = pl.ds(pl.multiple_of(64 * turned(side, a, 3), 64), 64)
        for q in range(start, stop):
            if not j0 <= q - a < j1:
                at = q - start
                taps[place, at * width : (at + 1) * width] = jnp.zeros((64, width), BF16)


def store_taps(side, taps, width, start, j, delta):
    for a in range(3):
        place = pl.ds(pl.multiple_of(64 * turned(side, a, 3), 64), 64)
        at = j + a - start
        taps[place, at * width : (at + 1) * width] = delta


def hand_out(side, mine, theirs, at, value):
    width = value.shape[1]
    left, right = value[:, : width // 2], value[:, width // 2 :]
    mine[at] = jnp.where(side == 0, left, right).astype(BF16)
    theirs[at] = jnp.where(side == 0, right, left).astype(BF16)


def inner_kernel(
    image_p,
    cot_p,
    swapped,
    fwd1,
    fwd2,
    bwd2,
    bias1,
    bias2,
    x3,
    h3,
    d3,
    e3,
    slopes,
    mine,
    theirs,
    grad2,
    grad1,
    image_s,
    cot_s,
    taps2,
    taps1,
):
    side = lax.axis_index("sx")
    half = image_p.shape[0] // 2
    width = 2 * image_p.shape[2]
    last = half + 8
    other = 1 - side
    image_s[side] = image_p[0 : half + 4]
    cot_s[side] = cot_p[0 : half + 2]
    for p in range(half + 4):
        image_s[other, p] = swapped[half + 3 - p]
    cot_s[other] = swapped[half + 4 : 2 * half + 6]
    ones = jnp.ones((16, x3.shape[1]), BF16)
    x3[192:208, :] = ones
    h3[192:208, :] = ones[:, : h3.shape[1]]
    clear(side, taps2, width, 2, half + 2, 2, half)
    clear(side, taps1, width, 3, half + 2, 3, half)
    for p in range(half + 4):
        spread(x3, p, jnp.concatenate([image_s[0, p], image_s[1, p]], axis=1))
    shift1 = jnp.broadcast_to(bias1[:, 0:1], (64, width))
    shift2 = jnp.broadcast_to(bias2[:, 0:1], (64, width))

    def first(e, acc):
        hidden, slope = silu_and_slope(acc + shift1)
        spread(h3, e - 5, hidden.astype(BF16))
        if e < half + 5:
            slopes[e - 5] = slope

    x_rows, h_rows = Rows(x3, width), Rows(h3, width)
    sweep(fwd1, [(x_rows, e - 4) for e in range(4, last)], 4, first)

    def second(e, acc):
        value, slope = silu_and_slope(acc + shift2)
        cot = jnp.concatenate([cot_s[0, e - 4], cot_s[1, e - 4]], axis=1).astype(F32)
        delta = (cot * slope).astype(BF16)
        spread(d3, e - 6, delta)
        if e < half + 4:
            hand_out(side, mine, theirs, e - 6, value)
            store_taps(side, taps2, width, 2, e - 4, delta)

    sweep(fwd2, [(h_rows, e - 5) for e in range(5, last - 1)], 5, second)

    def third(e, acc):
        delta = (acc * slopes[e - 5]).astype(BF16)
        spread(e3, e - 7, delta)
        if e < half + 4:
            store_taps(side, taps1, width, 3, e - 4, delta)

    sweep(bwd2, [(Rows(d3, width), e - 6) for e in range(6, last - 2)], 6, third)

    grad2[...] = lax.dot_general(
        h_rows.span(0, half), taps2[...], CONTRACT, preferred_element_type=F32
    )
    grad1[...] = lax.dot_general(
        x_rows.span(2, half + 1), taps1[...], CONTRACT, preferred_element_type=F32
    )


def outer_kernel(
    edges_own,
    edges_other,
    cot_p,
    swapped,
    fwd1,
    fwd2,
    bwd2,
    bias1,
    bias2,
    x3,
    h3,
    d3,
    slopes,
    grad2,
    grad1,
    e3_b,
    mine,
    theirs,
    grads,
    image_s,
    cot_s,
    x3_b,
    h3_b,
    d3_b,
    slopes_b,
    taps2,
    taps1,
):
    side = lax.axis_index("sx")
    place = lax.axis_index("sy")
    half = cot_p.shape[0] // 2
    width = 2 * cot_p.shape[2]
    other = 1 - side
    outside = place == side * (lax.axis_size("sy") - 1)


    def keep(value):
        return jnp.where(outside, 0.0, value.astype(F32)).astype(BF16)

    for half_of, edges in ((side, edges_own), (other, edges_other)):
        image_s[half_of] = keep(edges[0:4])
        cot_s[half_of, 0] = keep(edges[5])
        cot_s[half_of, 1] = keep(edges[4])
    cot_s[side, 2:4] = cot_p[0:2]
    cot_s[other, 2:4] = swapped[half + 4 : half + 6]
    ones = jnp.ones((16, x3_b.shape[1]), BF16)
    x3_b[192:208, :] = ones
    h3_b[192:208, :] = ones
    clear(side, taps2, width, 0, 4, 0, 2)
    clear(side, taps1, width, 0, 5, 0, 3)
    for e in range(4):
        spread(x3_b, e, jnp.concatenate([image_s[0, e], image_s[1, e]], axis=1))
    shift1 = jnp.broadcast_to(bias1[:, 0:1], (64, width))
    shift2 = jnp.broadcast_to(bias2[:, 0:1], (64, width))

    def first(e, acc):
        hidden, slope = silu_and_slope(acc + shift1)
        if e < 4:
            hidden = jnp.where(outside, 0.0, hidden)
        spread(h3_b, e - 1, hidden.astype(BF16))
        if e >= 3:
            slopes_b[e - 3] = slope

    sweep(fwd1, joined(width, x3_b, 0, x3, 4, 0, 6), 0, first)

    def second(e, acc):
        value, slope = silu_and_slope(acc + shift2)
        cot = jnp.concatenate([cot_s[0, e - 2], cot_s[1, e - 2]], axis=1).astype(F32)
        delta = (cot * slope).astype(BF16)
        spread(d3_b, e - 2, delta)
        if e >= 4:
            hand_out(side, mine, theirs, e - 4, value)
            store_taps(side, taps2, width, 0, e - 4, delta)

    sweep(fwd2, joined(width, h3_b, 1, h3, 5, 1, 6), 1, second)

    def third(e, acc):
        delta = acc * (slopes_b[e - 3] if e < 5 else slopes[e - 5])
        if e < 4:
            delta = jnp.where(outside, 0.0, delta)
        delta = delta.astype(BF16)
        spread(e3_b, e - 3, delta)
        if e >= 4:
            store_taps(side, taps1, width, 0, e - 4, delta)

    sweep(bwd2, joined(width, d3_b, 2, d3, 6, 2, 6), 2, third)

    def product(left, right):
        return lax.dot_general(left, right, CONTRACT, preferred_element_type=F32)

    total2 = (
        grad2[...]
        + product(Rows(h3_b, width).span(2, 4), taps2[:, : 2 * width])
        + product(Rows(h3, width).span(0, 2), taps2[:, 2 * width :])
    )
    total1 = (
        grad1[...]
        + product(Rows(x3_b, width).span(3, 4), taps1[:, :width])
        + product(Rows(x3, width).span(0, 4), taps1[:, width:])
    )
    both = jnp.concatenate([total2[0:192], total1[0:192]], axis=1)
    biases = jnp.concatenate([total2[192:200, 64:128], total1[192:200, 64:128]], axis=1)
    tiles = [
        both[8 * (t // 3) : 8 * (t // 3) + 8, 128 * (t % 3) : 128 * (t % 3) + 128]
        for t in range(72)
    ]
    for t, tile in enumerate(tiles + [biases]):
        grads[:, 128 * t : 128 * t + 128] = tile


def pair_kernel(own, received, out):
    out[...] = (own[...] + received[...]).astype(BF16)


def add_kernel(factor, *refs):
    out = refs[-1]
    terms = [ref[...].astype(F32) for ref in refs[:-1]]
    while len(terms) > 1:
        terms = [sum(terms[n + 1 : n + 2], terms[n]) for n in range(0, len(terms), 2)]
    out[...] = (terms[0] * factor).astype(out.dtype)


def passing_add(add, passed, *refs):
    add(*refs[:-1])


def behind_add(add, done, *refs):
    add(*refs)


def input_kernel(held, e3_b, e3, bwd1, mine_a, mine_b, theirs_a, theirs_b, mine, theirs):
    side = lax.axis_index("sx")
    half = mine.shape[0] // 2
    width = 2 * mine.shape[2]
    for whole, inner, outer in ((mine, mine_a, mine_b), (theirs, theirs_a, theirs_b)):
        whole[0:2] = outer[...]
        whole[2:half] = inner[...]

    def emit(e, acc):
        hand_out(side, mine, theirs, half + e - 4, acc)

    sweep(bwd1, joined(width, e3_b, 3, e3, 7, 3, half + 2), 3, emit)


def outputs_kernel(mine, back, out, image_grad, token, natural):
    side = lax.axis_index("sx")
    rows = out.shape[2]
    half = rows // 2
    for slot in range(2):
        for j in range(half):
            natural[slot, turned(side, j, rows)] = mine[slot * half + j]
            natural[slot, turned(side, rows - 1 - j, rows)] = back[slot * half + j]
    for slot, ref in ((0, out), (1, image_grad)):
        ref[0] = jnp.transpose(natural[slot], (1, 0, 2))
    token[...] = jnp.zeros(token.shape, F32)


def grads_kernel(held, swapped, gw1, gb1, gw2, gb2):
    side = lax.axis_index("sx")

    for block in range(24):
        at = slice(384 * block, 384 * block + 384)
        line = jnp.where(side == 1, held[:, at], swapped[:, at])
        b, i = block // 8, (block % 8) * 8
        for a in range(3):
            gw2[a, b, i : i + 8, :] = line[:, a * 64 : a * 64 + 64]
            gw1[a, b, i : i + 8, :] = line[:, 192 + a * 64 : 256 + a * 64]
    at = slice(72 * 128, 73 * 128)
    biases = jnp.where(side == 1, held[:, at], swapped[:, at])
    gb2[...] = biases[0:1, 0:64]
    gb1[...] = biases[0:1, 64:128]


def exchange_stages(places, planes):
    def groups(count, axis):
        bits = [1 << k for k in range(count.bit_length() - 1)]
        pairs = [bits[k : k + 2] for k in range(0, len(bits), 2)]
        return [(axis, [b[0]] + ([b[1], b[0] | b[1]] if len(b) == 2 else [])) for b in pairs]

    stages = []
    for axis, masks in groups(planes, 1) + groups(places, 0):
        stage = []
        for mask in masks:
            pairs = []
            for s in range(places):
                for g in range(planes):
                    t, h = (s ^ mask, g) if axis == 0 else (s, g ^ mask)
                    pairs.append((2 * s * planes + g, 2 * s * planes + g))
                    pairs.append(((2 * s + 1) * planes + g, (2 * t + 1) * planes + h))
            stage.append(pairs)
        stages.append(stage)
    return stages


def local(image, weight_one, bias_one, weight_two, bias_two, cotangent):
    _, chans, rows, cols = image.shape
    places, planes = lax.axis_size("sy"), lax.axis_size("grp")
    half = rows // 2
    width = 2 * cols
    factor = float(rows * cols * places * planes * lax.axis_size("sx")) ** (-0.5)
    call = functools.partial(pl.pallas_call, compiler_params=PARAMS)

    def rows_of(count):
        return pltpu.VMEM((count, chans, cols), BF16)

    def flat(height, count):
        return pltpu.VMEM((height, count * width), BF16)

    image_p, cot_p, swap, edges, far_edges, w1, b1, w2, b2 = call(
        pack_kernel,
        out_shape=[
            rows_of(rows),
            rows_of(rows),
            rows_of(2 * half + 6),
            rows_of(6),
            rows_of(6),
            pltpu.VMEM(weight_one.shape, BF16),
            pltpu.VMEM((1, chans), F32),
            pltpu.VMEM(weight_two.shape, BF16),
            pltpu.VMEM((1, chans), F32),
        ],
        in_specs=[pl.BlockSpec(memory_space=pltpu.HBM)] * 6,
        scratch_shapes=[
            pltpu.VMEM((chans, rows, cols), BF16),
            pltpu.VMEM((chans, rows, cols), BF16),
            pltpu.SemaphoreType.DMA((chans // 8 + 4,)),
        ],
        name="pack",
    )(
        *far(image, cotangent, weight_one, bias_one.reshape(1, chans)),
        *far(weight_two, bias_two.reshape(1, chans)),
    )
    swapped = lax.ppermute(swap, "sx", SWAP)
    across = []
    for s in range(places):
        upper, lower = 2 * s + 1, 2 * ((s + 1) % places)
        across += [(upper, lower), (lower, upper)]
    edges_other = lax.ppermute(edges, ("sy", "sx"), across)
    along = []
    for s in range(places):
        t = (s + 1) % places
        along += [(2 * s, 2 * t), (2 * t + 1, 2 * s + 1)]
    edges_own = lax.ppermute(far_edges, ("sy", "sx"), along)
    fwd1, fwd2, bwd2, bwd1, bias1, bias2 = call(
        weights_kernel,
        out_shape=[pltpu.VMEM((192, 192), BF16)] * 4 + [pltpu.VMEM((64, 128), F32)] * 2,
        cost_estimate=lasting(0.3),
        name="weights",
    )(*near(w1, b1, w2, b2))

    x3, h3, d3, e3, slopes, mine_a, theirs_a, grad2, grad1 = call(
        inner_kernel,
        out_shape=[
            flat(208, half + 4),
            flat(208, half + 2),
            flat(192, half),
            flat(192, half - 2),
            pltpu.VMEM((half, chans, width), F32),
            rows_of(half - 2),
            rows_of(half - 2),
            pltpu.VMEM((208, 192), F32),
            pltpu.VMEM((208, 192), F32),
        ],
        scratch_shapes=[
            pltpu.VMEM((2, half + 4, chans, cols), BF16),
            pltpu.VMEM((2, half + 2, chans, cols), BF16),
            flat(192, half),
            flat(192, half - 1),
        ],
        cost_estimate=lasting(4.0),
        name="inner",
    )(*near(image_p, cot_p, swapped, fwd1, fwd2, bwd2, bias1, bias2))
    whole_grads = pltpu.VMEM((8, TILES * 128), F32)
    e3_b, mine_b, theirs_b, grads = call(
        outer_kernel,
        out_shape=[flat(192, 4), rows_of(2), rows_of(2), whole_grads],
        scratch_shapes=[
            pltpu.VMEM((2, 4, chans, cols), BF16),
            pltpu.VMEM((2, 4, chans, cols), BF16),
            flat(208, 4),
            flat(208, 4),
            flat(192, 4),
            pltpu.VMEM((2, chans, width), F32),
            flat(192, 4),
            flat(192, 5),
        ],
        cost_estimate=lasting(2.0),
        name="outer",
    )(
        *near(edges_own, edges_other, cot_p, swapped, fwd1, fwd2, bwd2, bias1, bias2),
        *near(x3, h3, d3, slopes, grad2, grad1),
    )
    grads_received = lax.ppermute(grads, "sx", SWAP)
    held = call(pair_kernel, out_shape=pltpu.VMEM((8, TILES * 128), BF16), name="pair")(
        *near(grads, grads_received)
    )
    stages = exchange_stages(places, planes)
    for n, stage in enumerate(stages):
        final = n == len(stages) - 1
        received = [lax.ppermute(held, ("sy", "sx", "grp"), pairs) for pairs in stage]
        sums = pltpu.VMEM((8, TILES * 128), F32 if final else BF16)
        add = functools.partial(add_kernel, factor if final else 1.0)
        if n == 0:
            mine, theirs = call(
                input_kernel,
                out_shape=[rows_of(rows), rows_of(rows)],
                cost_estimate=lasting(1.0),
                name="input",
            )(*near(held, e3_b, e3, bwd1, mine_a, mine_b, theirs_a, theirs_b))
            held, theirs = call(
                functools.partial(passing_add, add),
                out_shape=[sums, rows_of(rows)],
                input_output_aliases={0: 1},
                name="add",
            )(*near(theirs, held, *received))
            back = lax.ppermute(theirs, "sx", SWAP)
            out, image_grad, done = call(
                outputs_kernel,
                out_shape=[shape_of(image.shape, BF16)] * 2 + [pltpu.VMEM((8, 128), F32)],
                scratch_shapes=[pltpu.VMEM((2, rows, chans, cols), BF16)],
                cost_estimate=lasting(1.3),
                name="outputs",
            )(*near(mine, back))
        elif n == 1:
            held = call(functools.partial(behind_add, add), out_shape=sums, name="add")(
                *near(done, held, *received)
            )
        else:
            held = call(add, out_shape=sums, name="add")(*near(held, *received))
    swapped_sums = lax.ppermute(held, "sx", SWAP)
    weight_shape = shape_of((3, 3, chans, chans), F32)
    bias_shape = shape_of((1, chans), F32)
    gw1, gb1, gw2, gb2 = call(
        grads_kernel,
        out_shape=[weight_shape, bias_shape, weight_shape, bias_shape],
        name="grads",
    )(*near(held, swapped_sums))
    return out, image_grad, gw1, gb1.reshape(chans), gw2, gb2.reshape(chans)


def solution(mesh):
    return jax.shard_map(
        local,
        mesh=mesh,
        in_specs=(P("grp", None, "sy", "sx"), P(), P(), P(), P(), P("grp", None, "sy", "sx")),
        out_specs=(P("grp", None, "sy", "sx"), P("grp", None, "sy", "sx"), P(), P(), P(), P()),
        check_vma=False,
    )
```

```python
import functools

import jax
import jax.numpy as jnp
from jax import lax
from jax.experimental import pallas as pl
from jax.experimental.pallas import tpu as pltpu
from jax.sharding import PartitionSpec as P

BF16 = jnp.bfloat16
F32 = jnp.float32
PARAMS = pltpu.CompilerParams(vmem_limit_bytes=32 * 1024 * 1024)
SWAP = [(0, 1), (1, 0)]
CONTRACT = (((1,), (1,)), ((), ()))
TILES = 37


def shape_of(shape, dtype):
    return jax.ShapeDtypeStruct(shape, dtype)


def near(*arrays):
    return [pltpu.with_memory_space_constraint(array, pltpu.VMEM) for array in arrays]


def far(*arrays):
    return [pltpu.with_memory_space_constraint(array, pltpu.HBM) for array in arrays]


def lasting(micros):
    return pl.CostEstimate(flops=int(micros * 1.1e9), transcendentals=0, bytes_accessed=0)


def turned(side, index, count):
    return index + side * (count - 1 - 2 * index)


def pack_kernel(
    image_ref,
    cot_ref,
    w1,
    b1,
    w2,
    b2,
    image_p,
    cot_p,
    swap,
    edges,
    w1_v,
    b1_v,
    w2_v,
    b2_v,
    image_v,
    cot_v,
    wides,
    sems,
):
    side = lax.axis_index("sx")
    rows = image_ref.shape[2]
    half = rows // 2
    jobs, small = [], []
    sources = ((image_ref, image_v, image_p), (cot_ref, cot_v, cot_p))
    for c in range(image_ref.shape[1] // 16):
        chans = slice(16 * c, 16 * c + 16)
        for n, (src, dst, out) in enumerate(sources):
            copy = pltpu.make_async_copy(src.at[0, chans], dst.at[chans], sems.at[2 * c + n])
            copy.start()
            jobs.append((copy, chans, dst, out))
    for n, (src, dst) in enumerate(((w1, w1_v), (b1, b1_v), (w2, w2_v), (b2, b2_v))):
        copy = pltpu.make_async_copy(src, dst, sems.at[len(jobs) + n])
        copy.start()
        small.append(copy)
    for n, (copy, chans, dst, out) in enumerate(jobs):
        copy.wait()
        wide = wides.at[n]
        wide[...] = dst[chans].astype(F32).reshape(wide.shape)
        for h in range(rows):
            row = wide[pl.ds(h, 16, stride=rows), :]
            out[turned(side, h, rows), chans, :] = row.astype(BF16)
    swap[0 : half + 4] = image_p[half - 4 : rows]
    for k in range(half + 2):
        swap[half + 4 + k] = cot_p[rows - 1 - k]
    for k in range(4):
        edges[k] = image_p[3 - k]
    edges[4:6] = cot_p[0:2]
    for copy in small:
        copy.wait()


def column(row):
    chans = row.shape[1]
    r = lax.broadcasted_iota(jnp.int32, (chans, chans), 0)
    c = lax.broadcasted_iota(jnp.int32, (chans, chans), 1)
    wide = jnp.broadcast_to(row, (chans, chans))
    return jnp.sum(jnp.where(r == c, wide, 0.0), axis=1, keepdims=True)


def weights_kernel(w1, b1, w2, b2, fwd1, fwd2, bwd2, bwd1, bias1, bias2):
    side = lax.axis_index("sx")
    for w, fwd, bwd in ((w1, fwd1, bwd1), (w2, fwd2, bwd2)):
        for a in range(3):
            tap = turned(side, a, 3)
            fwd[a * 64 : a * 64 + 64, :] = jnp.concatenate(
                [jnp.transpose(w[tap, b].astype(F32)) for b in range(3)], axis=1
            ).astype(BF16)
            bwd[a * 64 : a * 64 + 64, :] = jnp.concatenate(
                [w[2 - tap, 2 - b].astype(F32) for b in range(3)], axis=1
            ).astype(BF16)
    bias1[...] = jnp.broadcast_to(column(b1[...]), bias1.shape)
    bias2[...] = jnp.broadcast_to(column(b2[...]), bias2.shape)


def spread(dst, at, row):
    chans, width = row.shape
    zero = jnp.zeros((chans, 1), row.dtype)
    cols = slice(at * width, (at + 1) * width)
    dst[0:chans, cols] = jnp.concatenate([zero, row[:, :-1]], axis=1)
    dst[chans : 2 * chans, cols] = row
    dst[2 * chans : 3 * chans, cols] = jnp.concatenate([row[:, 1:], zero], axis=1)


def sweep(weight_ref, rows, first, emit):
    weight = weight_ref[...]
    upper = lower = None
    for n, (ref, at) in enumerate(rows):
        part = jnp.dot(weight, ref.spread_row(at), preferred_element_type=F32)
        if n >= 2:
            emit(first + n - 1, upper + part[128:192])
        upper = part[64:128] if lower is None else lower + part[64:128]
        lower = part[0:64]


class Rows:
    def __init__(self, ref, width):
        self.ref, self.width = ref, width

    def spread_row(self, at):
        return self.ref[0:192, at * self.width : (at + 1) * self.width]

    def span(self, start, stop):
        return self.ref[:, start * self.width : stop * self.width]


def joined(width, outer, start, inner, split, first, count):
    outer, inner = Rows(outer, width), Rows(inner, width)
    return [
        (outer, e - start) if e < split else (inner, e - split)
        for e in range(first, first + count)
    ]


def silu_and_slope(pre):
    gate = 0.5 + 0.5 * jnp.tanh(0.5 * pre)
    value = pre * gate
    return value, gate + value * (1.0 - gate)


def clear(side, taps, width, start, stop, j0, j1):
    for a in range(3):
        place = pl.ds(pl.multiple_of(64 * turned(side, a, 3), 64), 64)
        for q in range(start, stop):
            if not j0 <= q - a < j1:
                at = q - start
                taps[place, at * width : (at + 1) * width] = jnp.zeros((64, width), BF16)


def store_taps(side, taps, width, start, j, delta):
    for a in range(3):
        place = pl.ds(pl.multiple_of(64 * turned(side, a, 3), 64), 64)
        at = j + a - start
        taps[place, at * width : (at + 1) * width] = delta


def hand_out(side, mine, theirs, at, value):
    width = value.shape[1]
    left, right = value[:, : width // 2], value[:, width // 2 :]
    mine[at] = jnp.where(side == 0, left, right).astype(BF16)
    theirs[at] = jnp.where(side == 0, right, left).astype(BF16)


def inner_kernel(
    image_p,
    cot_p,
    swapped,
    fwd1,
    fwd2,
    bwd2,
    bias1,
    bias2,
    x3,
    h3,
    d3,
    e3,
    slopes,
    mine,
    theirs,
    grad2,
    grad1,
    image_s,
    cot_s,
    taps2,
    taps1,
):
    side = lax.axis_index("sx")
    half = image_p.shape[0] // 2
    width = 2 * image_p.shape[2]
    last = half + 8
    other = 1 - side
    image_s[side] = image_p[0 : half + 4]
    cot_s[side] = cot_p[0 : half + 2]
    for p in range(half + 4):
        image_s[other, p] = swapped[half + 3 - p]
    cot_s[other] = swapped[half + 4 : 2 * half + 6]
    ones = jnp.ones((16, x3.shape[1]), BF16)
    x3[192:208, :] = ones
    h3[192:208, :] = ones[:, : h3.shape[1]]
    clear(side, taps2, width, 2, half + 2, 2, half)
    clear(side, taps1, width, 3, half + 2, 3, half)
    for p in range(half + 4):
        spread(x3, p, jnp.concatenate([image_s[0, p], image_s[1, p]], axis=1))
    shift1 = jnp.broadcast_to(bias1[:, 0:1], (64, width))
    shift2 = jnp.broadcast_to(bias2[:, 0:1], (64, width))

    def first(e, acc):
        hidden, slope = silu_and_slope(acc + shift1)
        spread(h3, e - 5, hidden.astype(BF16))
        if e < half + 5:
            slopes[e - 5] = slope

    x_rows, h_rows = Rows(x3, width), Rows(h3, width)
    sweep(fwd1, [(x_rows, e - 4) for e in range(4, last)], 4, first)

    def second(e, acc):
        value, slope = silu_and_slope(acc + shift2)
        cot = jnp.concatenate([cot_s[0, e - 4], cot_s[1, e - 4]], axis=1).astype(F32)
        delta = (cot * slope).astype(BF16)
        spread(d3, e - 6, delta)
        if e < half + 4:
            hand_out(side, mine, theirs, e - 6, value)
            store_taps(side, taps2, width, 2, e - 4, delta)

    sweep(fwd2, [(h_rows, e - 5) for e in range(5, last - 1)], 5, second)

    def third(e, acc):
        delta = (acc * slopes[e - 5]).astype(BF16)
        spread(e3, e - 7, delta)
        if e < half + 4:
            store_taps(side, taps1, width, 3, e - 4, delta)

    sweep(bwd2, [(Rows(d3, width), e - 6) for e in range(6, last - 2)], 6, third)

    grad2[...] = lax.dot_general(
        h_rows.span(0, half), taps2[...], CONTRACT, preferred_element_type=F32
    )
    grad1[...] = lax.dot_general(
        x_rows.span(2, half + 1), taps1[...], CONTRACT, preferred_element_type=F32
    )


def outer_kernel(
    edges_own,
    edges_other,
    cot_p,
    swapped,
    fwd1,
    fwd2,
    bwd2,
    bias1,
    bias2,
    x3,
    h3,
    d3,
    slopes,
    grad2,
    grad1,
    e3_b,
    mine,
    theirs,
    grads_own,
    grads_send,
    image_s,
    cot_s,
    x3_b,
    h3_b,
    d3_b,
    slopes_b,
    taps2,
    taps1,
):
    side = lax.axis_index("sx")
    place = lax.axis_index("sy")
    half = cot_p.shape[0] // 2
    width = 2 * cot_p.shape[2]
    other = 1 - side
    outside = place == side * (lax.axis_size("sy") - 1)


    def keep(value):
        return jnp.where(outside, 0.0, value.astype(F32)).astype(BF16)

    for half_of, edges in ((side, edges_own), (other, edges_other)):
        image_s[half_of] = keep(edges[0:4])
        cot_s[half_of, 0] = keep(edges[5])
        cot_s[half_of, 1] = keep(edges[4])
    cot_s[side, 2:4] = cot_p[0:2]
    cot_s[other, 2:4] = swapped[half + 4 : half + 6]
    ones = jnp.ones((16, x3_b.shape[1]), BF16)
    x3_b[192:208, :] = ones
    h3_b[192:208, :] = ones
    clear(side, taps2, width, 0, 4, 0, 2)
    clear(side, taps1, width, 0, 5, 0, 3)
    for e in range(4):
        spread(x3_b, e, jnp.concatenate([image_s[0, e], image_s[1, e]], axis=1))
    shift1 = jnp.broadcast_to(bias1[:, 0:1], (64, width))
    shift2 = jnp.broadcast_to(bias2[:, 0:1], (64, width))

    def first(e, acc):
        hidden, slope = silu_and_slope(acc + shift1)
        if e < 4:
            hidden = jnp.where(outside, 0.0, hidden)
        spread(h3_b, e - 1, hidden.astype(BF16))
        if e >= 3:
            slopes_b[e - 3] = slope

    sweep(fwd1, joined(width, x3_b, 0, x3, 4, 0, 6), 0, first)

    def second(e, acc):
        value, slope = silu_and_slope(acc + shift2)
        cot = jnp.concatenate([cot_s[0, e - 2], cot_s[1, e - 2]], axis=1).astype(F32)
        delta = (cot * slope).astype(BF16)
        spread(d3_b, e - 2, delta)
        if e >= 4:
            hand_out(side, mine, theirs, e - 4, value)
            store_taps(side, taps2, width, 0, e - 4, delta)

    sweep(fwd2, joined(width, h3_b, 1, h3, 5, 1, 6), 1, second)

    def third(e, acc):
        delta = acc * (slopes_b[e - 3] if e < 5 else slopes[e - 5])
        if e < 4:
            delta = jnp.where(outside, 0.0, delta)
        delta = delta.astype(BF16)
        spread(e3_b, e - 3, delta)
        if e >= 4:
            store_taps(side, taps1, width, 0, e - 4, delta)

    sweep(bwd2, joined(width, d3_b, 2, d3, 6, 2, 6), 2, third)

    def product(left, right):
        return lax.dot_general(left, right, CONTRACT, preferred_element_type=F32)

    total2 = (
        grad2[...]
        + product(Rows(h3_b, width).span(2, 4), taps2[:, : 2 * width])
        + product(Rows(h3, width).span(0, 2), taps2[:, 2 * width :])
    )
    total1 = (
        grad1[...]
        + product(Rows(x3_b, width).span(3, 4), taps1[:, :width])
        + product(Rows(x3, width).span(0, 4), taps1[:, width:])
    )
    both = jnp.concatenate([total2[0:192], total1[0:192]], axis=1)
    biases = jnp.concatenate([total2[192:200, 64:128], total1[192:200, 64:128]], axis=1)
    tiles = [
        both[8 * (t // 3) : 8 * (t // 3) + 8, 128 * (t % 3) : 128 * (t % 3) + 128]
        for t in range(72)
    ]
    empty = jnp.zeros((8, 128), F32)
    low, high = tiles[:36] + [biases], tiles[36:] + [empty]
    for t in range(TILES):
        at = slice(128 * t, 128 * t + 128)
        grads_own[:, at] = jnp.where(side == 0, low[t], high[t])
        grads_send[:, at] = jnp.where(side == 0, high[t], low[t])


def pair_kernel(own, received, out):
    out[...] = (own[...] + received[...]).astype(BF16)


def add_kernel(factor, *refs):
    out = refs[-1]
    terms = [ref[...].astype(F32) for ref in refs[:-1]]
    while len(terms) > 1:
        terms = [sum(terms[n + 1 : n + 2], terms[n]) for n in range(0, len(terms), 2)]
    out[...] = (terms[0] * factor).astype(out.dtype)


def passing_add(add, passed, *refs):
    add(*refs[:-1])


def behind_add(add, done, *refs):
    add(*refs)


def input_kernel(held, e3_b, e3, bwd1, mine_a, mine_b, theirs_a, theirs_b, mine, theirs):
    side = lax.axis_index("sx")
    half = mine.shape[0] // 2
    width = 2 * mine.shape[2]
    for whole, inner, outer in ((mine, mine_a, mine_b), (theirs, theirs_a, theirs_b)):
        whole[0:2] = outer[...]
        whole[2:half] = inner[...]

    def emit(e, acc):
        hand_out(side, mine, theirs, half + e - 4, acc)

    sweep(bwd1, joined(width, e3_b, 3, e3, 7, 3, half + 2), 3, emit)


def outputs_kernel(mine, back, out, image_grad, token, natural):
    side = lax.axis_index("sx")
    rows = out.shape[2]
    half = rows // 2
    for slot in range(2):
        for j in range(half):
            natural[slot, turned(side, j, rows)] = mine[slot * half + j]
            natural[slot, turned(side, rows - 1 - j, rows)] = back[slot * half + j]
    for slot, ref in ((0, out), (1, image_grad)):
        ref[0] = jnp.transpose(natural[slot], (1, 0, 2))
    token[...] = jnp.zeros(token.shape, F32)


def grads_kernel(held, swapped, gw1, gb1, gw2, gb2):
    side = lax.axis_index("sx")

    def tile(part, t):
        at = slice(128 * t, 128 * t + 128)
        return jnp.where(side == part, held[:, at], swapped[:, at])

    for block in range(24):
        part, first = block // 12, 3 * (block % 12)
        line = jnp.concatenate([tile(part, first + p) for p in range(3)], axis=1)
        b, i = block // 8, (block % 8) * 8
        for a in range(3):
            gw2[a, b, i : i + 8, :] = line[:, a * 64 : a * 64 + 64]
            gw1[a, b, i : i + 8, :] = line[:, 192 + a * 64 : 256 + a * 64]
    biases = tile(0, 36)
    gb2[...] = biases[0:1, 0:64]
    gb1[...] = biases[0:1, 64:128]


def exchange_stages(places, planes):
    def groups(count, axis):
        bits = [1 << k for k in range(count.bit_length() - 1)]
        pairs = [bits[k : k + 2] for k in range(0, len(bits), 2)]
        return [(axis, [b[0]] + ([b[1], b[0] | b[1]] if len(b) == 2 else [])) for b in pairs]

    rows, slides = groups(places, 0), groups(planes, 1)
    stages = []
    for plan in zip(rows + slides, slides + rows):
        stage = []
        for k in range(3):
            pairs = []
            for s in range(places):
                for x, (axis, masks) in enumerate(plan):
                    for g in range(planes):
                        if k < len(masks):
                            t, h = (s ^ masks[k], g) if axis == 0 else (s, g ^ masks[k])
                            pairs.append(((2 * s + x) * planes + g, (2 * t + x) * planes + h))
            if pairs:
                stage.append(pairs)
        stages.append(stage)
    return stages


def local(image, weight_one, bias_one, weight_two, bias_two, cotangent):
    _, chans, rows, cols = image.shape
    places, planes = lax.axis_size("sy"), lax.axis_size("grp")
    half = rows // 2
    width = 2 * cols
    factor = float(rows * cols * places * planes * lax.axis_size("sx")) ** (-0.5)
    call = functools.partial(pl.pallas_call, compiler_params=PARAMS)

    def rows_of(count):
        return pltpu.VMEM((count, chans, cols), BF16)

    def flat(height, count):
        return pltpu.VMEM((height, count * width), BF16)

    image_p, cot_p, swap, edges, w1, b1, w2, b2 = call(
        pack_kernel,
        out_shape=[
            rows_of(rows),
            rows_of(rows),
            rows_of(2 * half + 6),
            rows_of(6),
            pltpu.VMEM(weight_one.shape, BF16),
            pltpu.VMEM((1, chans), F32),
            pltpu.VMEM(weight_two.shape, BF16),
            pltpu.VMEM((1, chans), F32),
        ],
        in_specs=[pl.BlockSpec(memory_space=pltpu.HBM)] * 6,
        scratch_shapes=[
            pltpu.VMEM((chans, rows, cols), BF16),
            pltpu.VMEM((chans, rows, cols), BF16),
            pltpu.VMEM((chans // 8, 16 * rows, cols), F32),
            pltpu.SemaphoreType.DMA((chans // 8 + 4,)),
        ],
        name="pack",
    )(
        *far(image, cotangent, weight_one, bias_one.reshape(1, chans)),
        *far(weight_two, bias_two.reshape(1, chans)),
    )
    swapped = lax.ppermute(swap, "sx", SWAP)
    across = []
    for s in range(places):
        for g in range(planes):
            lower, upper = 2 * s * planes + g, (2 * s + 1) * planes + g
            across.append((lower, lower - planes if s > 0 else lower ^ 1))
            across.append((upper, upper + planes if s < places - 1 else upper ^ 1))
    axes = ("sy", "sx", "grp")
    edges_other = lax.ppermute(edges, axes, across)
    edges_own = lax.ppermute(swapped[half : half + 6], axes, across)
    fwd1, fwd2, bwd2, bwd1, bias1, bias2 = call(
        weights_kernel,
        out_shape=[pltpu.VMEM((192, 192), BF16)] * 4 + [pltpu.VMEM((64, 128), F32)] * 2,
        cost_estimate=lasting(0.3),
        name="weights",
    )(*near(w1, b1, w2, b2))

    x3, h3, d3, e3, slopes, mine_a, theirs_a, grad2, grad1 = call(
        inner_kernel,
        out_shape=[
            flat(208, half + 4),
            flat(208, half + 2),
            flat(192, half),
            flat(192, half - 2),
            pltpu.VMEM((half, chans, width), F32),
            rows_of(half - 2),
            rows_of(half - 2),
            pltpu.VMEM((208, 192), F32),
            pltpu.VMEM((208, 192), F32),
        ],
        scratch_shapes=[
            pltpu.VMEM((2, half + 4, chans, cols), BF16),
            pltpu.VMEM((2, half + 2, chans, cols), BF16),
            flat(192, half),
            flat(192, half - 1),
        ],
        cost_estimate=lasting(4.0),
        name="inner",
    )(*near(image_p, cot_p, swapped, fwd1, fwd2, bwd2, bias1, bias2))
    half_grads = pltpu.VMEM((8, TILES * 128), F32)
    e3_b, mine_b, theirs_b, grads_own, grads_send = call(
        outer_kernel,
        out_shape=[flat(192, 4), rows_of(2), rows_of(2), half_grads, half_grads],
        scratch_shapes=[
            pltpu.VMEM((2, 4, chans, cols), BF16),
            pltpu.VMEM((2, 4, chans, cols), BF16),
            flat(208, 4),
            flat(208, 4),
            flat(192, 4),
            pltpu.VMEM((2, chans, width), F32),
            flat(192, 4),
            flat(192, 5),
        ],
        cost_estimate=lasting(2.0),
        name="outer",
    )(
        *near(edges_own, edges_other, cot_p, swapped, fwd1, fwd2, bwd2, bias1, bias2),
        *near(x3, h3, d3, slopes, grad2, grad1),
    )
    grads_received = lax.ppermute(grads_send, "sx", SWAP)
    held = call(pair_kernel, out_shape=pltpu.VMEM((8, TILES * 128), BF16), name="pair")(
        *near(grads_own, grads_received)
    )
    stages = exchange_stages(places, planes)
    for n, stage in enumerate(stages):
        final = n == len(stages) - 1
        received = [lax.ppermute(held, axes, pairs) for pairs in stage]
        sums = pltpu.VMEM((8, TILES * 128), F32 if final else BF16)
        add = functools.partial(add_kernel, factor if final else 1.0)
        if n == 0:
            mine, theirs = call(
                input_kernel,
                out_shape=[rows_of(rows), rows_of(rows)],
                cost_estimate=lasting(1.0),
                name="input",
            )(*near(held, e3_b, e3, bwd1, mine_a, mine_b, theirs_a, theirs_b))
            held, theirs = call(
                functools.partial(passing_add, add),
                out_shape=[sums, rows_of(rows)],
                input_output_aliases={0: 1},
                name="add",
            )(*near(theirs, held, *received))
            back = lax.ppermute(theirs, "sx", SWAP)
            out, image_grad, done = call(
                outputs_kernel,
                out_shape=[shape_of(image.shape, BF16)] * 2 + [pltpu.VMEM((8, 128), F32)],
                scratch_shapes=[pltpu.VMEM((2, rows, chans, cols), BF16)],
                cost_estimate=lasting(1.3),
                name="outputs",
            )(*near(mine, back))
        elif n == 1:
            held = call(functools.partial(behind_add, add), out_shape=sums, name="add")(
                *near(done, held, *received)
            )
        else:
            held = call(add, out_shape=sums, name="add")(*near(held, *received))
    swapped_sums = lax.ppermute(held, "sx", SWAP)
    weight_shape = shape_of((3, 3, chans, chans), F32)
    bias_shape = shape_of((1, chans), F32)
    gw1, gb1, gw2, gb2 = call(
        grads_kernel,
        out_shape=[weight_shape, bias_shape, weight_shape, bias_shape],
        name="grads",
    )(*near(held, swapped_sums))
    return out, image_grad, gw1, gb1.reshape(chans), gw2, gb2.reshape(chans)


def solution(mesh):
    return jax.shard_map(
        local,
        mesh=mesh,
        in_specs=(P("grp", None, "sy", "sx"), P(), P(), P(), P(), P("grp", None, "sy", "sx")),
        out_specs=(P("grp", None, "sy", "sx"), P("grp", None, "sy", "sx"), P(), P(), P(), P()),
        check_vma=False,
    )
```

```python
import functools

import jax
import jax.numpy as jnp
from jax import lax
from jax.experimental import pallas as pl
from jax.experimental.pallas import tpu as pltpu
from jax.sharding import PartitionSpec as P

BF16 = jnp.bfloat16
F32 = jnp.float32
PARAMS = pltpu.CompilerParams(vmem_limit_bytes=32 * 1024 * 1024)
SWAP = [(0, 1), (1, 0)]
CONTRACT = (((1,), (1,)), ((), ()))
TILES = 37


def half_of(side, place, plane):
    bits = place ^ plane
    return (side ^ bits ^ (bits >> 1) ^ (bits >> 2) ^ (bits >> 3)) & 1


def own_half():
    return half_of(lax.axis_index("sx"), lax.axis_index("sy"), lax.axis_index("grp"))


def shape_of(shape, dtype):
    return jax.ShapeDtypeStruct(shape, dtype)


def near(*arrays):
    return [pltpu.with_memory_space_constraint(array, pltpu.VMEM) for array in arrays]


def far(*arrays):
    return [pltpu.with_memory_space_constraint(array, pltpu.HBM) for array in arrays]


def lasting(micros):
    return pl.CostEstimate(flops=int(micros * 1.1e9), transcendentals=0, bytes_accessed=0)


def turned(side, index, count):
    return index + side * (count - 1 - 2 * index)


def pack_kernel(
    image_ref,
    cot_ref,
    w1,
    b1,
    w2,
    b2,
    image_p,
    cot_p,
    swap,
    edges,
    w1_v,
    b1_v,
    w2_v,
    b2_v,
    image_v,
    cot_v,
    sems,
):
    side = lax.axis_index("sx")
    rows = image_ref.shape[2]
    half = rows // 2
    jobs, small = [], []
    sources = ((image_ref, image_v, image_p), (cot_ref, cot_v, cot_p))
    for c in range(image_ref.shape[1] // 16):
        chans = slice(16 * c, 16 * c + 16)
        for n, (src, dst, out) in enumerate(sources):
            copy = pltpu.make_async_copy(src.at[0, chans], dst.at[chans], sems.at[2 * c + n])
            copy.start()
            jobs.append((copy, chans, dst, out))
    for n, (src, dst) in enumerate(((w1, w1_v), (b1, b1_v), (w2, w2_v), (b2, b2_v))):
        copy = pltpu.make_async_copy(src, dst, sems.at[len(jobs) + n])
        copy.start()
        small.append(copy)
    for copy, chans, dst, out in jobs:
        copy.wait()
        block = jnp.transpose(dst[chans], (1, 0, 2))
        for h in range(rows):
            out[turned(side, h, rows), chans, :] = block[h]
    swap[0 : half + 4] = image_p[half - 4 : rows]
    for k in range(half + 2):
        swap[half + 4 + k] = cot_p[rows - 1 - k]
    for k in range(4):
        edges[k] = image_p[3 - k]
    edges[4:6] = cot_p[0:2]
    for copy in small:
        copy.wait()


def column(row):
    chans = row.shape[1]
    r = lax.broadcasted_iota(jnp.int32, (chans, chans), 0)
    c = lax.broadcasted_iota(jnp.int32, (chans, chans), 1)
    wide = jnp.broadcast_to(row, (chans, chans))
    return jnp.sum(jnp.where(r == c, wide, 0.0), axis=1, keepdims=True)


def weights_kernel(w1, b1, w2, b2, fwd1, fwd2, bwd2, bwd1, bias1, bias2):
    side = lax.axis_index("sx")
    for w, fwd, bwd in ((w1, fwd1, bwd1), (w2, fwd2, bwd2)):
        for a in range(3):
            tap = turned(side, a, 3)
            fwd[a * 64 : a * 64 + 64, :] = jnp.concatenate(
                [jnp.transpose(w[tap, b].astype(F32)) for b in range(3)], axis=1
            ).astype(BF16)
            bwd[a * 64 : a * 64 + 64, :] = jnp.concatenate(
                [w[2 - tap, 2 - b].astype(F32) for b in range(3)], axis=1
            ).astype(BF16)
    bias1[...] = jnp.broadcast_to(column(b1[...]), bias1.shape)
    bias2[...] = jnp.broadcast_to(column(b2[...]), bias2.shape)


def spread(dst, at, row):
    chans, width = row.shape
    zero = jnp.zeros((chans, 1), row.dtype)
    cols = slice(at * width, (at + 1) * width)
    dst[0:chans, cols] = jnp.concatenate([zero, row[:, :-1]], axis=1)
    dst[chans : 2 * chans, cols] = row
    dst[2 * chans : 3 * chans, cols] = jnp.concatenate([row[:, 1:], zero], axis=1)


def sweep(weight_ref, rows, first, emit):
    weight = weight_ref[...]
    upper = lower = None
    for n, (ref, at) in enumerate(rows):
        part = jnp.dot(weight, ref.spread_row(at), preferred_element_type=F32)
        if n >= 2:
            emit(first + n - 1, upper + part[128:192])
        upper = part[64:128] if lower is None else lower + part[64:128]
        lower = part[0:64]


class Rows:
    def __init__(self, ref, width):
        self.ref, self.width = ref, width

    def spread_row(self, at):
        return self.ref[0:192, at * self.width : (at + 1) * self.width]

    def span(self, start, stop):
        return self.ref[:, start * self.width : stop * self.width]


def joined(width, outer, start, inner, split, first, count):
    outer, inner = Rows(outer, width), Rows(inner, width)
    return [
        (outer, e - start) if e < split else (inner, e - split)
        for e in range(first, first + count)
    ]


def silu_and_slope(pre):
    gate = 0.5 + 0.5 * jnp.tanh(0.5 * pre)
    value = pre * gate
    return value, gate + value * (1.0 - gate)


def clear(side, taps, width, start, stop, j0, j1):
    for a in range(3):
        place = pl.ds(pl.multiple_of(64 * turned(side, a, 3), 64), 64)
        for q in range(start, stop):
            if not j0 <= q - a < j1:
                at = q - start
                taps[place, at * width : (at + 1) * width] = jnp.zeros((64, width), BF16)


def store_taps(side, taps, width, start, j, delta):
    for a in range(3):
        place = pl.ds(pl.multiple_of(64 * turned(side, a, 3), 64), 64)
        at = j + a - start
        taps[place, at * width : (at + 1) * width] = delta


def hand_out(side, mine, theirs, at, value):
    width = value.shape[1]
    left, right = value[:, : width // 2], value[:, width // 2 :]
    mine[at] = jnp.where(side == 0, left, right).astype(BF16)
    theirs[at] = jnp.where(side == 0, right, left).astype(BF16)


def inner_kernel(
    image_p,
    cot_p,
    swapped,
    fwd1,
    fwd2,
    bwd2,
    bias1,
    bias2,
    x3,
    h3,
    d3,
    e3,
    slopes,
    mine,
    theirs,
    grad2,
    grad1,
    image_s,
    cot_s,
    taps2,
    taps1,
):
    side = lax.axis_index("sx")
    half = image_p.shape[0] // 2
    width = 2 * image_p.shape[2]
    last = half + 8
    other = 1 - side
    image_s[side] = image_p[0 : half + 4]
    cot_s[side] = cot_p[0 : half + 2]
    for p in range(half + 4):
        image_s[other, p] = swapped[half + 3 - p]
    cot_s[other] = swapped[half + 4 : 2 * half + 6]
    ones = jnp.ones((16, x3.shape[1]), BF16)
    x3[192:208, :] = ones
    h3[192:208, :] = ones[:, : h3.shape[1]]
    clear(side, taps2, width, 2, half + 2, 2, half)
    clear(side, taps1, width, 3, half + 2, 3, half)
    for p in range(half + 4):
        spread(x3, p, jnp.concatenate([image_s[0, p], image_s[1, p]], axis=1))
    shift1 = jnp.broadcast_to(bias1[:, 0:1], (64, width))
    shift2 = jnp.broadcast_to(bias2[:, 0:1], (64, width))

    def first(e, acc):
        hidden, slope = silu_and_slope(acc + shift1)
        spread(h3, e - 5, hidden.astype(BF16))
        if e < half + 5:
            slopes[e - 5] = slope

    x_rows, h_rows = Rows(x3, width), Rows(h3, width)
    sweep(fwd1, [(x_rows, e - 4) for e in range(4, last)], 4, first)

    def second(e, acc):
        value, slope = silu_and_slope(acc + shift2)
        cot = jnp.concatenate([cot_s[0, e - 4], cot_s[1, e - 4]], axis=1).astype(F32)
        delta = (cot * slope).astype(BF16)
        spread(d3, e - 6, delta)
        if e < half + 4:
            hand_out(side, mine, theirs, e - 6, value)
            store_taps(side, taps2, width, 2, e - 4, delta)

    sweep(fwd2, [(h_rows, e - 5) for e in range(5, last - 1)], 5, second)

    def third(e, acc):
        delta = (acc * slopes[e - 5]).astype(BF16)
        spread(e3, e - 7, delta)
        if e < half + 4:
            store_taps(side, taps1, width, 3, e - 4, delta)

    sweep(bwd2, [(Rows(d3, width), e - 6) for e in range(6, last - 2)], 6, third)

    grad2[...] = lax.dot_general(
        h_rows.span(0, half), taps2[...], CONTRACT, preferred_element_type=F32
    )
    grad1[...] = lax.dot_general(
        x_rows.span(2, half + 1), taps1[...], CONTRACT, preferred_element_type=F32
    )


def outer_kernel(
    edges_own,
    edges_other,
    cot_p,
    swapped,
    fwd1,
    fwd2,
    bwd2,
    bias1,
    bias2,
    x3,
    h3,
    d3,
    slopes,
    grad2,
    grad1,
    e3_b,
    mine,
    theirs,
    grads_own,
    grads_send,
    image_s,
    cot_s,
    x3_b,
    h3_b,
    d3_b,
    slopes_b,
    taps2,
    taps1,
):
    side = lax.axis_index("sx")
    place = lax.axis_index("sy")
    half = cot_p.shape[0] // 2
    width = 2 * cot_p.shape[2]
    other = 1 - side
    outside = place == side * (lax.axis_size("sy") - 1)


    def keep(value):
        return jnp.where(outside, 0.0, value.astype(F32)).astype(BF16)

    for cols, edges in ((side, edges_own), (other, edges_other)):
        image_s[cols] = keep(edges[0:4])
        cot_s[cols, 0] = keep(edges[5])
        cot_s[cols, 1] = keep(edges[4])
    cot_s[side, 2:4] = cot_p[0:2]
    cot_s[other, 2:4] = swapped[half + 4 : half + 6]
    ones = jnp.ones((16, x3_b.shape[1]), BF16)
    x3_b[192:208, :] = ones
    h3_b[192:208, :] = ones
    clear(side, taps2, width, 0, 4, 0, 2)
    clear(side, taps1, width, 0, 5, 0, 3)
    for e in range(4):
        spread(x3_b, e, jnp.concatenate([image_s[0, e], image_s[1, e]], axis=1))
    shift1 = jnp.broadcast_to(bias1[:, 0:1], (64, width))
    shift2 = jnp.broadcast_to(bias2[:, 0:1], (64, width))

    def first(e, acc):
        hidden, slope = silu_and_slope(acc + shift1)
        if e < 4:
            hidden = jnp.where(outside, 0.0, hidden)
        spread(h3_b, e - 1, hidden.astype(BF16))
        if e >= 3:
            slopes_b[e - 3] = slope

    sweep(fwd1, joined(width, x3_b, 0, x3, 4, 0, 6), 0, first)

    def second(e, acc):
        value, slope = silu_and_slope(acc + shift2)
        cot = jnp.concatenate([cot_s[0, e - 2], cot_s[1, e - 2]], axis=1).astype(F32)
        delta = (cot * slope).astype(BF16)
        spread(d3_b, e - 2, delta)
        if e >= 4:
            hand_out(side, mine, theirs, e - 4, value)
            store_taps(side, taps2, width, 0, e - 4, delta)

    sweep(fwd2, joined(width, h3_b, 1, h3, 5, 1, 6), 1, second)

    def third(e, acc):
        delta = acc * (slopes_b[e - 3] if e < 5 else slopes[e - 5])
        if e < 4:
            delta = jnp.where(outside, 0.0, delta)
        delta = delta.astype(BF16)
        spread(e3_b, e - 3, delta)
        if e >= 4:
            store_taps(side, taps1, width, 0, e - 4, delta)

    sweep(bwd2, joined(width, d3_b, 2, d3, 6, 2, 6), 2, third)

    def product(left, right):
        return lax.dot_general(left, right, CONTRACT, preferred_element_type=F32)

    total2 = (
        grad2[...]
        + product(Rows(h3_b, width).span(2, 4), taps2[:, : 2 * width])
        + product(Rows(h3, width).span(0, 2), taps2[:, 2 * width :])
    )
    total1 = (
        grad1[...]
        + product(Rows(x3_b, width).span(3, 4), taps1[:, :width])
        + product(Rows(x3, width).span(0, 4), taps1[:, width:])
    )
    both = jnp.concatenate([total2[0:192], total1[0:192]], axis=1)
    biases = jnp.concatenate([total2[192:200, 64:128], total1[192:200, 64:128]], axis=1)
    tiles = [
        both[8 * (t // 3) : 8 * (t // 3) + 8, 128 * (t % 3) : 128 * (t % 3) + 128]
        for t in range(72)
    ]
    empty = jnp.zeros((8, 128), F32)
    own = own_half()
    low, high = tiles[:36] + [biases], tiles[36:] + [empty]
    for t in range(TILES):
        at = slice(128 * t, 128 * t + 128)
        grads_own[:, at] = jnp.where(own == 0, low[t], high[t])
        grads_send[:, at] = jnp.where(own == 0, high[t], low[t])


def pair_kernel(own, received, out):
    out[...] = (own[...] + received[...]).astype(BF16)


def add_kernel(factor, *refs):
    out = refs[-1]
    terms = [ref[...].astype(F32) for ref in refs[:-1]]
    while len(terms) > 1:
        terms = [sum(terms[n + 1 : n + 2], terms[n]) for n in range(0, len(terms), 2)]
    out[...] = (terms[0] * factor).astype(out.dtype)


def passing_add(add, passed, *refs):
    add(*refs[:-1])


def behind_add(add, done, *refs):
    add(*refs)


def input_kernel(held, e3_b, e3, bwd1, mine_a, mine_b, theirs_a, theirs_b, mine, theirs):
    side = lax.axis_index("sx")
    half = mine.shape[0] // 2
    width = 2 * mine.shape[2]
    for whole, inner, outer in ((mine, mine_a, mine_b), (theirs, theirs_a, theirs_b)):
        whole[0:2] = outer[...]
        whole[2:half] = inner[...]

    def emit(e, acc):
        hand_out(side, mine, theirs, half + e - 4, acc)

    sweep(bwd1, joined(width, e3_b, 3, e3, 7, 3, half + 2), 3, emit)


def outputs_kernel(mine, back, out, image_grad, token, natural):
    side = lax.axis_index("sx")
    rows = out.shape[2]
    half = rows // 2
    for slot in range(2):
        for j in range(half):
            natural[slot, turned(side, j, rows)] = mine[slot * half + j]
            natural[slot, turned(side, rows - 1 - j, rows)] = back[slot * half + j]
    for slot, ref in ((0, out), (1, image_grad)):
        ref[0] = jnp.transpose(natural[slot], (1, 0, 2))
    token[...] = jnp.zeros(token.shape, F32)


def grads_kernel(held, swapped, gw1, gb1, gw2, gb2):
    own = own_half()

    def tile(part, t):
        at = slice(128 * t, 128 * t + 128)
        return jnp.where(own == part, held[:, at], swapped[:, at])

    for block in range(24):
        part, first = block // 12, 3 * (block % 12)
        line = jnp.concatenate([tile(part, first + p) for p in range(3)], axis=1)
        b, i = block // 8, (block % 8) * 8
        for a in range(3):
            gw2[a, b, i : i + 8, :] = line[:, a * 64 : a * 64 + 64]
            gw1[a, b, i : i + 8, :] = line[:, 192 + a * 64 : 256 + a * 64]
    biases = tile(0, 36)
    gb2[...] = biases[0:1, 0:64]
    gb1[...] = biases[0:1, 64:128]


def exchange_stages(places, planes):
    def groups(count, axis):
        bits = [1 << k for k in range(count.bit_length() - 1)]
        pairs = [bits[k : k + 2] for k in range(0, len(bits), 2)]
        return [(axis, [b[0]] + ([b[1], b[0] | b[1]] if len(b) == 2 else [])) for b in pairs]

    rows, slides = groups(places, 0), groups(planes, 1)
    stages = []
    for plan in zip(rows + slides, slides + rows):
        stage = []
        for k in range(3):
            pairs = []
            for s in range(places):
                for x in range(2):
                    for g in range(planes):
                        part = half_of(x, s, g)
                        axis, masks = plan[part]
                        if k < len(masks):
                            t, h = (s ^ masks[k], g) if axis == 0 else (s, g ^ masks[k])
                            y = half_of(part, t, h)
                            pairs.append(((2 * s + x) * planes + g, (2 * t + y) * planes + h))
            if pairs:
                stage.append(pairs)
        stages.append(stage)
    return stages


def local(image, weight_one, bias_one, weight_two, bias_two, cotangent):
    _, chans, rows, cols = image.shape
    places, planes = lax.axis_size("sy"), lax.axis_size("grp")
    half = rows // 2
    width = 2 * cols
    factor = float(rows * cols * places * planes * lax.axis_size("sx")) ** (-0.5)
    call = functools.partial(pl.pallas_call, compiler_params=PARAMS)

    def rows_of(count):
        return pltpu.VMEM((count, chans, cols), BF16)

    def flat(height, count):
        return pltpu.VMEM((height, count * width), BF16)

    image_p, cot_p, swap, edges, w1, b1, w2, b2 = call(
        pack_kernel,
        out_shape=[
            rows_of(rows),
            rows_of(rows),
            rows_of(2 * half + 6),
            rows_of(6),
            pltpu.VMEM(weight_one.shape, BF16),
            pltpu.VMEM((1, chans), F32),
            pltpu.VMEM(weight_two.shape, BF16),
            pltpu.VMEM((1, chans), F32),
        ],
        in_specs=[pl.BlockSpec(memory_space=pltpu.HBM)] * 6,
        scratch_shapes=[
            pltpu.VMEM((chans, rows, cols), BF16),
            pltpu.VMEM((chans, rows, cols), BF16),
            pltpu.SemaphoreType.DMA((chans // 8 + 4,)),
        ],
        name="pack",
    )(
        *far(image, cotangent, weight_one, bias_one.reshape(1, chans)),
        *far(weight_two, bias_two.reshape(1, chans)),
    )
    swapped = lax.ppermute(swap, "sx", SWAP)
    across = []
    for s in range(places):
        for g in range(planes):
            lower, upper = 2 * s * planes + g, (2 * s + 1) * planes + g
            across.append((lower, lower - planes if s > 0 else lower ^ 1))
            across.append((upper, upper + planes if s < places - 1 else upper ^ 1))
    axes = ("sy", "sx", "grp")
    edges_other = lax.ppermute(edges, axes, across)
    edges_own = lax.ppermute(swapped[half : half + 6], axes, across)
    fwd1, fwd2, bwd2, bwd1, bias1, bias2 = call(
        weights_kernel,
        out_shape=[pltpu.VMEM((192, 192), BF16)] * 4 + [pltpu.VMEM((64, 128), F32)] * 2,
        cost_estimate=lasting(0.3),
        name="weights",
    )(*near(w1, b1, w2, b2))

    x3, h3, d3, e3, slopes, mine_a, theirs_a, grad2, grad1 = call(
        inner_kernel,
        out_shape=[
            flat(208, half + 4),
            flat(208, half + 2),
            flat(192, half),
            flat(192, half - 2),
            pltpu.VMEM((half, chans, width), F32),
            rows_of(half - 2),
            rows_of(half - 2),
            pltpu.VMEM((208, 192), F32),
            pltpu.VMEM((208, 192), F32),
        ],
        scratch_shapes=[
            pltpu.VMEM((2, half + 4, chans, cols), BF16),
            pltpu.VMEM((2, half + 2, chans, cols), BF16),
            flat(192, half),
            flat(192, half - 1),
        ],
        cost_estimate=lasting(4.0),
        name="inner",
    )(*near(image_p, cot_p, swapped, fwd1, fwd2, bwd2, bias1, bias2))
    half_grads = pltpu.VMEM((8, TILES * 128), F32)
    e3_b, mine_b, theirs_b, grads_own, grads_send = call(
        outer_kernel,
        out_shape=[flat(192, 4), rows_of(2), rows_of(2), half_grads, half_grads],
        scratch_shapes=[
            pltpu.VMEM((2, 4, chans, cols), BF16),
            pltpu.VMEM((2, 4, chans, cols), BF16),
            flat(208, 4),
            flat(208, 4),
            flat(192, 4),
            pltpu.VMEM((2, chans, width), F32),
            flat(192, 4),
            flat(192, 5),
        ],
        cost_estimate=lasting(2.0),
        name="outer",
    )(
        *near(edges_own, edges_other, cot_p, swapped, fwd1, fwd2, bwd2, bias1, bias2),
        *near(x3, h3, d3, slopes, grad2, grad1),
    )
    grads_received = lax.ppermute(grads_send, "sx", SWAP)
    held = call(pair_kernel, out_shape=pltpu.VMEM((8, TILES * 128), BF16), name="pair")(
        *near(grads_own, grads_received)
    )
    stages = exchange_stages(places, planes)
    for n, stage in enumerate(stages):
        final = n == len(stages) - 1
        received = [lax.ppermute(held, axes, pairs) for pairs in stage]
        sums = pltpu.VMEM((8, TILES * 128), F32 if final else BF16)
        add = functools.partial(add_kernel, factor if final else 1.0)
        if n == 0:
            mine, theirs = call(
                input_kernel,
                out_shape=[rows_of(rows), rows_of(rows)],
                cost_estimate=lasting(1.0),
                name="input",
            )(*near(held, e3_b, e3, bwd1, mine_a, mine_b, theirs_a, theirs_b))
            held, theirs = call(
                functools.partial(passing_add, add),
                out_shape=[sums, rows_of(rows)],
                input_output_aliases={0: 1},
                name="add",
            )(*near(theirs, held, *received))
            back = lax.ppermute(theirs, "sx", SWAP)
            out, image_grad, done = call(
                outputs_kernel,
                out_shape=[shape_of(image.shape, BF16)] * 2 + [pltpu.VMEM((8, 128), F32)],
                scratch_shapes=[pltpu.VMEM((2, rows, chans, cols), BF16)],
                cost_estimate=lasting(1.3),
                name="outputs",
            )(*near(mine, back))
        elif n == 1:
            held = call(functools.partial(behind_add, add), out_shape=sums, name="add")(
                *near(done, held, *received)
            )
        else:
            held = call(add, out_shape=sums, name="add")(*near(held, *received))
    swapped_sums = lax.ppermute(held, "sx", SWAP)
    weight_shape = shape_of((3, 3, chans, chans), F32)
    bias_shape = shape_of((1, chans), F32)
    gw1, gb1, gw2, gb2 = call(
        grads_kernel,
        out_shape=[weight_shape, bias_shape, weight_shape, bias_shape],
        name="grads",
    )(*near(held, swapped_sums))
    return out, image_grad, gw1, gb1.reshape(chans), gw2, gb2.reshape(chans)


def solution(mesh):
    return jax.shard_map(
        local,
        mesh=mesh,
        in_specs=(P("grp", None, "sy", "sx"), P(), P(), P(), P(), P("grp", None, "sy", "sx")),
        out_specs=(P("grp", None, "sy", "sx"), P("grp", None, "sy", "sx"), P(), P(), P(), P()),
        check_vma=False,
    )
```

```python
import functools

import jax
import jax.numpy as jnp
from jax import lax
from jax.experimental import pallas as pl
from jax.experimental.pallas import tpu as pltpu
from jax.sharding import PartitionSpec as P

BF16 = jnp.bfloat16
F32 = jnp.float32
PARAMS = pltpu.CompilerParams(vmem_limit_bytes=32 * 1024 * 1024)
SWAP = [(0, 1), (1, 0)]
CONTRACT = (((1,), (1,)), ((), ()))
TILES = 37


def half_of(side, place, plane):
    bits = place ^ plane
    return (side ^ bits ^ (bits >> 1) ^ (bits >> 2) ^ (bits >> 3)) & 1


def own_half():
    return half_of(lax.axis_index("sx"), lax.axis_index("sy"), lax.axis_index("grp"))


def shape_of(shape, dtype):
    return jax.ShapeDtypeStruct(shape, dtype)


def near(*arrays):
    return [pltpu.with_memory_space_constraint(array, pltpu.VMEM) for array in arrays]


def far(*arrays):
    return [pltpu.with_memory_space_constraint(array, pltpu.HBM) for array in arrays]


def lasting(micros):
    return pl.CostEstimate(flops=int(micros * 1.1e9), transcendentals=0, bytes_accessed=0)


def turned(side, index, count):
    return index + side * (count - 1 - 2 * index)


def pack_kernel(
    image_ref,
    cot_ref,
    w1,
    b1,
    w2,
    b2,
    image_p,
    cot_p,
    swap,
    edges,
    w1_v,
    b1_v,
    w2_v,
    b2_v,
    image_v,
    cot_v,
    sems,
):
    side = lax.axis_index("sx")
    rows = image_ref.shape[2]
    half = rows // 2
    jobs, small = [], []
    sources = ((image_ref, image_v, image_p), (cot_ref, cot_v, cot_p))
    for c in range(image_ref.shape[1] // 16):
        chans = slice(16 * c, 16 * c + 16)
        for n, (src, dst, out) in enumerate(sources):
            copy = pltpu.make_async_copy(src.at[0, chans], dst.at[chans], sems.at[2 * c + n])
            copy.start()
            jobs.append((copy, chans, dst, out))
    for n, (src, dst) in enumerate(((w1, w1_v), (b1, b1_v), (w2, w2_v), (b2, b2_v))):
        copy = pltpu.make_async_copy(src, dst, sems.at[len(jobs) + n])
        copy.start()
        small.append(copy)
    for copy, chans, dst, out in jobs:
        copy.wait()
        block = jnp.transpose(dst[chans], (1, 0, 2))
        for h in range(rows):
            out[turned(side, h, rows), chans, :] = block[h]
    swap[0 : half + 4] = image_p[half - 4 : rows]
    for k in range(half + 2):
        swap[half + 4 + k] = cot_p[rows - 1 - k]
    for k in range(4):
        edges[k] = image_p[3 - k]
    edges[4:6] = cot_p[0:2]
    for copy in small:
        copy.wait()


def column(row):
    chans = row.shape[1]
    r = lax.broadcasted_iota(jnp.int32, (chans, chans), 0)
    c = lax.broadcasted_iota(jnp.int32, (chans, chans), 1)
    wide = jnp.broadcast_to(row, (chans, chans))
    return jnp.sum(jnp.where(r == c, wide, 0.0), axis=1, keepdims=True)


def weights_kernel(w1, b1, w2, b2, fwd1, fwd2, bwd2, bwd1, bias1, bias2):
    side = lax.axis_index("sx")
    for w, fwd, bwd in ((w1, fwd1, bwd1), (w2, fwd2, bwd2)):
        for a in range(3):
            tap = turned(side, a, 3)
            fwd[a * 64 : a * 64 + 64, :] = jnp.concatenate(
                [jnp.transpose(w[tap, b].astype(F32)) for b in range(3)], axis=1
            ).astype(BF16)
            bwd[a * 64 : a * 64 + 64, :] = jnp.concatenate(
                [w[2 - tap, 2 - b].astype(F32) for b in range(3)], axis=1
            ).astype(BF16)
    bias1[...] = jnp.broadcast_to(column(b1[...]), bias1.shape)
    bias2[...] = jnp.broadcast_to(column(b2[...]), bias2.shape)


def spread(dst, at, row):
    chans, width = row.shape
    zero = jnp.zeros((chans, 1), row.dtype)
    cols = slice(at * width, (at + 1) * width)
    dst[0:chans, cols] = jnp.concatenate([zero, row[:, :-1]], axis=1)
    dst[chans : 2 * chans, cols] = row
    dst[2 * chans : 3 * chans, cols] = jnp.concatenate([row[:, 1:], zero], axis=1)


def sweep(weight_ref, rows, first, emit):
    weight = weight_ref[...]
    upper = lower = None
    for n, (ref, at) in enumerate(rows):
        part = jnp.dot(weight, ref.spread_row(at), preferred_element_type=F32)
        if n >= 2:
            emit(first + n - 1, upper + part[128:192])
        upper = part[64:128] if lower is None else lower + part[64:128]
        lower = part[0:64]


class Rows:
    def __init__(self, ref, width):
        self.ref, self.width = ref, width

    def spread_row(self, at):
        return self.ref[0:192, at * self.width : (at + 1) * self.width]

    def span(self, start, stop):
        return self.ref[:, start * self.width : stop * self.width]


def joined(width, outer, start, inner, split, first, count):
    outer, inner = Rows(outer, width), Rows(inner, width)
    return [
        (outer, e - start) if e < split else (inner, e - split)
        for e in range(first, first + count)
    ]


def silu_and_slope(pre):
    gate = 0.5 + 0.5 * jnp.tanh(0.5 * pre)
    value = pre * gate
    return value, gate + value * (1.0 - gate)


def clear(side, taps, width, start, stop, j0, j1):
    for a in range(3):
        place = pl.ds(pl.multiple_of(64 * turned(side, a, 3), 64), 64)
        for q in range(start, stop):
            if not j0 <= q - a < j1:
                at = q - start
                taps[place, at * width : (at + 1) * width] = jnp.zeros((64, width), BF16)


def store_taps(side, taps, width, start, j, delta):
    for a in range(3):
        place = pl.ds(pl.multiple_of(64 * turned(side, a, 3), 64), 64)
        at = j + a - start
        taps[place, at * width : (at + 1) * width] = delta


def hand_out(side, mine, theirs, at, value):
    width = value.shape[1]
    left, right = value[:, : width // 2], value[:, width // 2 :]
    mine[at] = jnp.where(side == 0, left, right).astype(BF16)
    theirs[at] = jnp.where(side == 0, right, left).astype(BF16)


def inner_kernel(
    image_p,
    cot_p,
    swapped,
    fwd1,
    fwd2,
    bwd2,
    bias1,
    bias2,
    x3,
    h3,
    d3,
    e3,
    slopes,
    mine,
    theirs,
    grad2,
    grad1,
    image_s,
    cot_s,
    taps2,
    taps1,
):
    side = lax.axis_index("sx")
    half = image_p.shape[0] // 2
    width = 2 * image_p.shape[2]
    last = half + 8
    other = 1 - side
    image_s[side] = image_p[0 : half + 4]
    cot_s[side] = cot_p[0 : half + 2]
    for p in range(half + 4):
        image_s[other, p] = swapped[half + 3 - p]
    cot_s[other] = swapped[half + 4 : 2 * half + 6]
    ones = jnp.ones((16, x3.shape[1]), BF16)
    x3[192:208, :] = ones
    h3[192:208, :] = ones[:, : h3.shape[1]]
    clear(side, taps2, width, 2, half + 2, 2, half)
    clear(side, taps1, width, 3, half + 2, 3, half)
    for p in range(half + 4):
        spread(x3, p, jnp.concatenate([image_s[0, p], image_s[1, p]], axis=1))
    shift1 = jnp.broadcast_to(bias1[:, 0:1], (64, width))
    shift2 = jnp.broadcast_to(bias2[:, 0:1], (64, width))

    def first(e, acc):
        hidden, slope = silu_and_slope(acc + shift1)
        spread(h3, e - 5, hidden.astype(BF16))
        if e < half + 5:
            slopes[e - 5] = slope

    x_rows, h_rows = Rows(x3, width), Rows(h3, width)
    sweep(fwd1, [(x_rows, e - 4) for e in range(4, last)], 4, first)

    def second(e, acc):
        value, slope = silu_and_slope(acc + shift2)
        cot = jnp.concatenate([cot_s[0, e - 4], cot_s[1, e - 4]], axis=1).astype(F32)
        delta = (cot * slope).astype(BF16)
        spread(d3, e - 6, delta)
        if e < half + 4:
            hand_out(side, mine, theirs, e - 6, value)
            store_taps(side, taps2, width, 2, e - 4, delta)

    sweep(fwd2, [(h_rows, e - 5) for e in range(5, last - 1)], 5, second)

    def third(e, acc):
        delta = (acc * slopes[e - 5]).astype(BF16)
        spread(e3, e - 7, delta)
        if e < half + 4:
            store_taps(side, taps1, width, 3, e - 4, delta)

    sweep(bwd2, [(Rows(d3, width), e - 6) for e in range(6, last - 2)], 6, third)

    grad2[...] = lax.dot_general(
        h_rows.span(0, half), taps2[...], CONTRACT, preferred_element_type=F32
    )
    grad1[...] = lax.dot_general(
        x_rows.span(2, half + 1), taps1[...], CONTRACT, preferred_element_type=F32
    )


def outer_kernel(
    edges_own,
    edges_other,
    cot_p,
    swapped,
    fwd1,
    fwd2,
    bwd2,
    bias1,
    bias2,
    x3,
    h3,
    d3,
    slopes,
    grad2,
    grad1,
    e3_b,
    mine,
    theirs,
    grads_own,
    grads_send,
    image_s,
    cot_s,
    x3_b,
    h3_b,
    d3_b,
    slopes_b,
    taps2,
    taps1,
):
    side = lax.axis_index("sx")
    place = lax.axis_index("sy")
    half = cot_p.shape[0] // 2
    width = 2 * cot_p.shape[2]
    other = 1 - side
    outside = place == side * (lax.axis_size("sy") - 1)


    def keep(value):
        return jnp.where(outside, 0.0, value.astype(F32)).astype(BF16)

    for cols, edges in ((side, edges_own), (other, edges_other)):
        image_s[cols] = keep(edges[0:4])
        cot_s[cols, 0] = keep(edges[5])
        cot_s[cols, 1] = keep(edges[4])
    cot_s[side, 2:4] = cot_p[0:2]
    cot_s[other, 2:4] = swapped[half + 4 : half + 6]
    ones = jnp.ones((16, x3_b.shape[1]), BF16)
    x3_b[192:208, :] = ones
    h3_b[192:208, :] = ones
    clear(side, taps2, width, 0, 4, 0, 2)
    clear(side, taps1, width, 0, 5, 0, 3)
    for e in range(4):
        spread(x3_b, e, jnp.concatenate([image_s[0, e], image_s[1, e]], axis=1))
    shift1 = jnp.broadcast_to(bias1[:, 0:1], (64, width))
    shift2 = jnp.broadcast_to(bias2[:, 0:1], (64, width))

    def first(e, acc):
        hidden, slope = silu_and_slope(acc + shift1)
        if e < 4:
            hidden = jnp.where(outside, 0.0, hidden)
        spread(h3_b, e - 1, hidden.astype(BF16))
        if e >= 3:
            slopes_b[e - 3] = slope

    sweep(fwd1, joined(width, x3_b, 0, x3, 4, 0, 6), 0, first)

    def second(e, acc):
        value, slope = silu_and_slope(acc + shift2)
        cot = jnp.concatenate([cot_s[0, e - 2], cot_s[1, e - 2]], axis=1).astype(F32)
        delta = (cot * slope).astype(BF16)
        spread(d3_b, e - 2, delta)
        if e >= 4:
            hand_out(side, mine, theirs, e - 4, value)
            store_taps(side, taps2, width, 0, e - 4, delta)

    sweep(fwd2, joined(width, h3_b, 1, h3, 5, 1, 6), 1, second)

    def third(e, acc):
        delta = acc * (slopes_b[e - 3] if e < 5 else slopes[e - 5])
        if e < 4:
            delta = jnp.where(outside, 0.0, delta)
        delta = delta.astype(BF16)
        spread(e3_b, e - 3, delta)
        if e >= 4:
            store_taps(side, taps1, width, 0, e - 4, delta)

    sweep(bwd2, joined(width, d3_b, 2, d3, 6, 2, 6), 2, third)

    def product(left, right):
        return lax.dot_general(left, right, CONTRACT, preferred_element_type=F32)

    total2 = (
        grad2[...]
        + product(Rows(h3_b, width).span(2, 4), taps2[:, : 2 * width])
        + product(Rows(h3, width).span(0, 2), taps2[:, 2 * width :])
    )
    total1 = (
        grad1[...]
        + product(Rows(x3_b, width).span(3, 4), taps1[:, :width])
        + product(Rows(x3, width).span(0, 4), taps1[:, width:])
    )
    both = jnp.concatenate([total2[0:192], total1[0:192]], axis=1)
    biases = jnp.concatenate([total2[192:200, 64:128], total1[192:200, 64:128]], axis=1)
    tiles = [
        both[8 * (t // 3) : 8 * (t // 3) + 8, 128 * (t % 3) : 128 * (t % 3) + 128]
        for t in range(72)
    ]
    empty = jnp.zeros((8, 128), F32)
    own = own_half()
    low, high = tiles[:36] + [biases], tiles[36:] + [empty]
    for t in range(TILES):
        at = slice(128 * t, 128 * t + 128)
        grads_own[:, at] = jnp.where(own == 0, low[t], high[t])
        grads_send[:, at] = jnp.where(own == 0, high[t], low[t])


def pair_kernel(passed, own, received, out, through):
    out[...] = (own[...] + received[...]).astype(BF16)


def add_kernel(factor, *refs):
    out = refs[-1]
    terms = [ref[...].astype(F32) for ref in refs[:-1]]
    while len(terms) > 1:
        terms = [sum(terms[n + 1 : n + 2], terms[n]) for n in range(0, len(terms), 2)]
    out[...] = (terms[0] * factor).astype(out.dtype)


def behind_add(add, done, *refs):
    add(*refs)


def input_kernel(e3_b, e3, bwd1, mine_a, mine_b, theirs_a, theirs_b, mine, theirs):
    side = lax.axis_index("sx")
    half = mine.shape[0] // 2
    width = 2 * mine.shape[2]
    for whole, inner, outer in ((mine, mine_a, mine_b), (theirs, theirs_a, theirs_b)):
        whole[0:2] = outer[...]
        whole[2:half] = inner[...]

    def emit(e, acc):
        hand_out(side, mine, theirs, half + e - 4, acc)

    sweep(bwd1, joined(width, e3_b, 3, e3, 7, 3, half + 2), 3, emit)


def outputs_kernel(mine, back, out, image_grad, token, natural):
    side = lax.axis_index("sx")
    rows = out.shape[2]
    half = rows // 2
    for slot in range(2):
        for j in range(half):
            natural[slot, turned(side, j, rows)] = mine[slot * half + j]
            natural[slot, turned(side, rows - 1 - j, rows)] = back[slot * half + j]
    for slot, ref in ((0, out), (1, image_grad)):
        ref[0] = jnp.transpose(natural[slot], (1, 0, 2))
    token[...] = jnp.zeros(token.shape, F32)


def grads_kernel(held, swapped, gw1, gb1, gw2, gb2):
    own = own_half()

    def tile(part, t):
        at = slice(128 * t, 128 * t + 128)
        return jnp.where(own == part, held[:, at], swapped[:, at])

    for block in range(24):
        part, first = block // 12, 3 * (block % 12)
        line = jnp.concatenate([tile(part, first + p) for p in range(3)], axis=1)
        b, i = block // 8, (block % 8) * 8
        for a in range(3):
            gw2[a, b, i : i + 8, :] = line[:, a * 64 : a * 64 + 64]
            gw1[a, b, i : i + 8, :] = line[:, 192 + a * 64 : 256 + a * 64]
    biases = tile(0, 36)
    gb2[...] = biases[0:1, 0:64]
    gb1[...] = biases[0:1, 64:128]


def exchange_stages(places, planes):
    def groups(count, axis):
        bits = [1 << k for k in range(count.bit_length() - 1)]
        pairs = [bits[k : k + 2] for k in range(0, len(bits), 2)]
        return [(axis, [b[0]] + ([b[1], b[0] | b[1]] if len(b) == 2 else [])) for b in pairs]

    rows, slides = groups(places, 0), groups(planes, 1)
    stages = []
    for plan in zip(rows + slides, slides + rows):
        stage = []
        for k in range(3):
            pairs = []
            for s in range(places):
                for x in range(2):
                    for g in range(planes):
                        part = half_of(x, s, g)
                        axis, masks = plan[part]
                        if k < len(masks):
                            t, h = (s ^ masks[k], g) if axis == 0 else (s, g ^ masks[k])
                            y = half_of(part, t, h)
                            pairs.append(((2 * s + x) * planes + g, (2 * t + y) * planes + h))
            if pairs:
                stage.append(pairs)
        stages.append(stage)
    return stages


def local(image, weight_one, bias_one, weight_two, bias_two, cotangent):
    _, chans, rows, cols = image.shape
    places, planes = lax.axis_size("sy"), lax.axis_size("grp")
    half = rows // 2
    width = 2 * cols
    factor = float(rows * cols * places * planes * lax.axis_size("sx")) ** (-0.5)
    call = functools.partial(pl.pallas_call, compiler_params=PARAMS)

    def rows_of(count):
        return pltpu.VMEM((count, chans, cols), BF16)

    def flat(height, count):
        return pltpu.VMEM((height, count * width), BF16)

    image_p, cot_p, swap, edges, w1, b1, w2, b2 = call(
        pack_kernel,
        out_shape=[
            rows_of(rows),
            rows_of(rows),
            rows_of(2 * half + 6),
            rows_of(6),
            pltpu.VMEM(weight_one.shape, BF16),
            pltpu.VMEM((1, chans), F32),
            pltpu.VMEM(weight_two.shape, BF16),
            pltpu.VMEM((1, chans), F32),
        ],
        in_specs=[pl.BlockSpec(memory_space=pltpu.HBM)] * 6,
        scratch_shapes=[
            pltpu.VMEM((chans, rows, cols), BF16),
            pltpu.VMEM((chans, rows, cols), BF16),
            pltpu.SemaphoreType.DMA((chans // 8 + 4,)),
        ],
        name="pack",
    )(
        *far(image, cotangent, weight_one, bias_one.reshape(1, chans)),
        *far(weight_two, bias_two.reshape(1, chans)),
    )
    swapped = lax.ppermute(swap, "sx", SWAP)
    across = []
    for s in range(places):
        for g in range(planes):
            lower, upper = 2 * s * planes + g, (2 * s + 1) * planes + g
            across.append((lower, lower - planes if s > 0 else lower ^ 1))
            across.append((upper, upper + planes if s < places - 1 else upper ^ 1))
    axes = ("sy", "sx", "grp")
    edges_other = lax.ppermute(edges, axes, across)
    edges_own = lax.ppermute(swapped[half : half + 6], axes, across)
    fwd1, fwd2, bwd2, bwd1, bias1, bias2 = call(
        weights_kernel,
        out_shape=[pltpu.VMEM((192, 192), BF16)] * 4 + [pltpu.VMEM((64, 128), F32)] * 2,
        cost_estimate=lasting(0.3),
        name="weights",
    )(*near(w1, b1, w2, b2))

    x3, h3, d3, e3, slopes, mine_a, theirs_a, grad2, grad1 = call(
        inner_kernel,
        out_shape=[
            flat(208, half + 4),
            flat(208, half + 2),
            flat(192, half),
            flat(192, half - 2),
            pltpu.VMEM((half, chans, width), F32),
            rows_of(half - 2),
            rows_of(half - 2),
            pltpu.VMEM((208, 192), F32),
            pltpu.VMEM((208, 192), F32),
        ],
        scratch_shapes=[
            pltpu.VMEM((2, half + 4, chans, cols), BF16),
            pltpu.VMEM((2, half + 2, chans, cols), BF16),
            flat(192, half),
            flat(192, half - 1),
        ],
        cost_estimate=lasting(4.0),
        name="inner",
    )(*near(image_p, cot_p, swapped, fwd1, fwd2, bwd2, bias1, bias2))
    half_grads = pltpu.VMEM((8, TILES * 128), F32)
    e3_b, mine_b, theirs_b, grads_own, grads_send = call(
        outer_kernel,
        out_shape=[flat(192, 4), rows_of(2), rows_of(2), half_grads, half_grads],
        scratch_shapes=[
            pltpu.VMEM((2, 4, chans, cols), BF16),
            pltpu.VMEM((2, 4, chans, cols), BF16),
            flat(208, 4),
            flat(208, 4),
            flat(192, 4),
            pltpu.VMEM((2, chans, width), F32),
            flat(192, 4),
            flat(192, 5),
        ],
        cost_estimate=lasting(2.0),
        name="outer",
    )(
        *near(edges_own, edges_other, cot_p, swapped, fwd1, fwd2, bwd2, bias1, bias2),
        *near(x3, h3, d3, slopes, grad2, grad1),
    )
    grads_received = lax.ppermute(grads_send, "sx", SWAP)
    mine, theirs = call(
        input_kernel,
        out_shape=[rows_of(rows), rows_of(rows)],
        cost_estimate=lasting(0.7),
        name="input",
    )(*near(e3_b, e3, bwd1, mine_a, mine_b, theirs_a, theirs_b))
    held, theirs = call(
        pair_kernel,
        out_shape=[pltpu.VMEM((8, TILES * 128), BF16), rows_of(rows)],
        input_output_aliases={0: 1},
        name="pair",
    )(*near(theirs, grads_own, grads_received))
    back = lax.ppermute(theirs, "sx", SWAP)
    out, image_grad, done = call(
        outputs_kernel,
        out_shape=[shape_of(image.shape, BF16)] * 2 + [pltpu.VMEM((8, 128), F32)],
        scratch_shapes=[pltpu.VMEM((2, rows, chans, cols), BF16)],
        cost_estimate=lasting(1.3),
        name="outputs",
    )(*near(mine, back))
    stages = exchange_stages(places, planes)
    for n, stage in enumerate(stages):
        final = n == len(stages) - 1
        received = [lax.ppermute(held, axes, pairs) for pairs in stage]
        add = functools.partial(add_kernel, factor if final else 1.0)
        behind = [done] if n == 0 else []
        held = call(
            functools.partial(behind_add, add) if behind else add,
            out_shape=pltpu.VMEM((8, TILES * 128), F32 if final else BF16),
            name="add",
        )(*near(*behind, held, *received))
    swapped_sums = lax.ppermute(held, "sx", SWAP)
    weight_shape = shape_of((3, 3, chans, chans), F32)
    bias_shape = shape_of((1, chans), F32)
    gw1, gb1, gw2, gb2 = call(
        grads_kernel,
        out_shape=[weight_shape, bias_shape, weight_shape, bias_shape],
        name="grads",
    )(*near(held, swapped_sums))
    return out, image_grad, gw1, gb1.reshape(chans), gw2, gb2.reshape(chans)


def solution(mesh):
    return jax.shard_map(
        local,
        mesh=mesh,
        in_specs=(P("grp", None, "sy", "sx"), P(), P(), P(), P(), P("grp", None, "sy", "sx")),
        out_specs=(P("grp", None, "sy", "sx"), P("grp", None, "sy", "sx"), P(), P(), P(), P()),
        check_vma=False,
    )
```

```python
import functools

import jax
import jax.numpy as jnp
from jax import lax
from jax.experimental import pallas as pl
from jax.experimental.pallas import tpu as pltpu
from jax.sharding import PartitionSpec as P

BF16 = jnp.bfloat16
F32 = jnp.float32
PARAMS = pltpu.CompilerParams(vmem_limit_bytes=32 * 1024 * 1024)
SWAP = [(0, 1), (1, 0)]
CONTRACT = (((1,), (1,)), ((), ()))
TILES = 37


def half_of(side, place, plane):
    bits = place ^ plane
    return (side ^ (bits >> 1) ^ (bits >> 3)) & 1


def own_half():
    return half_of(lax.axis_index("sx"), lax.axis_index("sy"), lax.axis_index("grp"))


def shape_of(shape, dtype):
    return jax.ShapeDtypeStruct(shape, dtype)


def near(*arrays):
    return [pltpu.with_memory_space_constraint(array, pltpu.VMEM) for array in arrays]


def far(*arrays):
    return [pltpu.with_memory_space_constraint(array, pltpu.HBM) for array in arrays]


def lasting(micros):
    return pl.CostEstimate(flops=int(micros * 1.1e9), transcendentals=0, bytes_accessed=0)


def turned(side, index, count):
    return index + side * (count - 1 - 2 * index)


def pack_kernel(
    image_ref,
    cot_ref,
    w1,
    b1,
    w2,
    b2,
    image_p,
    cot_p,
    swap,
    edges,
    w1_v,
    b1_v,
    w2_v,
    b2_v,
    image_v,
    cot_v,
    sems,
):
    side = lax.axis_index("sx")
    rows = image_ref.shape[2]
    half = rows // 2
    jobs, small = [], []
    sources = ((image_ref, image_v, image_p), (cot_ref, cot_v, cot_p))
    for c in range(image_ref.shape[1] // 16):
        chans = slice(16 * c, 16 * c + 16)
        for n, (src, dst, out) in enumerate(sources):
            copy = pltpu.make_async_copy(src.at[0, chans], dst.at[chans], sems.at[2 * c + n])
            copy.start()
            jobs.append((copy, chans, dst, out))
    for n, (src, dst) in enumerate(((w1, w1_v), (b1, b1_v), (w2, w2_v), (b2, b2_v))):
        small.append(pltpu.make_async_copy(src, dst, sems.at[len(jobs) + n]))
    for m, (copy, chans, dst, out) in enumerate(jobs):
        copy.wait()
        if m == len(jobs) // 2 - 1:
            for late in small:
                late.start()
        block = jnp.transpose(dst[chans], (1, 0, 2))
        for h in range(rows):
            out[turned(side, h, rows), chans, :] = block[h]
    swap[0 : half + 4] = image_p[half - 4 : rows]
    for k in range(half + 2):
        swap[half + 4 + k] = cot_p[rows - 1 - k]
    for k in range(4):
        edges[k] = image_p[3 - k]
    edges[4:6] = cot_p[0:2]
    for copy in small:
        copy.wait()


def column(row):
    chans = row.shape[1]
    r = lax.broadcasted_iota(jnp.int32, (chans, chans), 0)
    c = lax.broadcasted_iota(jnp.int32, (chans, chans), 1)
    wide = jnp.broadcast_to(row, (chans, chans))
    return jnp.sum(jnp.where(r == c, wide, 0.0), axis=1, keepdims=True)


def weights_kernel(w1, b1, w2, b2, fwd1, fwd2, bwd2, bwd1, bias1, bias2):
    side = lax.axis_index("sx")
    for w, fwd, bwd in ((w1, fwd1, bwd1), (w2, fwd2, bwd2)):
        for a in range(3):
            tap = turned(side, a, 3)
            fwd[a * 64 : a * 64 + 64, :] = jnp.concatenate(
                [jnp.transpose(w[tap, b].astype(F32)) for b in range(3)], axis=1
            ).astype(BF16)
            bwd[a * 64 : a * 64 + 64, :] = jnp.concatenate(
                [w[2 - tap, 2 - b].astype(F32) for b in range(3)], axis=1
            ).astype(BF16)
    bias1[...] = jnp.broadcast_to(column(b1[...]), bias1.shape)
    bias2[...] = jnp.broadcast_to(column(b2[...]), bias2.shape)


def spread(dst, at, row):
    chans, width = row.shape
    zero = jnp.zeros((chans, 1), row.dtype)
    cols = slice(at * width, (at + 1) * width)
    dst[0:chans, cols] = jnp.concatenate([zero, row[:, :-1]], axis=1)
    dst[chans : 2 * chans, cols] = row
    dst[2 * chans : 3 * chans, cols] = jnp.concatenate([row[:, 1:], zero], axis=1)


def sweep(weight_ref, rows, first, emit):
    weight = weight_ref[...]
    upper = lower = None
    for n, (ref, at) in enumerate(rows):
        part = jnp.dot(weight, ref.spread_row(at), preferred_element_type=F32)
        if n >= 2:
            emit(first + n - 1, upper + part[128:192])
        upper = part[64:128] if lower is None else lower + part[64:128]
        lower = part[0:64]


class Rows:
    def __init__(self, ref, width):
        self.ref, self.width = ref, width

    def spread_row(self, at):
        return self.ref[0:192, at * self.width : (at + 1) * self.width]

    def span(self, start, stop):
        return self.ref[:, start * self.width : stop * self.width]


def joined(width, outer, start, inner, split, first, count):
    outer, inner = Rows(outer, width), Rows(inner, width)
    return [
        (outer, e - start) if e < split else (inner, e - split)
        for e in range(first, first + count)
    ]


def silu_and_slope(pre):
    gate = 0.5 + 0.5 * jnp.tanh(0.5 * pre)
    value = pre * gate
    return value, gate + value * (1.0 - gate)


def clear(side, taps, width, start, stop, j0, j1):
    for a in range(3):
        place = pl.ds(pl.multiple_of(64 * turned(side, a, 3), 64), 64)
        for q in range(start, stop):
            if not j0 <= q - a < j1:
                at = q - start
                taps[place, at * width : (at + 1) * width] = jnp.zeros((64, width), BF16)


def store_taps(side, taps, width, start, j, delta):
    for a in range(3):
        place = pl.ds(pl.multiple_of(64 * turned(side, a, 3), 64), 64)
        at = j + a - start
        taps[place, at * width : (at + 1) * width] = delta


def hand_out(side, mine, theirs, at, value):
    width = value.shape[1]
    left, right = value[:, : width // 2], value[:, width // 2 :]
    mine[at] = jnp.where(side == 0, left, right).astype(BF16)
    theirs[at] = jnp.where(side == 0, right, left).astype(BF16)


def inner_kernel(
    image_p,
    cot_p,
    swapped,
    fwd1,
    fwd2,
    bwd2,
    bias1,
    bias2,
    x3,
    h3,
    d3,
    e3,
    slopes,
    mine,
    theirs,
    grad2,
    grad1,
    image_s,
    cot_s,
    taps2,
    taps1,
):
    side = lax.axis_index("sx")
    half = image_p.shape[0] // 2
    width = 2 * image_p.shape[2]
    last = half + 8
    other = 1 - side
    image_s[side] = image_p[0 : half + 4]
    cot_s[side] = cot_p[0 : half + 2]
    for p in range(half + 4):
        image_s[other, p] = swapped[half + 3 - p]
    cot_s[other] = swapped[half + 4 : 2 * half + 6]
    ones = jnp.ones((16, x3.shape[1]), BF16)
    x3[192:208, :] = ones
    h3[192:208, :] = ones[:, : h3.shape[1]]
    clear(side, taps2, width, 2, half + 2, 2, half)
    clear(side, taps1, width, 3, half + 2, 3, half)
    for p in range(half + 4):
        spread(x3, p, jnp.concatenate([image_s[0, p], image_s[1, p]], axis=1))
    shift1 = jnp.broadcast_to(bias1[:, 0:1], (64, width))
    shift2 = jnp.broadcast_to(bias2[:, 0:1], (64, width))

    def first(e, acc):
        hidden, slope = silu_and_slope(acc + shift1)
        spread(h3, e - 5, hidden.astype(BF16))
        if e < half + 5:
            slopes[e - 5] = slope

    x_rows, h_rows = Rows(x3, width), Rows(h3, width)
    sweep(fwd1, [(x_rows, e - 4) for e in range(4, last)], 4, first)

    def second(e, acc):
        value, slope = silu_and_slope(acc + shift2)
        cot = jnp.concatenate([cot_s[0, e - 4], cot_s[1, e - 4]], axis=1).astype(F32)
        delta = (cot * slope).astype(BF16)
        spread(d3, e - 6, delta)
        if e < half + 4:
            hand_out(side, mine, theirs, e - 6, value)
            store_taps(side, taps2, width, 2, e - 4, delta)

    sweep(fwd2, [(h_rows, e - 5) for e in range(5, last - 1)], 5, second)

    def third(e, acc):
        delta = (acc * slopes[e - 5]).astype(BF16)
        spread(e3, e - 7, delta)
        if e < half + 4:
            store_taps(side, taps1, width, 3, e - 4, delta)

    sweep(bwd2, [(Rows(d3, width), e - 6) for e in range(6, last - 2)], 6, third)

    grad2[...] = lax.dot_general(
        h_rows.span(0, half), taps2[...], CONTRACT, preferred_element_type=F32
    )
    grad1[...] = lax.dot_general(
        x_rows.span(2, half + 1), taps1[...], CONTRACT, preferred_element_type=F32
    )


def outer_kernel(
    edges_own,
    edges_other,
    cot_p,
    swapped,
    fwd1,
    fwd2,
    bwd2,
    bias1,
    bias2,
    x3,
    h3,
    d3,
    slopes,
    grad2,
    grad1,
    e3_b,
    mine,
    theirs,
    grads_own,
    grads_send,
    image_s,
    cot_s,
    x3_b,
    h3_b,
    d3_b,
    slopes_b,
    taps2,
    taps1,
):
    side = lax.axis_index("sx")
    place = lax.axis_index("sy")
    half = cot_p.shape[0] // 2
    width = 2 * cot_p.shape[2]
    other = 1 - side
    outside = place == side * (lax.axis_size("sy") - 1)


    def keep(value):
        return jnp.where(outside, 0.0, value.astype(F32)).astype(BF16)

    for cols, edges in ((side, edges_own), (other, edges_other)):
        image_s[cols] = keep(edges[0:4])
        cot_s[cols, 0] = keep(edges[5])
        cot_s[cols, 1] = keep(edges[4])
    cot_s[side, 2:4] = cot_p[0:2]
    cot_s[other, 2:4] = swapped[half + 4 : half + 6]
    ones = jnp.ones((16, x3_b.shape[1]), BF16)
    x3_b[192:208, :] = ones
    h3_b[192:208, :] = ones
    clear(side, taps2, width, 0, 4, 0, 2)
    clear(side, taps1, width, 0, 5, 0, 3)
    for e in range(4):
        spread(x3_b, e, jnp.concatenate([image_s[0, e], image_s[1, e]], axis=1))
    shift1 = jnp.broadcast_to(bias1[:, 0:1], (64, width))
    shift2 = jnp.broadcast_to(bias2[:, 0:1], (64, width))

    def first(e, acc):
        hidden, slope = silu_and_slope(acc + shift1)
        if e < 4:
            hidden = jnp.where(outside, 0.0, hidden)
        spread(h3_b, e - 1, hidden.astype(BF16))
        if e >= 3:
            slopes_b[e - 3] = slope

    sweep(fwd1, joined(width, x3_b, 0, x3, 4, 0, 6), 0, first)

    def second(e, acc):
        value, slope = silu_and_slope(acc + shift2)
        cot = jnp.concatenate([cot_s[0, e - 2], cot_s[1, e - 2]], axis=1).astype(F32)
        delta = (cot * slope).astype(BF16)
        spread(d3_b, e - 2, delta)
        if e >= 4:
            hand_out(side, mine, theirs, e - 4, value)
            store_taps(side, taps2, width, 0, e - 4, delta)

    sweep(fwd2, joined(width, h3_b, 1, h3, 5, 1, 6), 1, second)

    def third(e, acc):
        delta = acc * (slopes_b[e - 3] if e < 5 else slopes[e - 5])
        if e < 4:
            delta = jnp.where(outside, 0.0, delta)
        delta = delta.astype(BF16)
        spread(e3_b, e - 3, delta)
        if e >= 4:
            store_taps(side, taps1, width, 0, e - 4, delta)

    sweep(bwd2, joined(width, d3_b, 2, d3, 6, 2, 6), 2, third)

    def product(left, right):
        return lax.dot_general(left, right, CONTRACT, preferred_element_type=F32)

    total2 = (
        grad2[...]
        + product(Rows(h3_b, width).span(2, 4), taps2[:, : 2 * width])
        + product(Rows(h3, width).span(0, 2), taps2[:, 2 * width :])
    )
    total1 = (
        grad1[...]
        + product(Rows(x3_b, width).span(3, 4), taps1[:, :width])
        + product(Rows(x3, width).span(0, 4), taps1[:, width:])
    )
    both = jnp.concatenate([total2[0:192], total1[0:192]], axis=1)
    biases = jnp.concatenate([total2[192:200, 64:128], total1[192:200, 64:128]], axis=1)
    tiles = [
        both[8 * (t // 3) : 8 * (t // 3) + 8, 128 * (t % 3) : 128 * (t % 3) + 128]
        for t in range(72)
    ]
    empty = jnp.zeros((8, 128), F32)
    own = own_half()
    low, high = tiles[:36] + [biases], tiles[36:] + [empty]
    for t in range(TILES):
        at = slice(128 * t, 128 * t + 128)
        grads_own[:, at] = jnp.where(own == 0, low[t], high[t])
        grads_send[:, at] = jnp.where(own == 0, high[t], low[t])


def pair_kernel(passed, own, received, out, through):
    out[...] = (own[...] + received[...]).astype(BF16)


def add_kernel(factor, *refs):
    out = refs[-1]
    terms = [ref[...].astype(F32) for ref in refs[:-1]]
    while len(terms) > 1:
        terms = [sum(terms[n + 1 : n + 2], terms[n]) for n in range(0, len(terms), 2)]
    out[...] = (terms[0] * factor).astype(out.dtype)


def behind_add(add, done, *refs):
    add(*refs)


def input_kernel(e3_b, e3, bwd1, mine_a, mine_b, theirs_a, theirs_b, mine, theirs):
    side = lax.axis_index("sx")
    half = mine.shape[0] // 2
    width = 2 * mine.shape[2]
    for whole, inner, outer in ((mine, mine_a, mine_b), (theirs, theirs_a, theirs_b)):
        whole[0:2] = outer[...]
        whole[2:half] = inner[...]

    def emit(e, acc):
        hand_out(side, mine, theirs, half + e - 4, acc)

    sweep(bwd1, joined(width, e3_b, 3, e3, 7, 3, half + 2), 3, emit)


def outputs_kernel(mine, back, out, image_grad, token, natural):
    side = lax.axis_index("sx")
    rows = out.shape[2]
    half = rows // 2
    for slot in range(2):
        for j in range(half):
            natural[slot, turned(side, j, rows)] = mine[slot * half + j]
            natural[slot, turned(side, rows - 1 - j, rows)] = back[slot * half + j]
    for slot, ref in ((0, out), (1, image_grad)):
        ref[0] = jnp.transpose(natural[slot], (1, 0, 2))
    token[...] = jnp.zeros(token.shape, F32)


def grads_kernel(held, swapped, gw1, gb1, gw2, gb2):
    own = own_half()

    def tile(part, t):
        at = slice(128 * t, 128 * t + 128)
        return jnp.where(own == part, held[:, at], swapped[:, at])

    for block in range(24):
        part, first = block // 12, 3 * (block % 12)
        line = jnp.concatenate([tile(part, first + p) for p in range(3)], axis=1)
        b, i = block // 8, (block % 8) * 8
        for a in range(3):
            gw2[a, b, i : i + 8, :] = line[:, a * 64 : a * 64 + 64]
            gw1[a, b, i : i + 8, :] = line[:, 192 + a * 64 : 256 + a * 64]
    biases = tile(0, 36)
    gb2[...] = biases[0:1, 0:64]
    gb1[...] = biases[0:1, 64:128]


def exchange_stages(places, planes):
    def groups(count, axis):
        bits = [1 << k for k in range(count.bit_length() - 1)]
        pairs = [bits[k : k + 2] for k in range(0, len(bits), 2)]
        return [(axis, [b[0]] + ([b[1], b[0] | b[1]] if len(b) == 2 else [])) for b in pairs]

    rows, slides = groups(places, 0), groups(planes, 1)
    stages = []
    for plan in zip(rows + slides, slides + rows):
        stage = []
        for k in range(3):
            pairs = []
            for s in range(places):
                for x in range(2):
                    for g in range(planes):
                        part = half_of(x, s, g)
                        axis, masks = plan[part]
                        if k < len(masks):
                            t, h = (s ^ masks[k], g) if axis == 0 else (s, g ^ masks[k])
                            y = half_of(part, t, h)
                            pairs.append(((2 * s + x) * planes + g, (2 * t + y) * planes + h))
            if pairs:
                stage.append(pairs)
        stages.append(stage)
    return stages


def local(image, weight_one, bias_one, weight_two, bias_two, cotangent):
    _, chans, rows, cols = image.shape
    places, planes = lax.axis_size("sy"), lax.axis_size("grp")
    half = rows // 2
    width = 2 * cols
    factor = float(rows * cols * places * planes * lax.axis_size("sx")) ** (-0.5)
    call = functools.partial(pl.pallas_call, compiler_params=PARAMS)

    def rows_of(count):
        return pltpu.VMEM((count, chans, cols), BF16)

    def flat(height, count):
        return pltpu.VMEM((height, count * width), BF16)

    image_p, cot_p, swap, edges, w1, b1, w2, b2 = call(
        pack_kernel,
        out_shape=[
            rows_of(rows),
            rows_of(rows),
            rows_of(2 * half + 6),
            rows_of(6),
            pltpu.VMEM(weight_one.shape, BF16),
            pltpu.VMEM((1, chans), F32),
            pltpu.VMEM(weight_two.shape, BF16),
            pltpu.VMEM((1, chans), F32),
        ],
        in_specs=[pl.BlockSpec(memory_space=pltpu.HBM)] * 6,
        scratch_shapes=[
            pltpu.VMEM((chans, rows, cols), BF16),
            pltpu.VMEM((chans, rows, cols), BF16),
            pltpu.SemaphoreType.DMA((chans // 8 + 4,)),
        ],
        name="pack",
    )(
        *far(image, cotangent, weight_one, bias_one.reshape(1, chans)),
        *far(weight_two, bias_two.reshape(1, chans)),
    )
    swapped = lax.ppermute(swap, "sx", SWAP)
    across = []
    for s in range(places):
        for g in range(planes):
            lower, upper = 2 * s * planes + g, (2 * s + 1) * planes + g
            across.append((lower, lower - planes if s > 0 else lower ^ 1))
            across.append((upper, upper + planes if s < places - 1 else upper ^ 1))
    axes = ("sy", "sx", "grp")
    edges_other = lax.ppermute(edges, axes, across)
    edges_own = lax.ppermute(swapped[half : half + 6], axes, across)
    fwd1, fwd2, bwd2, bwd1, bias1, bias2 = call(
        weights_kernel,
        out_shape=[pltpu.VMEM((192, 192), BF16)] * 4 + [pltpu.VMEM((64, 128), F32)] * 2,
        cost_estimate=lasting(0.3),
        name="weights",
    )(*near(w1, b1, w2, b2))

    x3, h3, d3, e3, slopes, mine_a, theirs_a, grad2, grad1 = call(
        inner_kernel,
        out_shape=[
            flat(208, half + 4),
            flat(208, half + 2),
            flat(192, half),
            flat(192, half - 2),
            pltpu.VMEM((half, chans, width), F32),
            rows_of(half - 2),
            rows_of(half - 2),
            pltpu.VMEM((208, 192), F32),
            pltpu.VMEM((208, 192), F32),
        ],
        scratch_shapes=[
            pltpu.VMEM((2, half + 4, chans, cols), BF16),
            pltpu.VMEM((2, half + 2, chans, cols), BF16),
            flat(192, half),
            flat(192, half - 1),
        ],
        cost_estimate=lasting(4.0),
        name="inner",
    )(*near(image_p, cot_p, swapped, fwd1, fwd2, bwd2, bias1, bias2))
    half_grads = pltpu.VMEM((8, TILES * 128), F32)
    e3_b, mine_b, theirs_b, grads_own, grads_send = call(
        outer_kernel,
        out_shape=[flat(192, 4), rows_of(2), rows_of(2), half_grads, half_grads],
        scratch_shapes=[
            pltpu.VMEM((2, 4, chans, cols), BF16),
            pltpu.VMEM((2, 4, chans, cols), BF16),
            flat(208, 4),
            flat(208, 4),
            flat(192, 4),
            pltpu.VMEM((2, chans, width), F32),
            flat(192, 4),
            flat(192, 5),
        ],
        cost_estimate=lasting(2.0),
        name="outer",
    )(
        *near(edges_own, edges_other, cot_p, swapped, fwd1, fwd2, bwd2, bias1, bias2),
        *near(x3, h3, d3, slopes, grad2, grad1),
    )
    grads_received = lax.ppermute(grads_send, "sx", SWAP)
    mine, theirs = call(
        input_kernel,
        out_shape=[rows_of(rows), rows_of(rows)],
        cost_estimate=lasting(0.7),
        name="input",
    )(*near(e3_b, e3, bwd1, mine_a, mine_b, theirs_a, theirs_b))
    held, theirs = call(
        pair_kernel,
        out_shape=[pltpu.VMEM((8, TILES * 128), BF16), rows_of(rows)],
        input_output_aliases={0: 1},
        name="pair",
    )(*near(theirs, grads_own, grads_received))
    back = lax.ppermute(theirs, "sx", SWAP)
    out, image_grad, done = call(
        outputs_kernel,
        out_shape=[shape_of(image.shape, BF16)] * 2 + [pltpu.VMEM((8, 128), F32)],
        scratch_shapes=[pltpu.VMEM((2, rows, chans, cols), BF16)],
        cost_estimate=lasting(1.3),
        name="outputs",
    )(*near(mine, back))
    stages = exchange_stages(places, planes)
    for n, stage in enumerate(stages):
        final = n == len(stages) - 1
        received = [lax.ppermute(held, axes, pairs) for pairs in stage]
        add = functools.partial(add_kernel, factor if final else 1.0)
        behind = [done] if n == 0 else []
        held = call(
            functools.partial(behind_add, add) if behind else add,
            out_shape=pltpu.VMEM((8, TILES * 128), F32 if final else BF16),
            name="add",
        )(*near(*behind, held, *received))
    swapped_sums = lax.ppermute(held, "sx", SWAP)
    weight_shape = shape_of((3, 3, chans, chans), F32)
    bias_shape = shape_of((1, chans), F32)
    gw1, gb1, gw2, gb2 = call(
        grads_kernel,
        out_shape=[weight_shape, bias_shape, weight_shape, bias_shape],
        name="grads",
    )(*near(held, swapped_sums))
    return out, image_grad, gw1, gb1.reshape(chans), gw2, gb2.reshape(chans)


def solution(mesh):
    return jax.shard_map(
        local,
        mesh=mesh,
        in_specs=(P("grp", None, "sy", "sx"), P(), P(), P(), P(), P("grp", None, "sy", "sx")),
        out_specs=(P("grp", None, "sy", "sx"), P("grp", None, "sy", "sx"), P(), P(), P(), P()),
        check_vma=False,
    )
```

```python
import functools

import jax
import jax.numpy as jnp
from jax import lax
from jax.experimental import pallas as pl
from jax.experimental.pallas import tpu as pltpu
from jax.sharding import PartitionSpec as P

BF16 = jnp.bfloat16
F32 = jnp.float32
PARAMS = pltpu.CompilerParams(vmem_limit_bytes=32 * 1024 * 1024)
SWAP = [(0, 1), (1, 0)]
CONTRACT = (((1,), (1,)), ((), ()))
TILES = 37


def half_of(side, place, plane):
    bits = place ^ plane
    return (side ^ bits ^ (bits >> 1) ^ (bits >> 2) ^ (bits >> 3)) & 1


def own_half():
    return half_of(lax.axis_index("sx"), lax.axis_index("sy"), lax.axis_index("grp"))


def shape_of(shape, dtype):
    return jax.ShapeDtypeStruct(shape, dtype)


def near(*arrays):
    return [pltpu.with_memory_space_constraint(array, pltpu.VMEM) for array in arrays]


def far(*arrays):
    return [pltpu.with_memory_space_constraint(array, pltpu.HBM) for array in arrays]


def lasting(micros):
    return pl.CostEstimate(flops=int(micros * 1.1e9), transcendentals=0, bytes_accessed=0)


def turned(side, index, count):
    return index + side * (count - 1 - 2 * index)


def cut_edges(image_p, cot_p, edges):
    for k in range(4):
        edges[k] = image_p[3 - k]
    edges[4:6] = cot_p[0:2]


def repack_kernel(image, cot, image_p, cot_p, edges):
    side = lax.axis_index("sx")
    rows = image.shape[2]
    for src, out in ((image, image_p), (cot, cot_p)):
        for c in range(image.shape[1] // 16):
            chans = slice(16 * c, 16 * c + 16)
            block = jnp.transpose(src[0, chans], (1, 0, 2))
            for h in range(rows):
                out[turned(side, h, rows), chans, :] = block[h]
    cut_edges(image_p, cot_p, edges)


def pack_kernel(
    image_ref,
    cot_ref,
    w1,
    b1,
    w2,
    b2,
    image_p,
    cot_p,
    edges,
    w1_v,
    b1_v,
    w2_v,
    b2_v,
    image_v,
    cot_v,
    sems,
):
    side = lax.axis_index("sx")
    rows = image_ref.shape[2]
    jobs, small = [], []
    sources = ((image_ref, image_v, image_p), (cot_ref, cot_v, cot_p))
    for c in range(image_ref.shape[1] // 16):
        chans = slice(16 * c, 16 * c + 16)
        for n, (src, dst, out) in enumerate(sources):
            copy = pltpu.make_async_copy(src.at[0, chans], dst.at[chans], sems.at[2 * c + n])
            copy.start()
            jobs.append((copy, chans, dst, out))
    for n, (src, dst) in enumerate(((w1, w1_v), (b1, b1_v), (w2, w2_v), (b2, b2_v))):
        copy = pltpu.make_async_copy(src, dst, sems.at[len(jobs) + n])
        copy.start()
        small.append(copy)
    for copy, chans, dst, out in jobs:
        copy.wait()
        block = jnp.transpose(dst[chans], (1, 0, 2))
        for h in range(rows):
            out[turned(side, h, rows), chans, :] = block[h]
    cut_edges(image_p, cot_p, edges)
    for copy in small:
        copy.wait()


def column(row):
    chans = row.shape[1]
    r = lax.broadcasted_iota(jnp.int32, (chans, chans), 0)
    c = lax.broadcasted_iota(jnp.int32, (chans, chans), 1)
    wide = jnp.broadcast_to(row, (chans, chans))
    return jnp.sum(jnp.where(r == c, wide, 0.0), axis=1, keepdims=True)


def weights_kernel(w1, b1, w2, b2, fwd1, fwd2, bwd2, bwd1, bias1, bias2):
    side = lax.axis_index("sx")
    for w, fwd, bwd in ((w1, fwd1, bwd1), (w2, fwd2, bwd2)):
        for a in range(3):
            tap = turned(side, a, 3)
            fwd[a * 64 : a * 64 + 64, :] = jnp.concatenate(
                [jnp.transpose(w[tap, b].astype(F32)) for b in range(3)], axis=1
            ).astype(BF16)
            bwd[a * 64 : a * 64 + 64, :] = jnp.concatenate(
                [w[2 - tap, 2 - b].astype(F32) for b in range(3)], axis=1
            ).astype(BF16)
    bias1[...] = jnp.broadcast_to(column(b1[...]), bias1.shape)
    bias2[...] = jnp.broadcast_to(column(b2[...]), bias2.shape)


def spread(dst, at, row):
    chans, width = row.shape
    zero = jnp.zeros((chans, 1), row.dtype)
    cols = slice(at * width, (at + 1) * width)
    dst[0:chans, cols] = jnp.concatenate([zero, row[:, :-1]], axis=1)
    dst[chans : 2 * chans, cols] = row
    dst[2 * chans : 3 * chans, cols] = jnp.concatenate([row[:, 1:], zero], axis=1)


def sweep(weight_ref, rows, first, emit):
    weight = weight_ref[...]
    upper = lower = None
    for n, (ref, at) in enumerate(rows):
        part = jnp.dot(weight, ref.spread_row(at), preferred_element_type=F32)
        if n >= 2:
            emit(first + n - 1, upper + part[128:192])
        upper = part[64:128] if lower is None else lower + part[64:128]
        lower = part[0:64]


class Rows:
    def __init__(self, ref, width):
        self.ref, self.width = ref, width

    def spread_row(self, at):
        return self.ref[0:192, at * self.width : (at + 1) * self.width]

    def span(self, start, stop):
        return self.ref[:, start * self.width : stop * self.width]


def joined(width, outer, start, inner, split, first, count):
    outer, inner = Rows(outer, width), Rows(inner, width)
    return [
        (outer, e - start) if e < split else (inner, e - split)
        for e in range(first, first + count)
    ]


def silu_and_slope(pre):
    gate = 0.5 + 0.5 * jnp.tanh(0.5 * pre)
    value = pre * gate
    return value, gate + value * (1.0 - gate)


def clear(side, taps, width, start, stop, j0, j1):
    for a in range(3):
        place = pl.ds(pl.multiple_of(64 * turned(side, a, 3), 64), 64)
        for q in range(start, stop):
            if not j0 <= q - a < j1:
                at = q - start
                taps[place, at * width : (at + 1) * width] = jnp.zeros((64, width), BF16)


def store_taps(side, taps, width, start, j, delta):
    for a in range(3):
        place = pl.ds(pl.multiple_of(64 * turned(side, a, 3), 64), 64)
        at = j + a - start
        taps[place, at * width : (at + 1) * width] = delta


def hand_out(side, mine, theirs, at, value):
    width = value.shape[1]
    left, right = value[:, : width // 2], value[:, width // 2 :]
    mine[at] = jnp.where(side == 0, left, right).astype(BF16)
    theirs[at] = jnp.where(side == 0, right, left).astype(BF16)


def inner_kernel(
    image_p,
    cot_p,
    image_o,
    cot_o,
    fwd1,
    fwd2,
    bwd2,
    bias1,
    bias2,
    x3,
    h3,
    d3,
    e3,
    slopes,
    mine,
    theirs,
    grad2,
    grad1,
    image_s,
    cot_s,
    taps2,
    taps1,
):
    side = lax.axis_index("sx")
    half = image_p.shape[0] // 2
    width = 2 * image_p.shape[2]
    last = half + 8
    other = 1 - side
    image_s[side] = image_p[0 : half + 4]
    cot_s[side] = cot_p[0 : half + 2]
    image_s[other] = image_o[0 : half + 4]
    cot_s[other] = cot_o[0 : half + 2]
    ones = jnp.ones((16, x3.shape[1]), BF16)
    x3[192:208, :] = ones
    h3[192:208, :] = ones[:, : h3.shape[1]]
    clear(side, taps2, width, 2, half + 2, 2, half)
    clear(side, taps1, width, 3, half + 2, 3, half)
    for p in range(half + 4):
        spread(x3, p, jnp.concatenate([image_s[0, p], image_s[1, p]], axis=1))
    shift1 = jnp.broadcast_to(bias1[:, 0:1], (64, width))
    shift2 = jnp.broadcast_to(bias2[:, 0:1], (64, width))

    def first(e, acc):
        hidden, slope = silu_and_slope(acc + shift1)
        spread(h3, e - 5, hidden.astype(BF16))
        if e < half + 5:
            slopes[e - 5] = slope

    x_rows, h_rows = Rows(x3, width), Rows(h3, width)
    sweep(fwd1, [(x_rows, e - 4) for e in range(4, last)], 4, first)

    def second(e, acc):
        value, slope = silu_and_slope(acc + shift2)
        cot = jnp.concatenate([cot_s[0, e - 4], cot_s[1, e - 4]], axis=1).astype(F32)
        delta = (cot * slope).astype(BF16)
        spread(d3, e - 6, delta)
        if e < half + 4:
            hand_out(side, mine, theirs, e - 6, value)
            store_taps(side, taps2, width, 2, e - 4, delta)

    sweep(fwd2, [(h_rows, e - 5) for e in range(5, last - 1)], 5, second)

    def third(e, acc):
        delta = (acc * slopes[e - 5]).astype(BF16)
        spread(e3, e - 7, delta)
        if e < half + 4:
            store_taps(side, taps1, width, 3, e - 4, delta)

    sweep(bwd2, [(Rows(d3, width), e - 6) for e in range(6, last - 2)], 6, third)

    grad2[...] = lax.dot_general(
        h_rows.span(0, half), taps2[...], CONTRACT, preferred_element_type=F32
    )
    grad1[...] = lax.dot_general(
        x_rows.span(2, half + 1), taps1[...], CONTRACT, preferred_element_type=F32
    )


def outer_kernel(
    edges_own,
    edges_other,
    cot_p,
    cot_o,
    fwd1,
    fwd2,
    bwd2,
    bias1,
    bias2,
    x3,
    h3,
    d3,
    slopes,
    grad2,
    grad1,
    e3_b,
    mine,
    theirs,
    grads_own,
    grads_send,
    image_s,
    cot_s,
    x3_b,
    h3_b,
    d3_b,
    slopes_b,
    taps2,
    taps1,
):
    side = lax.axis_index("sx")
    place = lax.axis_index("sy")
    half = cot_p.shape[0] // 2
    width = 2 * cot_p.shape[2]
    other = 1 - side
    outside = place == side * (lax.axis_size("sy") - 1)


    def keep(value):
        return jnp.where(outside, 0.0, value.astype(F32)).astype(BF16)

    for cols, edges in ((side, edges_own), (other, edges_other)):
        image_s[cols] = keep(edges[0:4])
        cot_s[cols, 0] = keep(edges[5])
        cot_s[cols, 1] = keep(edges[4])
    cot_s[side, 2:4] = cot_p[0:2]
    cot_s[other, 2:4] = cot_o[0:2]
    ones = jnp.ones((16, x3_b.shape[1]), BF16)
    x3_b[192:208, :] = ones
    h3_b[192:208, :] = ones
    clear(side, taps2, width, 0, 4, 0, 2)
    clear(side, taps1, width, 0, 5, 0, 3)
    for e in range(4):
        spread(x3_b, e, jnp.concatenate([image_s[0, e], image_s[1, e]], axis=1))
    shift1 = jnp.broadcast_to(bias1[:, 0:1], (64, width))
    shift2 = jnp.broadcast_to(bias2[:, 0:1], (64, width))

    def first(e, acc):
        hidden, slope = silu_and_slope(acc + shift1)
        if e < 4:
            hidden = jnp.where(outside, 0.0, hidden)
        spread(h3_b, e - 1, hidden.astype(BF16))
        if e >= 3:
            slopes_b[e - 3] = slope

    sweep(fwd1, joined(width, x3_b, 0, x3, 4, 0, 6), 0, first)

    def second(e, acc):
        value, slope = silu_and_slope(acc + shift2)
        cot = jnp.concatenate([cot_s[0, e - 2], cot_s[1, e - 2]], axis=1).astype(F32)
        delta = (cot * slope).astype(BF16)
        spread(d3_b, e - 2, delta)
        if e >= 4:
            hand_out(side, mine, theirs, e - 4, value)
            store_taps(side, taps2, width, 0, e - 4, delta)

    sweep(fwd2, joined(width, h3_b, 1, h3, 5, 1, 6), 1, second)

    def third(e, acc):
        delta = acc * (slopes_b[e - 3] if e < 5 else slopes[e - 5])
        if e < 4:
            delta = jnp.where(outside, 0.0, delta)
        delta = delta.astype(BF16)
        spread(e3_b, e - 3, delta)
        if e >= 4:
            store_taps(side, taps1, width, 0, e - 4, delta)

    sweep(bwd2, joined(width, d3_b, 2, d3, 6, 2, 6), 2, third)

    def product(left, right):
        return lax.dot_general(left, right, CONTRACT, preferred_element_type=F32)

    total2 = (
        grad2[...]
        + product(Rows(h3_b, width).span(2, 4), taps2[:, : 2 * width])
        + product(Rows(h3, width).span(0, 2), taps2[:, 2 * width :])
    )
    total1 = (
        grad1[...]
        + product(Rows(x3_b, width).span(3, 4), taps1[:, :width])
        + product(Rows(x3, width).span(0, 4), taps1[:, width:])
    )
    both = jnp.concatenate([total2[0:192], total1[0:192]], axis=1)
    biases = jnp.concatenate([total2[192:200, 64:128], total1[192:200, 64:128]], axis=1)
    tiles = [
        both[8 * (t // 3) : 8 * (t // 3) + 8, 128 * (t % 3) : 128 * (t % 3) + 128]
        for t in range(72)
    ]
    empty = jnp.zeros((8, 128), F32)
    own = own_half()
    low, high = tiles[:36] + [biases], tiles[36:] + [empty]
    for t in range(TILES):
        at = slice(128 * t, 128 * t + 128)
        grads_own[:, at] = jnp.where(own == 0, low[t], high[t])
        grads_send[:, at] = jnp.where(own == 0, high[t], low[t])


def pair_kernel(passed, own, received, out, through):
    out[...] = (own[...] + received[...]).astype(BF16)


def add_kernel(factor, *refs):
    out = refs[-1]
    terms = [ref[...].astype(F32) for ref in refs[:-1]]
    while len(terms) > 1:
        terms = [sum(terms[n + 1 : n + 2], terms[n]) for n in range(0, len(terms), 2)]
    out[...] = (terms[0] * factor).astype(out.dtype)


def behind_add(add, done, *refs):
    add(*refs)


def input_kernel(e3_b, e3, bwd1, mine_a, mine_b, theirs_a, theirs_b, mine, theirs):
    side = lax.axis_index("sx")
    half = mine.shape[0] // 2
    width = 2 * mine.shape[2]
    for whole, inner, outer in ((mine, mine_a, mine_b), (theirs, theirs_a, theirs_b)):
        whole[0:2] = outer[...]
        whole[2:half] = inner[...]

    def emit(e, acc):
        hand_out(side, mine, theirs, half + e - 4, acc)

    sweep(bwd1, joined(width, e3_b, 3, e3, 7, 3, half + 2), 3, emit)


def outputs_kernel(mine, back, out, image_grad, token, natural):
    side = lax.axis_index("sx")
    rows = out.shape[2]
    half = rows // 2
    for slot in range(2):
        for j in range(half):
            natural[slot, turned(side, j, rows)] = mine[slot * half + j]
            natural[slot, turned(side, rows - 1 - j, rows)] = back[slot * half + j]
    for slot, ref in ((0, out), (1, image_grad)):
        ref[0] = jnp.transpose(natural[slot], (1, 0, 2))
    token[...] = jnp.zeros(token.shape, F32)


def grads_kernel(held, swapped, gw1, gb1, gw2, gb2):
    own = own_half()

    def tile(part, t):
        at = slice(128 * t, 128 * t + 128)
        return jnp.where(own == part, held[:, at], swapped[:, at])

    for block in range(24):
        part, first = block // 12, 3 * (block % 12)
        line = jnp.concatenate([tile(part, first + p) for p in range(3)], axis=1)
        b, i = block // 8, (block % 8) * 8
        for a in range(3):
            gw2[a, b, i : i + 8, :] = line[:, a * 64 : a * 64 + 64]
            gw1[a, b, i : i + 8, :] = line[:, 192 + a * 64 : 256 + a * 64]
    biases = tile(0, 36)
    gb2[...] = biases[0:1, 0:64]
    gb1[...] = biases[0:1, 64:128]


def exchange_stages(places, planes):
    def groups(count, axis):
        bits = [1 << k for k in range(count.bit_length() - 1)]
        pairs = [bits[k : k + 2] for k in range(0, len(bits), 2)]
        return [(axis, [b[0]] + ([b[1], b[0] | b[1]] if len(b) == 2 else [])) for b in pairs]

    rows, slides = groups(places, 0), groups(planes, 1)
    stages = []
    for plan in zip(rows + slides, slides + rows):
        stage = []
        for k in range(3):
            pairs = []
            for s in range(places):
                for x in range(2):
                    for g in range(planes):
                        part = half_of(x, s, g)
                        axis, masks = plan[part]
                        if k < len(masks):
                            t, h = (s ^ masks[k], g) if axis == 0 else (s, g ^ masks[k])
                            y = half_of(part, t, h)
                            pairs.append(((2 * s + x) * planes + g, (2 * t + y) * planes + h))
            if pairs:
                stage.append(pairs)
        stages.append(stage)
    return stages


def local(image, weight_one, bias_one, weight_two, bias_two, cotangent):
    _, chans, rows, cols = image.shape
    places, planes = lax.axis_size("sy"), lax.axis_size("grp")
    half = rows // 2
    width = 2 * cols
    factor = float(rows * cols * places * planes * lax.axis_size("sx")) ** (-0.5)
    call = functools.partial(pl.pallas_call, compiler_params=PARAMS)

    def rows_of(count):
        return pltpu.VMEM((count, chans, cols), BF16)

    def flat(height, count):
        return pltpu.VMEM((height, count * width), BF16)

    image_o = lax.ppermute(image, "sx", SWAP)
    cot_o = lax.ppermute(cotangent, "sx", SWAP)
    image_p, cot_p, edges, w1, b1, w2, b2 = call(
        pack_kernel,
        out_shape=[
            rows_of(rows),
            rows_of(rows),
            rows_of(6),
            pltpu.VMEM(weight_one.shape, BF16),
            pltpu.VMEM((1, chans), F32),
            pltpu.VMEM(weight_two.shape, BF16),
            pltpu.VMEM((1, chans), F32),
        ],
        in_specs=[pl.BlockSpec(memory_space=pltpu.HBM)] * 6,
        scratch_shapes=[
            pltpu.VMEM((chans, rows, cols), BF16),
            pltpu.VMEM((chans, rows, cols), BF16),
            pltpu.SemaphoreType.DMA((chans // 8 + 4,)),
        ],
        cost_estimate=lasting(1.5),
        name="pack",
    )(
        *far(image, cotangent, weight_one, bias_one.reshape(1, chans)),
        *far(weight_two, bias_two.reshape(1, chans)),
    )
    image_o, cot_o, edges_next = call(
        repack_kernel,
        out_shape=[rows_of(rows), rows_of(rows), rows_of(6)],
        cost_estimate=lasting(0.5),
        name="repack",
    )(*near(image_o, cot_o))
    across = []
    for s in range(places):
        for g in range(planes):
            lower, upper = 2 * s * planes + g, (2 * s + 1) * planes + g
            across.append((lower, lower - planes if s > 0 else lower ^ 1))
            across.append((upper, upper + planes if s < places - 1 else upper ^ 1))
    axes = ("sy", "sx", "grp")
    edges_other = lax.ppermute(edges, axes, across)
    edges_own = lax.ppermute(edges_next, axes, across)
    fwd1, fwd2, bwd2, bwd1, bias1, bias2 = call(
        weights_kernel,
        out_shape=[pltpu.VMEM((192, 192), BF16)] * 4 + [pltpu.VMEM((64, 128), F32)] * 2,
        cost_estimate=lasting(0.3),
        name="weights",
    )(*near(w1, b1, w2, b2))

    x3, h3, d3, e3, slopes, mine_a, theirs_a, grad2, grad1 = call(
        inner_kernel,
        out_shape=[
            flat(208, half + 4),
            flat(208, half + 2),
            flat(192, half),
            flat(192, half - 2),
            pltpu.VMEM((half, chans, width), F32),
            rows_of(half - 2),
            rows_of(half - 2),
            pltpu.VMEM((208, 192), F32),
            pltpu.VMEM((208, 192), F32),
        ],
        scratch_shapes=[
            pltpu.VMEM((2, half + 4, chans, cols), BF16),
            pltpu.VMEM((2, half + 2, chans, cols), BF16),
            flat(192, half),
            flat(192, half - 1),
        ],
        cost_estimate=lasting(4.0),
        name="inner",
    )(*near(image_p, cot_p, image_o, cot_o, fwd1, fwd2, bwd2, bias1, bias2))
    half_grads = pltpu.VMEM((8, TILES * 128), F32)
    e3_b, mine_b, theirs_b, grads_own, grads_send = call(
        outer_kernel,
        out_shape=[flat(192, 4), rows_of(2), rows_of(2), half_grads, half_grads],
        scratch_shapes=[
            pltpu.VMEM((2, 4, chans, cols), BF16),
            pltpu.VMEM((2, 4, chans, cols), BF16),
            flat(208, 4),
            flat(208, 4),
            flat(192, 4),
            pltpu.VMEM((2, chans, width), F32),
            flat(192, 4),
            flat(192, 5),
        ],
        cost_estimate=lasting(2.0),
        name="outer",
    )(
        *near(edges_own, edges_other, cot_p, cot_o, fwd1, fwd2, bwd2, bias1, bias2),
        *near(x3, h3, d3, slopes, grad2, grad1),
    )
    grads_received = lax.ppermute(grads_send, "sx", SWAP)
    mine, theirs = call(
        input_kernel,
        out_shape=[rows_of(rows), rows_of(rows)],
        cost_estimate=lasting(0.7),
        name="input",
    )(*near(e3_b, e3, bwd1, mine_a, mine_b, theirs_a, theirs_b))
    held, theirs = call(
        pair_kernel,
        out_shape=[pltpu.VMEM((8, TILES * 128), BF16), rows_of(rows)],
        input_output_aliases={0: 1},
        name="pair",
    )(*near(theirs, grads_own, grads_received))
    back = lax.ppermute(theirs, "sx", SWAP)
    out, image_grad, done = call(
        outputs_kernel,
        out_shape=[shape_of(image.shape, BF16)] * 2 + [pltpu.VMEM((8, 128), F32)],
        scratch_shapes=[pltpu.VMEM((2, rows, chans, cols), BF16)],
        cost_estimate=lasting(1.3),
        name="outputs",
    )(*near(mine, back))
    stages = exchange_stages(places, planes)
    for n, stage in enumerate(stages):
        final = n == len(stages) - 1
        received = [lax.ppermute(held, axes, pairs) for pairs in stage]
        add = functools.partial(add_kernel, factor if final else 1.0)
        behind = [done] if n == 0 else []
        held = call(
            functools.partial(behind_add, add) if behind else add,
            out_shape=pltpu.VMEM((8, TILES * 128), F32 if final else BF16),
            name="add",
        )(*near(*behind, held, *received))
    swapped_sums = lax.ppermute(held, "sx", SWAP)
    weight_shape = shape_of((3, 3, chans, chans), F32)
    bias_shape = shape_of((1, chans), F32)
    gw1, gb1, gw2, gb2 = call(
        grads_kernel,
        out_shape=[weight_shape, bias_shape, weight_shape, bias_shape],
        name="grads",
    )(*near(held, swapped_sums))
    return out, image_grad, gw1, gb1.reshape(chans), gw2, gb2.reshape(chans)


def solution(mesh):
    return jax.shard_map(
        local,
        mesh=mesh,
        in_specs=(P("grp", None, "sy", "sx"), P(), P(), P(), P(), P("grp", None, "sy", "sx")),
        out_specs=(P("grp", None, "sy", "sx"), P("grp", None, "sy", "sx"), P(), P(), P(), P()),
        check_vma=False,
    )
```

```python
import functools

import jax
import jax.numpy as jnp
from jax import lax
from jax.experimental import pallas as pl
from jax.experimental.pallas import tpu as pltpu
from jax.sharding import PartitionSpec as P

BF16 = jnp.bfloat16
F32 = jnp.float32
PARAMS = pltpu.CompilerParams(vmem_limit_bytes=32 * 1024 * 1024)
SWAP = [(0, 1), (1, 0)]
CONTRACT = (((1,), (1,)), ((), ()))
TILES = 37


def half_of(side, place, plane):
    bits = place ^ plane
    return (side ^ bits ^ (bits >> 1) ^ (bits >> 2) ^ (bits >> 3)) & 1


def own_half():
    return half_of(lax.axis_index("sx"), lax.axis_index("sy"), lax.axis_index("grp"))


def shape_of(shape, dtype):
    return jax.ShapeDtypeStruct(shape, dtype)


def near(*arrays):
    return [pltpu.with_memory_space_constraint(array, pltpu.VMEM) for array in arrays]


def far(*arrays):
    return [pltpu.with_memory_space_constraint(array, pltpu.HBM) for array in arrays]


def lasting(micros):
    return pl.CostEstimate(flops=int(micros * 1.1e9), transcendentals=0, bytes_accessed=0)


def turned(side, index, count):
    return index + side * (count - 1 - 2 * index)


def pack_kernel(
    image_ref,
    cot_ref,
    w1,
    b1,
    w2,
    b2,
    image_p,
    cot_p,
    swap,
    edges,
    w1_v,
    b1_v,
    w2_v,
    b2_v,
    image_v,
    cot_v,
    sems,
):
    side = lax.axis_index("sx")
    rows = image_ref.shape[2]
    half = rows // 2
    jobs, small = [], []
    sources = ((image_ref, image_v, image_p), (cot_ref, cot_v, cot_p))
    for c in range(image_ref.shape[1] // 16):
        chans = slice(16 * c, 16 * c + 16)
        for n, (src, dst, out) in enumerate(sources):
            copy = pltpu.make_async_copy(src.at[0, chans], dst.at[chans], sems.at[2 * c + n])
            copy.start()
            jobs.append((copy, chans, dst, out))
    for n, (src, dst) in enumerate(((w1, w1_v), (b1, b1_v), (w2, w2_v), (b2, b2_v))):
        copy = pltpu.make_async_copy(src, dst, sems.at[len(jobs) + n])
        copy.start()
        small.append(copy)
    for copy, chans, dst, out in jobs:
        copy.wait()
        block = jnp.transpose(dst[chans], (1, 0, 2))
        for h in range(rows):
            out[turned(side, h, rows), chans, :] = block[h]
    swap[0 : half + 4] = image_p[half - 4 : rows]
    for k in range(half + 2):
        swap[half + 4 + k] = cot_p[rows - 1 - k]
    for k in range(4):
        edges[k] = image_p[3 - k]
    edges[4:6] = cot_p[0:2]
    for copy in small:
        copy.wait()


def column(row):
    chans = row.shape[1]
    r = lax.broadcasted_iota(jnp.int32, (chans, chans), 0)
    c = lax.broadcasted_iota(jnp.int32, (chans, chans), 1)
    wide = jnp.broadcast_to(row, (chans, chans))
    return jnp.sum(jnp.where(r == c, wide, 0.0), axis=1, keepdims=True)


def weights_kernel(w1, b1, w2, b2, fwd1, fwd2, bwd2, bwd1, bias1, bias2):
    side = lax.axis_index("sx")
    for w, fwd, bwd in ((w1, fwd1, bwd1), (w2, fwd2, bwd2)):
        for a in range(3):
            tap = turned(side, a, 3)
            fwd[a * 64 : a * 64 + 64, :] = jnp.concatenate(
                [jnp.transpose(w[tap, b].astype(F32)) for b in range(3)], axis=1
            ).astype(BF16)
            bwd[a * 64 : a * 64 + 64, :] = jnp.concatenate(
                [w[2 - tap, 2 - b].astype(F32) for b in range(3)], axis=1
            ).astype(BF16)
    bias1[...] = jnp.broadcast_to(column(b1[...]), bias1.shape)
    bias2[...] = jnp.broadcast_to(column(b2[...]), bias2.shape)


def spread(dst, at, row):
    chans, width = row.shape
    zero = jnp.zeros((chans, 1), row.dtype)
    cols = slice(at * width, (at + 1) * width)
    dst[0:chans, cols] = jnp.concatenate([zero, row[:, :-1]], axis=1)
    dst[chans : 2 * chans, cols] = row
    dst[2 * chans : 3 * chans, cols] = jnp.concatenate([row[:, 1:], zero], axis=1)


def sweep(weight_ref, rows, first, emit):
    weight = weight_ref[...]
    upper = lower = None
    for n, (ref, at) in enumerate(rows):
        part = jnp.dot(weight, ref.spread_row(at), preferred_element_type=F32)
        if n >= 2:
            emit(first + n - 1, upper + part[128:192])
        upper = part[64:128] if lower is None else lower + part[64:128]
        lower = part[0:64]


class Rows:
    def __init__(self, ref, width):
        self.ref, self.width = ref, width

    def spread_row(self, at):
        return self.ref[0:192, at * self.width : (at + 1) * self.width]

    def span(self, start, stop):
        return self.ref[:, start * self.width : stop * self.width]


def joined(width, outer, start, inner, split, first, count):
    outer, inner = Rows(outer, width), Rows(inner, width)
    return [
        (outer, e - start) if e < split else (inner, e - split)
        for e in range(first, first + count)
    ]


def silu_and_slope(pre):
    gate = 0.5 + 0.5 * jnp.tanh(0.5 * pre)
    value = pre * gate
    return value, gate + value * (1.0 - gate)


def clear(side, taps, width, start, stop, j0, j1):
    for a in range(3):
        place = pl.ds(pl.multiple_of(64 * turned(side, a, 3), 64), 64)
        for q in range(start, stop):
            if not j0 <= q - a < j1:
                at = q - start
                taps[place, at * width : (at + 1) * width] = jnp.zeros((64, width), BF16)


def store_taps(side, taps, width, start, j, delta):
    for a in range(3):
        place = pl.ds(pl.multiple_of(64 * turned(side, a, 3), 64), 64)
        at = j + a - start
        taps[place, at * width : (at + 1) * width] = delta


def hand_out(side, mine, theirs, at, value):
    width = value.shape[1]
    left, right = value[:, : width // 2], value[:, width // 2 :]
    mine[at] = jnp.where(side == 0, left, right).astype(BF16)
    theirs[at] = jnp.where(side == 0, right, left).astype(BF16)


def inner_kernel(
    image_p,
    cot_p,
    swapped,
    fwd1,
    fwd2,
    bwd2,
    bias1,
    bias2,
    x3,
    h3,
    d3,
    e3,
    slopes,
    mine,
    theirs,
    grad2,
    grad1,
    image_s,
    cot_s,
    taps2,
    taps1,
):
    side = lax.axis_index("sx")
    half = image_p.shape[0] // 2
    width = 2 * image_p.shape[2]
    last = half + 8
    other = 1 - side
    image_s[side] = image_p[0 : half + 4]
    cot_s[side] = cot_p[0 : half + 2]
    for p in range(half + 4):
        image_s[other, p] = swapped[half + 3 - p]
    cot_s[other] = swapped[half + 4 : 2 * half + 6]
    ones = jnp.ones((16, x3.shape[1]), BF16)
    x3[192:208, :] = ones
    h3[192:208, :] = ones[:, : h3.shape[1]]
    clear(side, taps2, width, 2, half + 2, 2, half)
    clear(side, taps1, width, 3, half + 2, 3, half)
    for p in range(half + 4):
        spread(x3, p, jnp.concatenate([image_s[0, p], image_s[1, p]], axis=1))
    shift1 = jnp.broadcast_to(bias1[:, 0:1], (64, width))
    shift2 = jnp.broadcast_to(bias2[:, 0:1], (64, width))

    def first(e, acc):
        hidden, slope = silu_and_slope(acc + shift1)
        spread(h3, e - 5, hidden.astype(BF16))
        if e < half + 5:
            slopes[e - 5] = slope

    x_rows, h_rows = Rows(x3, width), Rows(h3, width)
    sweep(fwd1, [(x_rows, e - 4) for e in range(4, last)], 4, first)

    def second(e, acc):
        value, slope = silu_and_slope(acc + shift2)
        cot = jnp.concatenate([cot_s[0, e - 4], cot_s[1, e - 4]], axis=1).astype(F32)
        delta = (cot * slope).astype(BF16)
        spread(d3, e - 6, delta)
        if e < half + 4:
            hand_out(side, mine, theirs, e - 6, value)
            store_taps(side, taps2, width, 2, e - 4, delta)

    sweep(fwd2, [(h_rows, e - 5) for e in range(5, last - 1)], 5, second)

    def third(e, acc):
        delta = (acc * slopes[e - 5]).astype(BF16)
        spread(e3, e - 7, delta)
        if e < half + 4:
            store_taps(side, taps1, width, 3, e - 4, delta)

    sweep(bwd2, [(Rows(d3, width), e - 6) for e in range(6, last - 2)], 6, third)

    grad2[...] = lax.dot_general(
        h_rows.span(0, half), taps2[...], CONTRACT, preferred_element_type=F32
    )
    grad1[...] = lax.dot_general(
        x_rows.span(2, half + 1), taps1[...], CONTRACT, preferred_element_type=F32
    )


def outer_kernel(
    edges_own,
    edges_other,
    cot_p,
    swapped,
    fwd1,
    fwd2,
    bwd2,
    bias1,
    bias2,
    x3,
    h3,
    d3,
    slopes,
    grad2,
    grad1,
    e3_b,
    mine,
    theirs,
    grads_own,
    grads_send,
    image_s,
    cot_s,
    x3_b,
    h3_b,
    d3_b,
    slopes_b,
    taps2,
    taps1,
):
    side = lax.axis_index("sx")
    place = lax.axis_index("sy")
    half = cot_p.shape[0] // 2
    width = 2 * cot_p.shape[2]
    other = 1 - side
    outside = place == side * (lax.axis_size("sy") - 1)


    def keep(value):
        return jnp.where(outside, 0.0, value.astype(F32)).astype(BF16)

    for cols, edges in ((side, edges_own), (other, edges_other)):
        image_s[cols] = keep(edges[0:4])
        cot_s[cols, 0] = keep(edges[5])
        cot_s[cols, 1] = keep(edges[4])
    cot_s[side, 2:4] = cot_p[0:2]
    cot_s[other, 2:4] = swapped[half + 4 : half + 6]
    ones = jnp.ones((16, x3_b.shape[1]), BF16)
    x3_b[192:208, :] = ones
    h3_b[192:208, :] = ones
    clear(side, taps2, width, 0, 4, 0, 2)
    clear(side, taps1, width, 0, 5, 0, 3)
    for e in range(4):
        spread(x3_b, e, jnp.concatenate([image_s[0, e], image_s[1, e]], axis=1))
    shift1 = jnp.broadcast_to(bias1[:, 0:1], (64, width))
    shift2 = jnp.broadcast_to(bias2[:, 0:1], (64, width))

    def first(e, acc):
        hidden, slope = silu_and_slope(acc + shift1)
        if e < 4:
            hidden = jnp.where(outside, 0.0, hidden)
        spread(h3_b, e - 1, hidden.astype(BF16))
        if e >= 3:
            slopes_b[e - 3] = slope

    sweep(fwd1, joined(width, x3_b, 0, x3, 4, 0, 6), 0, first)

    def second(e, acc):
        value, slope = silu_and_slope(acc + shift2)
        cot = jnp.concatenate([cot_s[0, e - 2], cot_s[1, e - 2]], axis=1).astype(F32)
        delta = (cot * slope).astype(BF16)
        spread(d3_b, e - 2, delta)
        if e >= 4:
            hand_out(side, mine, theirs, e - 4, value)
            store_taps(side, taps2, width, 0, e - 4, delta)

    sweep(fwd2, joined(width, h3_b, 1, h3, 5, 1, 6), 1, second)

    def third(e, acc):
        delta = acc * (slopes_b[e - 3] if e < 5 else slopes[e - 5])
        if e < 4:
            delta = jnp.where(outside, 0.0, delta)
        delta = delta.astype(BF16)
        spread(e3_b, e - 3, delta)
        if e >= 4:
            store_taps(side, taps1, width, 0, e - 4, delta)

    sweep(bwd2, joined(width, d3_b, 2, d3, 6, 2, 6), 2, third)

    def product(left, right):
        return lax.dot_general(left, right, CONTRACT, preferred_element_type=F32)

    total2 = (
        grad2[...]
        + product(Rows(h3_b, width).span(2, 4), taps2[:, : 2 * width])
        + product(Rows(h3, width).span(0, 2), taps2[:, 2 * width :])
    )
    total1 = (
        grad1[...]
        + product(Rows(x3_b, width).span(3, 4), taps1[:, :width])
        + product(Rows(x3, width).span(0, 4), taps1[:, width:])
    )
    both = jnp.concatenate([total2[0:192], total1[0:192]], axis=1)
    biases = jnp.concatenate([total2[192:200, 64:128], total1[192:200, 64:128]], axis=1)
    tiles = [
        both[8 * (t // 3) : 8 * (t // 3) + 8, 128 * (t % 3) : 128 * (t % 3) + 128]
        for t in range(72)
    ]
    empty = jnp.zeros((8, 128), F32)
    own = own_half()
    low, high = tiles[:36] + [biases], tiles[36:] + [empty]
    for t in range(TILES):
        at = slice(128 * t, 128 * t + 128)
        grads_own[:, at] = jnp.where(own == 0, low[t], high[t])
        grads_send[:, at] = jnp.where(own == 0, high[t], low[t])


def pair_kernel(passed, own, received, out, through):
    out[...] = (own[...] + received[...]).astype(BF16)


def add_kernel(factor, *refs):
    out = refs[-1]
    terms = [ref[...].astype(F32) for ref in refs[:-1]]
    while len(terms) > 1:
        terms = [sum(terms[n + 1 : n + 2], terms[n]) for n in range(0, len(terms), 2)]
    out[...] = (terms[0] * factor).astype(out.dtype)


def behind_add(add, done, *refs):
    add(*refs)


def input_kernel(e3_b, e3, bwd1, mine_a, mine_b, theirs_a, theirs_b, mine, theirs):
    side = lax.axis_index("sx")
    half = mine.shape[0] // 2
    width = 2 * mine.shape[2]
    for whole, inner, outer in ((mine, mine_a, mine_b), (theirs, theirs_a, theirs_b)):
        whole[0:2] = outer[...]
        whole[2:half] = inner[...]

    def emit(e, acc):
        hand_out(side, mine, theirs, half + e - 4, acc)

    sweep(bwd1, joined(width, e3_b, 3, e3, 7, 3, half + 2), 3, emit)


def outputs_kernel(mine, back, out, image_grad, token, natural):
    side = lax.axis_index("sx")
    rows = out.shape[2]
    half = rows // 2
    for slot in range(2):
        for j in range(half):
            natural[slot, turned(side, j, rows)] = mine[slot * half + j]
            natural[slot, turned(side, rows - 1 - j, rows)] = back[slot * half + j]
    for slot, ref in ((0, out), (1, image_grad)):
        ref[0] = jnp.transpose(natural[slot], (1, 0, 2))
    token[...] = jnp.zeros(token.shape, F32)


def grads_kernel(held, swapped, gw1, gb1, gw2, gb2, gw1_v, gw2_v, sems):
    own = own_half()

    def tile(part, t):
        at = slice(128 * t, 128 * t + 128)
        return jnp.where(own == part, held[:, at], swapped[:, at])

    copies = []
    for layer, buffer, out in ((0, gw2_v, gw2), (1, gw1_v, gw1)):
        for block in range(24):
            part, first = block // 12, 3 * (block % 12) + layer
            pair = jnp.concatenate([tile(part, first), tile(part, first + 1)], axis=1)
            b, i = block // 8, (block % 8) * 8
            for a in range(3):
                at = 64 * layer + 64 * a
                buffer[a, b, i : i + 8, :] = pair[:, at : at + 64]
        copy = pltpu.make_async_copy(buffer, out, sems.at[layer])
        copy.start()
        copies.append(copy)
    biases = tile(0, 36)
    gb2[...] = biases[0:1, 0:64]
    gb1[...] = biases[0:1, 64:128]
    for copy in copies:
        copy.wait()


def exchange_stages(places, planes):
    def groups(count, axis):
        bits = [1 << k for k in range(count.bit_length() - 1)]
        pairs = [bits[k : k + 2] for k in range(0, len(bits), 2)]
        return [(axis, [b[0]] + ([b[1], b[0] | b[1]] if len(b) == 2 else [])) for b in pairs]

    rows, slides = groups(places, 0), groups(planes, 1)
    stages = []
    for plan in zip(rows + slides, slides + rows):
        stage = []
        for k in range(3):
            pairs = []
            for s in range(places):
                for x in range(2):
                    for g in range(planes):
                        part = half_of(x, s, g)
                        axis, masks = plan[part]
                        if k < len(masks):
                            t, h = (s ^ masks[k], g) if axis == 0 else (s, g ^ masks[k])
                            y = half_of(part, t, h)
                            pairs.append(((2 * s + x) * planes + g, (2 * t + y) * planes + h))
            if pairs:
                stage.append(pairs)
        stages.append(stage)
    return stages


def local(image, weight_one, bias_one, weight_two, bias_two, cotangent):
    _, chans, rows, cols = image.shape
    places, planes = lax.axis_size("sy"), lax.axis_size("grp")
    half = rows // 2
    width = 2 * cols
    factor = float(rows * cols * places * planes * lax.axis_size("sx")) ** (-0.5)
    call = functools.partial(pl.pallas_call, compiler_params=PARAMS)

    def rows_of(count):
        return pltpu.VMEM((count, chans, cols), BF16)

    def flat(height, count):
        return pltpu.VMEM((height, count * width), BF16)

    image_p, cot_p, swap, edges, w1, b1, w2, b2 = call(
        pack_kernel,
        out_shape=[
            rows_of(rows),
            rows_of(rows),
            rows_of(2 * half + 6),
            rows_of(6),
            pltpu.VMEM(weight_one.shape, BF16),
            pltpu.VMEM((1, chans), F32),
            pltpu.VMEM(weight_two.shape, BF16),
            pltpu.VMEM((1, chans), F32),
        ],
        in_specs=[pl.BlockSpec(memory_space=pltpu.HBM)] * 6,
        scratch_shapes=[
            pltpu.VMEM((chans, rows, cols), BF16),
            pltpu.VMEM((chans, rows, cols), BF16),
            pltpu.SemaphoreType.DMA((chans // 8 + 4,)),
        ],
        name="pack",
    )(
        *far(image, cotangent, weight_one, bias_one.reshape(1, chans)),
        *far(weight_two, bias_two.reshape(1, chans)),
    )
    swapped = lax.ppermute(swap, "sx", SWAP)
    across = []
    for s in range(places):
        for g in range(planes):
            lower, upper = 2 * s * planes + g, (2 * s + 1) * planes + g
            across.append((lower, lower - planes if s > 0 else lower ^ 1))
            across.append((upper, upper + planes if s < places - 1 else upper ^ 1))
    axes = ("sy", "sx", "grp")
    edges_other = lax.ppermute(edges, axes, across)
    edges_own = lax.ppermute(swapped[half : half + 6], axes, across)
    fwd1, fwd2, bwd2, bwd1, bias1, bias2 = call(
        weights_kernel,
        out_shape=[pltpu.VMEM((192, 192), BF16)] * 4 + [pltpu.VMEM((64, 128), F32)] * 2,
        cost_estimate=lasting(0.3),
        name="weights",
    )(*near(w1, b1, w2, b2))

    x3, h3, d3, e3, slopes, mine_a, theirs_a, grad2, grad1 = call(
        inner_kernel,
        out_shape=[
            flat(208, half + 4),
            flat(208, half + 2),
            flat(192, half),
            flat(192, half - 2),
            pltpu.VMEM((half, chans, width), F32),
            rows_of(half - 2),
            rows_of(half - 2),
            pltpu.VMEM((208, 192), F32),
            pltpu.VMEM((208, 192), F32),
        ],
        scratch_shapes=[
            pltpu.VMEM((2, half + 4, chans, cols), BF16),
            pltpu.VMEM((2, half + 2, chans, cols), BF16),
            flat(192, half),
            flat(192, half - 1),
        ],
        cost_estimate=lasting(4.0),
        name="inner",
    )(*near(image_p, cot_p, swapped, fwd1, fwd2, bwd2, bias1, bias2))
    half_grads = pltpu.VMEM((8, TILES * 128), F32)
    e3_b, mine_b, theirs_b, grads_own, grads_send = call(
        outer_kernel,
        out_shape=[flat(192, 4), rows_of(2), rows_of(2), half_grads, half_grads],
        scratch_shapes=[
            pltpu.VMEM((2, 4, chans, cols), BF16),
            pltpu.VMEM((2, 4, chans, cols), BF16),
            flat(208, 4),
            flat(208, 4),
            flat(192, 4),
            pltpu.VMEM((2, chans, width), F32),
            flat(192, 4),
            flat(192, 5),
        ],
        cost_estimate=lasting(2.0),
        name="outer",
    )(
        *near(edges_own, edges_other, cot_p, swapped, fwd1, fwd2, bwd2, bias1, bias2),
        *near(x3, h3, d3, slopes, grad2, grad1),
    )
    grads_received = lax.ppermute(grads_send, "sx", SWAP)
    mine, theirs = call(
        input_kernel,
        out_shape=[rows_of(rows), rows_of(rows)],
        cost_estimate=lasting(0.7),
        name="input",
    )(*near(e3_b, e3, bwd1, mine_a, mine_b, theirs_a, theirs_b))
    held, theirs = call(
        pair_kernel,
        out_shape=[pltpu.VMEM((8, TILES * 128), BF16), rows_of(rows)],
        input_output_aliases={0: 1},
        name="pair",
    )(*near(theirs, grads_own, grads_received))
    back = lax.ppermute(theirs, "sx", SWAP)
    out, image_grad, done = call(
        outputs_kernel,
        out_shape=[shape_of(image.shape, BF16)] * 2 + [pltpu.VMEM((8, 128), F32)],
        scratch_shapes=[pltpu.VMEM((2, rows, chans, cols), BF16)],
        cost_estimate=lasting(1.3),
        name="outputs",
    )(*near(mine, back))
    stages = exchange_stages(places, planes)
    for n, stage in enumerate(stages):
        final = n == len(stages) - 1
        received = [lax.ppermute(held, axes, pairs) for pairs in stage]
        add = functools.partial(add_kernel, factor if final else 1.0)
        behind = [done] if n == 0 else []
        held = call(
            functools.partial(behind_add, add) if behind else add,
            out_shape=pltpu.VMEM((8, TILES * 128), F32 if final else BF16),
            name="add",
        )(*near(*behind, held, *received))
    swapped_sums = lax.ppermute(held, "sx", SWAP)
    weight_shape = shape_of((3, 3, chans, chans), F32)
    bias_shape = shape_of((1, chans), F32)
    gw1, gb1, gw2, gb2 = call(
        grads_kernel,
        out_shape=[weight_shape, bias_shape, weight_shape, bias_shape],
        out_specs=[pl.BlockSpec(memory_space=m) for m in (pltpu.HBM, pltpu.VMEM) * 2],
        scratch_shapes=[
            pltpu.VMEM((3, 3, chans, chans), F32),
            pltpu.VMEM((3, 3, chans, chans), F32),
            pltpu.SemaphoreType.DMA((2,)),
        ],
        name="grads",
    )(*near(held, swapped_sums))
    return out, image_grad, gw1, gb1.reshape(chans), gw2, gb2.reshape(chans)


def solution(mesh):
    return jax.shard_map(
        local,
        mesh=mesh,
        in_specs=(P("grp", None, "sy", "sx"), P(), P(), P(), P(), P("grp", None, "sy", "sx")),
        out_specs=(P("grp", None, "sy", "sx"), P("grp", None, "sy", "sx"), P(), P(), P(), P()),
        check_vma=False,
    )
```
